32 devices in a mesh: expert: 8 (over z, y), tensor: 4 (over x, core).
Axes of the slice: x: 2, y: 2, z: 4, core: 2. Of those that a mesh axis runs over, the one named last changes fastest.
Arguments:
- tokens: bfloat16 [4096, 2048], P('expert', 'tensor'), may hold values from -6 to 6
- segments: int32 [4096], P('expert'), may hold values from 0 to 255, never falling along the last dimension, each value on 1 to 512 neighbouring positions
- routes: int32 [4096, 8], P('expert'), may hold values from 0 to 15, all different within a row; in each aligned block of 512 rows (0 to 511, 512 to 1023, ...) at most 320 rows name the same one
- norm1_gain: float32 [2048], replicated, may hold values from 0.1 to 1.9
- w_query: bfloat16 [2048, 2048], P(None, 'tensor'), may hold values from -0.125 to 0.125
- w_key: bfloat16 [2048, 2048], P(None, 'tensor'), may hold values from -0.125 to 0.125
- w_value: bfloat16 [2048, 2048], P(None, 'tensor'), may hold values from -0.125 to 0.125
- w_out: bfloat16 [2048, 2048], P('tensor'), may hold values from -0.5 to 0.5
- query_gain: float32 [128], replicated, may hold values from 0.1 to 1.9
- key_gain: float32 [128], replicated, may hold values from 0.1 to 1.9
- norm2_gain: float32 [2048], replicated, may hold values from 0.1 to 1.9
- router: bfloat16 [2048, 16], replicated, may hold values from -0.0625 to 0.0625
- w_gate: bfloat16 [16, 2048, 1024], P('expert', None, 'tensor'), may hold values from -0.125 to 0.125
- w_up: bfloat16 [16, 2048, 1024], P('expert', None, 'tensor'), may hold values from -0.125 to 0.125
- w_down: bfloat16 [16, 1024, 2048], P('expert', 'tensor'), may hold values from -1.5 to 1.5
- cotangent: bfloat16 [4096, 2048], P('expert', 'tensor'), may hold values from -6 to 6
Outputs:
- mixed: bfloat16 [4096, 2048], P('expert', 'tensor')
- tokens_grad: float32 [4096, 2048], P('expert', 'tensor')
- norm1_gain_grad: float32 [2048], replicated
- w_query_grad: float32 [2048, 2048], P(None, 'tensor')
- w_key_grad: float32 [2048, 2048], P(None, 'tensor')
- w_value_grad: float32 [2048, 2048], P(None, 'tensor')
- w_out_grad: float32 [2048, 2048], P('tensor')
- query_gain_grad: float32 [128], replicated
- key_gain_grad: float32 [128], replicated
- norm2_gain_grad: float32 [2048], replicated
- router_grad: float32 [2048, 16], replicated
- w_gate_grad: float32 [16, 2048, 1024], P('expert', None, 'tensor')
- w_up_grad: float32 [16, 2048, 1024], P('expert', None, 'tensor')
- w_down_grad: float32 [16, 1024, 2048], P('expert', 'tensor')
The draws below stay inside these ranges and needn't reach their ends.
Inputs may be any that keep to these rules, and one draw needn't show every extreme that they name: `segments`: numbers never fall along the tokens; each document has 1 to 512 tokens, and one has exactly 512. `routes`: each row names 8 different experts; among the rows of one index of expert (aligned blocks of 512 rows) no expert is named by more than 320 rows, a bound that some block reaches.
All inputs are finite; a program needn't handle non-finite values.
Results may differ from the reference program's by a relative error of at most 0.02.
Values may be sent and summed in bfloat16 or wider, within the bound.
A program may use at most 512 MiB of HBM per device.

```python
import math
import jax
import jax.numpy as jnp
import numpy as np
from jax import lax

D = 2048
HEADS = 16
HEAD_DIM = 128
FFE = 1024
TOPK = 8
TOK_DEV = 512
EXPERTS = 16
TOKENS = 4096
CAP = 320
N_EXPERT = 8


def shard_levels(stream_key, shape, shards, least, high):
    level = 1.0
    for dim, blocks in shards:
        steps = jax.random.uniform(jax.random.fold_in(jax.random.fold_in(stream_key, 6), dim), (blocks,), jnp.float32, least / len(shards), high / len(shards))
        level = level * jnp.repeat(jnp.exp(steps), shape[dim] // blocks).reshape((-1,) + (1,) * (len(shape) - 1 - dim))
    return level


def length_profile(amount, total, most, slope):
    weights = [(1 << 20) // math.isqrt(standing ** slope) + 1 for standing in range(2, amount + 1)]
    surplus, given = total - most - (amount - 1), [1] * (amount - 1)
    while surplus > 0:
        candidates = [i for i in range(amount - 1) if given[i] < most]
        pool, budget = sum([weights[i] for i in candidates]), surplus
        for i in candidates:
            extra = min(most - given[i], max(1, budget * weights[i] // pool), surplus)
            given[i] = given[i] + extra
            surplus = surplus - extra
    return np.array([most] + given)


def ragged(rng, number_of, total, bound, skew):
    if number_of == 2:
        one = jax.random.randint(rng, (), max(1, total - bound), min(bound, total - 1) + 1)
        return jnp.stack([one, total - one])
    sizes = jnp.asarray(length_profile(number_of, total, bound, skew), jnp.int32)
    pairs = (number_of - 1) // 2
    donor, receiver = sizes[1:1 + 2 * pairs:2], sizes[2:2 + 2 * pairs:2]
    slack = jnp.minimum(donor - 1, bound - receiver)
    shifted = jax.random.randint(jax.random.fold_in(rng, 1), (pairs,), 0, 1 << 20) % (slack + 1)
    sizes = sizes.at[1:1 + 2 * pairs:2].set(donor - shifted).at[2:2 + 2 * pairs:2].set(receiver + shifted)
    return sizes[jax.random.permutation(jax.random.fold_in(rng, 2), number_of)]


def assign_block(own_key, own, number, rows, number_of, top, most, slope):
    ranking = jax.random.permutation(own_key, number_of)
    heavy_load, common = shares(number_of, rows * top, most, slope, True), shares(number_of, rows * top, most, slope, False)
    places = jnp.arange(number_of)

    def named(sizes, offset_by):
        used = int((sizes > 0).sum())
        fixed = max(1, used // 4)
        shifted = fixed + (places - fixed + offset_by * (used - fixed)) % max(1, number_of - fixed)
        return jnp.zeros((number_of,), jnp.int32).at[ranking[jnp.where(places < fixed, places, shifted)]].set(jnp.asarray(sizes, jnp.int32))

    sizes = jnp.where(number % 4 == 0, named(heavy_load, number // 4), named(common, number - number // 4 - 1))
    mixed = jax.random.permutation(jax.random.fold_in(own, 3), number_of)
    donor, taker = mixed[0:number_of // 2 * 2:2], mixed[1:number_of // 2 * 2:2]
    margin = jnp.minimum(sizes[donor] - 1, most - sizes[taker]) // 2
    margin = jnp.where((donor == ranking[0]) | (taker == ranking[0]) | (sizes[taker] == 0), 0, jnp.maximum(margin, 0))
    shifted = jax.random.randint(jax.random.fold_in(own, 4), (number_of // 2,), 0, 1 << 20) % (margin + 1)
    sizes = sizes.at[donor].add(-shifted).at[taker].add(shifted)
    items = jnp.searchsorted(jnp.cumsum(sizes), jnp.arange(rows * top), side="right").astype(jnp.int32)
    listing = items.reshape(top, rows).T
    listing = listing[jax.random.permutation(jax.random.fold_in(own, 1), rows)]
    offset_by = jax.random.randint(jax.random.fold_in(own, 2), (rows, 1), 0, top)
    return jnp.take_along_axis(listing, (jnp.arange(top)[None, :] + offset_by) % top, axis=1)


def shares(count, total, limit, lean, full):
    weights = [(1 << 20) // math.isqrt(standing ** lean) + 1 for standing in range(1, count + 1)]
    largest = limit if full else min(limit, max(-(-total // count), total * weights[0] // sum(weights)))
    least = 1 if total - largest >= count - 1 else 0
    holding, spare = [largest] + [least] * (count - 1), total - largest - least * (count - 1)
    while spare > 0:
        candidates = [i for i in range(1, count) if holding[i] < largest] or [i for i in range(1, count) if holding[i] < limit]
        mass, remaining = sum([weights[i] for i in candidates]), spare
        for i in candidates:
            addition = min(limit - holding[i], max(1, remaining * weights[i] // mass), spare)
            holding[i] = holding[i] + addition
            spare = spare - addition
    return np.array(holding)


def centred(rng, extent, deviation, limit, shards=(), kind=jnp.bfloat16):
    values = deviation * jax.random.normal(rng, extent, jnp.float32)
    if shards:
        values = values * shard_levels(rng, extent, shards, -0.22, 0.18)
    return jnp.clip(values, -limit, limit).astype(kind)


def setup_inputs(seed: int = 0) -> dict:
    arg_keys = jax.random.split(jax.random.key(seed), 17)
    tokens = centred(arg_keys[0], (TOKENS, D), 1.0, 6.0, ((0, 8), (1, 4)))
    segments = jnp.searchsorted(jnp.cumsum(ragged(arg_keys[1], TOKENS // 16, TOKENS, TOK_DEV, 2)), jnp.arange(TOKENS), side="right").astype(jnp.int32)
    routes_keys = jax.random.split(jax.random.fold_in(arg_keys[2], 1), TOKENS // TOK_DEV)
    routes_turns = jax.random.permutation(jax.random.fold_in(arg_keys[2], 3), TOKENS // TOK_DEV)
    routes = jax.vmap(lambda own, number: assign_block(jax.random.fold_in(arg_keys[2], 2), own, number, TOK_DEV, EXPERTS, TOPK, CAP, 1))(routes_keys, routes_turns).reshape((TOKENS, TOPK))
    norm1_gain = jnp.clip(1.0 + 0.18 * jax.random.normal(arg_keys[3], (D,), jnp.float32), 0.1, 1.9)
    w_query = centred(arg_keys[4], (D, HEADS * HEAD_DIM), D ** -0.5, 0.125, ((1, 4),))
    w_key = centred(arg_keys[5], (D, HEADS * HEAD_DIM), D ** -0.5, 0.125, ((1, 4),))
    w_value = centred(arg_keys[6], (D, HEADS * HEAD_DIM), D ** -0.5, 0.125, ((1, 4),))
    w_out = centred(arg_keys[7], (HEADS * HEAD_DIM, D), (HEADS * HEAD_DIM // 16) ** -0.5, 0.5, ((0, 4),))
    query_gain = jnp.clip(1.0 + 0.18 * jax.random.normal(arg_keys[8], (HEAD_DIM,), jnp.float32), 0.1, 1.9)
    key_gain = jnp.clip(1.0 + 0.18 * jax.random.normal(arg_keys[9], (HEAD_DIM,), jnp.float32), 0.1, 1.9)
    norm2_gain = jnp.clip(1.0 + 0.18 * jax.random.normal(arg_keys[10], (D,), jnp.float32), 0.1, 1.9)
    router = centred(arg_keys[11], (D, EXPERTS), (0.5 / D ** 0.5), 0.0625)
    w_gate = centred(arg_keys[12], (EXPERTS, D, FFE), D ** -0.5, 0.125, ((0, 8), (2, 4)))
    w_up = centred(arg_keys[13], (EXPERTS, D, FFE), D ** -0.5, 0.125, ((0, 8), (2, 4)))
    w_down = centred(arg_keys[14], (EXPERTS, FFE, D), (0.53 * EXPERTS / FFE ** 0.5), 1.5, ((0, 8), (1, 4)))
    cotangent = centred(arg_keys[15], (TOKENS, D), 1.0, 6.0, ((0, 8), (1, 4)))
    return dict(tokens=tokens, segments=segments, routes=routes, norm1_gain=norm1_gain, w_query=w_query, w_key=w_key, w_value=w_value, w_out=w_out, query_gain=query_gain, key_gain=key_gain, norm2_gain=norm2_gain, router=router, w_gate=w_gate, w_up=w_up, w_down=w_down, cotangent=cotangent)


EPSILON = 1e-06
ROPE_BASE = 50000.0
HIGHEST = lax.Precision.HIGHEST

@jax.custom_vjp
def low(v):
    return lax.optimization_barrier(v.astype(jnp.bfloat16)).astype(jnp.float32)

@jax.custom_vjp
def low_back(v):
    return v

def low_keep(v):
    return (low(v), None)

def low_pass(kept, grad):
    return (grad,)

def back_keep(v):
    return (v, None)

def back_low(kept, grad):
    return (low(grad),)
low.defvjp(low_keep, low_pass)
low_back.defvjp(back_keep, back_low)

def rms_scale(values):
    return lax.rsqrt(lax.optimization_barrier(jnp.mean(values * values, axis=-1, keepdims=True)) + EPSILON)

def rotate(values, cosine, sine_table):
    half_dim = values.shape[-1] // 2
    front_half = values[..., :half_dim]
    back_half = values[..., half_dim:]
    return jnp.concatenate([front_half * cosine - back_half * sine_table, back_half * cosine + front_half * sine_table], axis=-1)

def route_tables(routes):
    blocks = routes.reshape(N_EXPERT, TOK_DEV * TOPK)
    expert_ids = jnp.arange(EXPERTS, dtype=jnp.int32)
    onehot = (blocks[:, :, None] == expert_ids[None, None, :]).astype(jnp.int32)
    slot_ids = lax.optimization_barrier(jnp.sum(jnp.cumsum(onehot, axis=1) * onehot, axis=2)) - 1
    block_ids = jnp.arange(N_EXPERT, dtype=jnp.int32)[:, None]
    positions = (blocks * (N_EXPERT * CAP) + block_ids * CAP + slot_ids).astype(jnp.int32)
    flat_positions = positions.reshape(-1)
    owners = (jnp.arange(TOKENS * TOPK, dtype=jnp.int32) // TOPK).astype(jnp.int32)
    total_slots = EXPERTS * N_EXPERT * CAP
    table_tokens = jnp.zeros((total_slots,), jnp.int32).at[flat_positions].set(owners)
    table_valid = jnp.zeros((total_slots,), jnp.float32).at[flat_positions].set(1.0)
    return (positions.reshape(TOKENS, TOPK), table_tokens.reshape(EXPERTS, N_EXPERT * CAP), table_valid.reshape(EXPERTS, N_EXPERT * CAP))

def attend(pieces):
    query, key_rows, value, segment_ids = pieces
    scores = low_back(jnp.einsum('qhd,khd->hqk', query, key_rows, precision=HIGHEST) * HEAD_DIM ** (-0.5))
    same_doc = (segment_ids[:, None] == segment_ids[None, :])[None]
    scores = jnp.where(same_doc, scores, -1e+30)
    weights = jnp.exp(scores - lax.optimization_barrier(jnp.max(scores, axis=-1, keepdims=True)))
    probs_low = low(weights / lax.optimization_barrier(jnp.sum(weights, axis=-1, keepdims=True)))
    return jnp.einsum('hqk,khd->qhd', probs_low, value, precision=HIGHEST)

def reference(tokens, segments, routes, norm1_gain, w_query, w_key, w_value, w_out, query_gain, key_gain, norm2_gain, router, w_gate, w_up, w_down, cotangent):
    positions, table_tokens, table_valid = route_tables(routes)
    head_count = w_query.shape[1] // HEAD_DIM
    places = (jnp.arange(TOKENS, dtype=jnp.int32) % TOK_DEV).astype(jnp.float32)
    frequency = ROPE_BASE ** (-jnp.arange(HEAD_DIM // 2, dtype=jnp.float32) * 2.0 / HEAD_DIM)
    angles = places[:, None] * frequency[None, :]
    cosine = jnp.cos(angles)[:, None, :]
    sine_table = jnp.sin(angles)[:, None, :]
    segment_rows = segments.reshape(N_EXPERT, TOK_DEV)

    def by_sequence(values):
        return values.reshape(N_EXPERT, TOK_DEV, head_count, HEAD_DIM)

    def layer(inputs, norm1_w, query_w, key_w, value_w, out_w, query_g, key_g, norm2_w, router_w, gate_w, up_w, down_w):
        normed = low(inputs * rms_scale(inputs) * norm1_w)
        query_pre = low_back(jnp.dot(normed, query_w, precision=HIGHEST)).reshape(TOKENS, head_count, HEAD_DIM)
        key_pre = low_back(jnp.dot(normed, key_w, precision=HIGHEST)).reshape(TOKENS, head_count, HEAD_DIM)
        value_low = low_back(low(jnp.dot(normed, value_w, precision=HIGHEST))).reshape(TOKENS, head_count, HEAD_DIM)
        query_rot = low(rotate(query_pre * rms_scale(query_pre) * query_g, cosine, sine_table))
        key_rot = low(rotate(key_pre * rms_scale(key_pre) * key_g, cosine, sine_table))
        attended = lax.map(jax.checkpoint(attend), (by_sequence(query_rot), by_sequence(key_rot), by_sequence(value_low), segment_rows))
        attended = low_back(low(attended.reshape(TOKENS, head_count * HEAD_DIM)))
        residual = inputs + low_back(jnp.dot(attended, out_w, precision=HIGHEST))
        normed_two = low(residual * rms_scale(residual) * norm2_w)
        router_probs = jax.nn.softmax(jnp.dot(normed_two, router_w, precision=HIGHEST), axis=-1)
        gate_values = jnp.take_along_axis(router_probs, routes, axis=1)

        def expert_rows(pieces):
            row_tokens, row_valid, gate_mat, up_mat, down_mat = pieces
            rows = low_back(normed_two[row_tokens]) * row_valid[:, None]
            gate_act = low_back(jnp.dot(rows, gate_mat, precision=HIGHEST))
            up_act = low_back(jnp.dot(rows, up_mat, precision=HIGHEST))
            hidden = low(jax.nn.silu(gate_act) * up_act)
            return low_back(low(jnp.dot(hidden, down_mat, precision=HIGHEST)))
        expert_out = lax.map(jax.checkpoint(expert_rows), (table_tokens, table_valid, gate_w, up_w, down_w))
        flat_out = expert_out.reshape(EXPERTS * N_EXPERT * CAP, D)
        result = residual
        for choice_index in range(TOPK):
            result = result + gate_values[:, choice_index:choice_index + 1] * flat_out[positions[:, choice_index]]
        return result
    floats = (tokens.astype(jnp.float32), norm1_gain.astype(jnp.float32), w_query.astype(jnp.float32), w_key.astype(jnp.float32), w_value.astype(jnp.float32), w_out.astype(jnp.float32), query_gain.astype(jnp.float32), key_gain.astype(jnp.float32), norm2_gain.astype(jnp.float32), router.astype(jnp.float32), w_gate.astype(jnp.float32), w_up.astype(jnp.float32), w_down.astype(jnp.float32))
    mixed, pullback = jax.vjp(layer, *floats)
    grads = pullback(cotangent.astype(jnp.float32))
    return (mixed.astype(jnp.bfloat16), grads[0], grads[1], grads[2], grads[3], grads[4], grads[5], grads[6], grads[7], grads[8], grads[9], grads[10], grads[11], grads[12])
```

```python
import functools

import jax
import jax.numpy as jnp
from jax import lax
from jax.experimental import pallas as pl
from jax.experimental.pallas import tpu as pltpu
from jax.sharding import PartitionSpec as P

HEAD_DIM = 128
EPSILON = 1e-06
ROPE_BASE = 50000.0
BF = jnp.bfloat16
F32 = jnp.float32
BOTH = ("expert", "tensor")


def rms_backward(values, scale_row, grad_out):
    return scale_row * (
        grad_out
        - values * scale_row * scale_row * jnp.mean(grad_out * values, axis=-1, keepdims=True)
    )


def rope_tables(length, head_dim):
    half_dim = head_dim // 2
    frequency = ROPE_BASE ** (-jnp.arange(half_dim, dtype=F32) * 2.0 / head_dim)
    angles = jnp.arange(length, dtype=F32)[:, None] * frequency[None, :]
    return jnp.cos(angles), jnp.sin(angles)


def rows_product(left, right):
    return lax.dot_general(left, right, (((0,), (0,)), ((), ())), preferred_element_type=F32)


def cols_product(left, right):
    return lax.dot_general(left, right, (((1,), (1,)), ((), ())), preferred_element_type=F32)


def as_column(row):
    return jnp.broadcast_to(row.astype(F32), (128, row.shape[1])).T[:, 0:1]


def dot(left, right):
    return jnp.dot(left, right, preferred_element_type=F32)


ANY = pl.BlockSpec(memory_space=pl.ANY)
VMEM = pl.BlockSpec(memory_space=pltpu.VMEM)


class Place:
    def __init__(self, groups):
        self.e, self.t = lax.axis_index("expert"), lax.axis_index("tensor")
        self.rounds = groups // 2
        self.high, self.low = self.e // 2, self.e % 2
        self.side, self.core = self.t // 2, self.t % 2
        self.y = (2 * self.high + 1 - self.low, self.t)
        self.x = (self.e, 2 * (1 - self.side) + self.core)
        self.c = (self.e, 2 * self.side + 1 - self.core)

    def far(self, r):
        return lax.rem(self.high + self.rounds - r, self.rounds)

    def z(self, r):
        return (2 * self.far(r) + self.low, self.t)

    def greet(self, partners):
        barrier = pltpu.get_barrier_semaphore()
        for partner in partners:
            pl.semaphore_signal(
                barrier, inc=1, device_id=partner, device_id_type=pl.DeviceIdType.MESH
            )
        pl.semaphore_wait(barrier, len(partners))


class Sends:
    def __init__(self, sems):
        self.sems, self.copies = sems, []

    def start(self, src, dst, recv_sem, device, when=None):
        copy = remote(src, dst, self.sems.at[len(self.copies)], recv_sem, device)
        if when is None:
            copy.start()
        else:
            pl.when(when)(copy.start)
        self.copies.append((copy, when))

    def finish(self):
        for copy, when in self.copies:
            if when is None:
                copy.wait_send()
            else:
                pl.when(when)(copy.wait_send)


def remote(src, dst, send_sem, recv_sem, device):
    return pltpu.make_async_remote_copy(
        src_ref=src,
        dst_ref=dst,
        send_sem=send_sem,
        recv_sem=recv_sem,
        device_id=device,
        device_id_type=pl.DeviceIdType.MESH,
    )


def arrived(ref, recv_sem, send_sem, device):
    remote(ref, ref, send_sem, recv_sem, device).wait_recv()


def departed(ref, recv_sem, send_sem, device):
    remote(ref, ref, send_sem, recv_sem, device).wait_send()


def gather_kernel(
    x_ref,
    mask_ref,
    out_ref,
    masks_ref,
    send_sems,
    recv_sems,
    mask_sems,
    own_sem,
):
    groups, tok = out_ref.shape[0], out_ref.shape[2]
    half = tok // 2
    p = Place(groups)
    rounds = p.rounds
    p.greet([p.y, p.x, p.c] + [p.z(r) for r in range(1, rounds)])
    sends = Sends(send_sems)
    low2, side2 = 1 - p.low, 1 - p.side

    def shard(h, e, t):
        return out_ref.at[e, t, pl.ds(h * half, half)]

    def send(h, e, t, device, src=None):
        dst = shard(h, e, t)
        sends.start(dst if src is None else src, dst, recv_sems.at[h, e, t], device)

    def wait(h, e, t, device):
        arrived(shard(h, e, t), recv_sems.at[h, e, t], send_sems.at[0], device)

    own = pltpu.make_async_copy(x_ref, out_ref.at[p.e, p.t], own_sem)
    own.start()

    def send_mask(e, device):
        sends.start(masks_ref.at[e], masks_ref.at[e], mask_sems.at[e], device)

    masks_ref[p.e] = mask_ref[...]

    def first(r):
        e = 2 * p.far(r) + p.low
        if r > 0:
            arrived(masks_ref.at[e], mask_sems.at[e], send_sems.at[0], p.z(r))
        send_mask(e, p.y)
        for h in range(2):
            src = x_ref.at[pl.ds(h * half, half)] if r == 0 else None
            if r > 0:
                wait(h, e, p.t, p.z(r))
            send(h, e, p.t, p.x if h else p.y, src)
            send(h, e, p.t, p.y if h else p.x, src)
            send(h, e, p.t, p.c, src)

    def second(r):
        e, e2 = 2 * p.far(r) + p.low, 2 * p.far(r) + low2
        wait(0, e2, p.t, p.y)
        send(0, e2, p.t, p.x)
        send(0, e2, p.t, p.c)
        t2 = 2 * side2 + p.core
        wait(1, e, t2, p.x)
        send(1, e, t2, p.y)
        send(1, e, t2, p.c)

    def third(r):
        e, e2 = 2 * p.far(r) + p.low, 2 * p.far(r) + low2
        t2 = 2 * side2 + p.core
        wait(0, e, t2, p.x)
        send(0, e, t2, p.c)
        wait(1, e2, p.t, p.y)
        send(1, e2, p.t, p.c)
        wait(0, e2, t2, p.x)
        send(0, e2, t2, p.c)
        wait(1, e2, t2, p.y)
        send(1, e2, t2, p.c)

    for r in range(1, rounds):
        to = (2 * lax.rem(p.high + r, rounds) + p.low, p.t)
        send_mask(p.e, to)
        for h in range(2):
            send(h, p.e, p.t, to, x_ref.at[pl.ds(h * half, half)])
    for r in range(rounds + 2):
        if r < rounds:
            first(r)
        if 0 <= r - 1 < rounds:
            second(r - 1)
        if 0 <= r - 2 < rounds:
            third(r - 2)
    other = 1 - p.core
    for r in range(rounds):
        e2 = 2 * p.far(r) + low2
        arrived(masks_ref.at[e2], mask_sems.at[e2], send_sems.at[0], p.y)
        for e in (2 * p.far(r) + p.low, 2 * p.far(r) + low2):
            for t in (2 * p.side + other, 2 * side2 + other):
                for h in range(2):
                    wait(h, e, t, p.c)
    own.wait()
    sends.finish()


def gather_all(x, mask, groups, tensors, collective_id):
    tok, width = x.shape
    rounds = groups // 2
    count = 3 * (rounds - 1) + 7 * rounds + 4 * rounds + 4 * rounds
    return pl.pallas_call(
        gather_kernel,
        name="gather_all",
        in_specs=[ANY, VMEM],
        out_specs=[ANY, VMEM],
        out_shape=[
            jax.ShapeDtypeStruct((groups, tensors, tok, width), x.dtype),
            jax.ShapeDtypeStruct((groups,) + mask.shape, mask.dtype),
        ],
        scratch_shapes=[
            pltpu.SemaphoreType.DMA((count,)),
            pltpu.SemaphoreType.DMA((2, groups, tensors)),
            pltpu.SemaphoreType.DMA((groups,)),
            pltpu.SemaphoreType.DMA,
        ],
        compiler_params=pltpu.CompilerParams(
            collective_id=collective_id, has_side_effects=True, vmem_limit_bytes=32 * 2**20
        ),
        cost_estimate=pl.CostEstimate(
            flops=0, bytes_accessed=groups * tensors * tok * width * 2, transcendentals=0
        ),
    )(x, mask)


class Scatter:
    def __init__(self, p, bufs, sems):
        self.p = p
        self.total, self.from_x0, self.from_y0, self.from_x1, self.from_y1, self.from_z = bufs
        self.send_sems, self.core_sems, self.x0_sems, self.y0_sems = sems[:4]
        self.x1_sems, self.y1_sems, self.z_sems = sems[4:]
        self.tok, cut = self.total.shape[2], self.from_x0.shape[1]
        self.halves = (pl.ds(0, cut), pl.ds(cut, self.tok - cut))
        self.lows = (1 - p.low, p.low)
        self.sides = (1 - p.side, p.side)

    @staticmethod
    def scratch(groups, tok, width, cut):
        rounds, rest = groups // 2, tok - cut
        dma = pltpu.SemaphoreType.DMA
        bufs = [
            pltpu.VMEM((groups, 2, tok, width), BF),
            pltpu.VMEM((groups, cut, width), BF),
            pltpu.VMEM((rounds, cut, width), BF),
            pltpu.VMEM((rounds, rest, width), BF),
            pltpu.VMEM((rounds, 2, rest, width), BF),
            pltpu.VMEM((rounds, tok, width), BF),
        ]
        sems = [
            dma((12, rounds)),
            dma((groups, 2)),
            dma((groups,)),
            dma((rounds,)),
            dma((rounds,)),
            dma((rounds, 2)),
            dma((rounds, 2)),
        ]
        return bufs, sems

    def order(self, k):
        return (k + 1) % self.p.rounds

    def block(self, r, i):
        return 2 * self.p.far(r) + self.lows[i]

    def wait(self, ref, sem, device):
        arrived(ref, sem, self.send_sems.at[0, 0], device)

    def send(self, n, r, src, dst, sem, device):
        remote(src, dst, self.send_sems.at[n, r], sem, device).start()

    def add(self, target, received):
        self.total[target] = self.total[target] + received

    def core(self, r, i, j, src):
        e, side = self.block(r, i), self.sides[j]
        dst, sem = self.total.at[e, side], self.core_sems.at[e, side]
        self.send(2 * i + j, r, src, dst, sem, self.p.c)

    def core_sent(self, r, i, j, src):
        departed(src, self.core_sems.at[0, 0], self.send_sems.at[2 * i + j, r], self.p.c)

    def core_add(self, r, i, j, mine):
        e, side = self.block(r, i), self.sides[j]
        self.wait(self.total.at[e, side], self.core_sems.at[e, side], self.p.c)
        self.total[e, side] = self.total[e, side] + mine

    def first(self, r, i, j):
        p, (h0, h1) = self.p, self.halves
        e, far, side = self.block(r, i), p.far(r), self.sides[j]
        if j == 0:
            src = self.total.at[e, side, h0]
            self.send(4 + i, r, src, self.from_x0.at[e], self.x0_sems.at[e], p.x)
        if i == 0:
            src, dst = self.total.at[e, side, h1], self.from_y1.at[far, side]
            self.send(6 + j, r, src, dst, self.y1_sems.at[far, side], p.y)

    def second0(self, r, i):
        p, far, e = self.p, self.p.far(r), self.block(r, i)
        rows = self.halves[0]
        self.wait(self.from_x0.at[e], self.x0_sems.at[e], p.x)
        self.add((e, p.side, rows), self.from_x0[e])
        if i == 0:
            src = self.total.at[e, p.side, rows]
            self.send(8, r, src, self.from_y0.at[far], self.y0_sems.at[far], p.y)

    def second1(self, r, j):
        p, far, side = self.p, self.p.far(r), self.sides[j]
        e, rows = 2 * far + p.low, self.halves[1]
        self.wait(self.from_y1.at[far, side], self.y1_sems.at[far, side], p.y)
        self.add((e, side, rows), self.from_y1[far, side])
        if j == 0:
            src = self.total.at[e, side, rows]
            self.send(9, r, src, self.from_x1.at[far], self.x1_sems.at[far], p.x)

    def third(self, r, h):
        p, far = self.p, self.p.far(r)
        e, rows = 2 * far + p.low, self.halves[h]
        if h == 0:
            received, sem, device = self.from_y0, self.y0_sems, p.y
        else:
            received, sem, device = self.from_x1, self.x1_sems, p.x
        self.wait(received.at[far], sem.at[far], device)
        self.add((e, p.side, rows), received[far])

        @pl.when(r > 0)
        def _():
            src, dst = self.total.at[e, p.side, rows], self.from_z.at[r, rows]
            self.send(10 + h, r, src, dst, self.z_sems.at[r, h], p.z(r))

    def finish(self, out_ref):
        p = self.p
        for h, rows in enumerate(self.halves):
            total = self.total[p.e, p.side, rows].astype(F32)
            for r in range(1, p.rounds):
                source = (2 * lax.rem(p.high + r, p.rounds) + p.low, p.t)
                self.wait(self.from_z.at[r, rows], self.z_sems.at[r, h], source)
                total += self.from_z[r, rows].astype(F32)
            out_ref[rows, :] = total
        h0, h1 = self.halves
        for r in range(p.rounds):
            ends = [(4, h0, p.x), (5, h0, p.x), (6, h1, p.y), (7, h1, p.y), (8, h0, p.y)]
            ends += [(9, h1, p.x)]
            if r > 0:
                ends += [(10, h0, p.z(r)), (11, h1, p.z(r))]
            for n, rows, device in ends:
                departed(
                    self.total.at[0, 0, rows],
                    self.core_sems.at[0, 0],
                    self.send_sems.at[n, r],
                    device,
                )


class ScatterSteps:
    def __init__(self, scatter, part_ref):
        self.scatter, self.part = scatter, part_ref

    def load(self, k, i, j):
        s = self.scatter
        at = (s.block(s.order(k), i), s.sides[j])
        return pltpu.make_async_copy(self.part.at[at], s.total.at[at], s.core_sems.at[at])

    def start(self, k):
        for i in range(2):
            for j in range(2):
                self.load(k, i, j).start()

    def first(self, k, i, j):
        self.load(k, i, j).wait()
        self.scatter.first(self.scatter.order(k), i, j)

    def steps(self):
        s, part = self.scatter, functools.partial
        rounds = s.p.rounds
        out = [part(self.start, k) for k in range(rounds)]
        for k in range(rounds + 2):
            if k < rounds:
                out += [part(self.first, k, i, j) for i in range(2) for j in range(2)]
            if 0 <= k - 1 < rounds:
                for i in range(2):
                    out.append(part(s.second0, s.order(k - 1), i))
                    out.append(part(s.second1, s.order(k - 1), i))
            if 0 <= k - 2 < rounds:
                out += [part(s.third, s.order(k - 2), h) for h in range(2)]
        return out


def interleave(*groups):
    marked = []
    for n, (low, high, steps) in enumerate(groups):
        for i, step in enumerate(steps):
            marked.append((low + (high - low) * (i + 0.5) / len(steps), n, step))
    for _, _, step in sorted(marked, key=lambda m: (m[0], m[1])):
        step()


class Weights:
    def __init__(self, inputs, lg_ref, outs, router, bufs, sems):
        self.inputs, self.lg, self.outs, self.router = inputs, lg_ref, outs, router
        self.held, self.sums = bufs[:5], bufs[5:]
        self.load_sems, self.store_sems = sems
        self.groups, self.parts, self.tok, self.width = inputs[0].shape

    @staticmethod
    def scratch(local, tok, ffe, width):
        dma = pltpu.SemaphoreType.DMA
        act = pltpu.VMEM((2, local, tok, ffe), BF)
        bufs = [pltpu.VMEM((2, tok, width), BF)] * 2 + [act] * 3
        bufs += [pltpu.VMEM((2, local, width, ffe), F32)] * 2
        return bufs + [pltpu.VMEM((2, local, ffe, width), F32)], [dma((5, 2)), dma((3, 2))]

    def loads(self, step):
        t, e, slot = step // self.groups, step % self.groups, step % 2
        return [
            pltpu.make_async_copy(
                ref.at[e, t] if n < 2 else ref.at[e],
                self.held[n].at[slot],
                self.load_sems.at[n, slot],
            )
            for n, ref in enumerate(self.inputs)
        ]

    def stores(self, t):
        cols = pl.ds(pl.multiple_of(t * self.width, self.width), self.width)
        targets = (
            self.outs[0].at[:, cols, :],
            self.outs[1].at[:, cols, :],
            self.outs[2].at[:, :, cols],
        )
        return [
            pltpu.make_async_copy(total.at[t % 2], target, self.store_sems.at[i, t % 2])
            for i, (total, target) in enumerate(zip(self.sums, targets))
        ]

    def start(self):
        for copy in self.loads(0):
            copy.start()
        self.router[...] = jnp.zeros_like(self.router)

    def step(self, s):
        t, e, slot = s // self.groups, s % self.groups, s % 2
        for copy in self.loads(s):
            copy.wait()

        @pl.when(s + 1 < self.groups * self.parts)
        def _():
            for copy in self.loads(s + 1):
                copy.start()

        @pl.when(jnp.logical_and(e == 0, t >= 2))
        def _():
            for copy in self.stores(t - 2):
                copy.wait()

        @pl.when(e == 0)
        def _():
            for total in self.sums:
                total[t % 2] = jnp.zeros(total.shape[1:], F32)

        x, up, hid, gga, uga = (ref[slot] for ref in self.held)
        for j in range(hid.shape[0]):
            self.sums[0][t % 2, j] += rows_product(x, gga[j])
            self.sums[1][t % 2, j] += rows_product(x, uga[j])
            self.sums[2][t % 2, j] += rows_product(hid[j], up)
        self.router[t] += rows_product(x, self.lg[e])

        @pl.when(e == self.groups - 1)
        def _():
            for copy in self.stores(t):
                copy.start()

    def steps(self, size):
        total = self.groups * self.parts

        def chunk(first):
            def body(s, carry):
                self.step(s)
                return carry

            lax.fori_loop(first, min(first + size, total), body, 0)

        return [functools.partial(chunk, first) for first in range(0, total, size)]

    def finish(self):
        for t in (self.parts - 2, self.parts - 1):
            for copy in self.stores(t):
                copy.wait()


class Chain:
    def __init__(self, p, sends, held, up, down, done, out, sems):
        self.p, self.sends = p, sends
        self.held, self.up, self.down, self.done, self.out = held, up, down, done, out
        self.up_sems, self.down_sems, self.out_sems = sems

    def step(self, way):
        p = self.p
        high = jnp.clip(p.high + way, 0, p.rounds - 1)
        return p.high + way == high, (2 * high + p.low, p.t)

    def wait(self, ref, sem, device):
        arrived(ref, sem, self.sends.sems.at[0], device)

    def piece(self, i):
        valid = jnp.logical_and(i >= 0, i < self.p.rounds)
        return valid, jnp.clip(i, 0, self.p.rounds - 1)

    def receive(self, i, way, valid):
        buf, sems = (self.up, self.up_sems) if way > 0 else (self.down, self.down_sems)
        behind, source = self.step(-way)

        @pl.when(jnp.logical_and(valid, behind))
        def _():
            received, held = buf(i), self.held(i)
            self.wait(received, sems.at[i], source)
            held[...] = held[...] + received[...]

    def toward(self, k, way):
        valid, i = self.piece(self.p.high + way * k)
        self.receive(i, way, valid)
        buf, sems = (self.up, self.up_sems) if way > 0 else (self.down, self.down_sems)
        self.sends.start(self.held(i), buf(i), sems.at[i], self.step(way)[1], valid)

    def close(self):
        for way in (1, -1):
            self.receive(self.p.high, way, True)

    def spread(self):
        high = self.p.high
        for way in (1, -1):
            there, ahead = self.step(way)
            self.sends.start(self.done, self.out(high), self.out_sems.at[high], ahead, there)

    def follow(self, k, way, then=None):
        valid, i = self.piece(self.p.high - way * k)
        piece, sem = self.out(i), self.out_sems.at[i]

        @pl.when(valid)
        def _():
            self.wait(piece, sem, self.step(-way)[1])

        there, ahead = self.step(way)
        self.sends.start(piece, piece, sem, ahead, jnp.logical_and(valid, there))
        if then is not None:
            then(i, valid)


class Reduce:
    def __init__(self, p, refs, outs, ua, ub, bufs, sems):
        self.p, self.refs, self.outs, self.ua, self.ub = p, refs, outs, ua, ub
        self.base = 2 * p.rounds * ua
        self.a_own, self.a_y, self.a_up, self.a_down = bufs[:4]
        self.b_own, self.b_up, self.b_down, self.b_y, self.b_done = bufs[4:]
        send_sems, self.own_sems, self.y_sems = sems[:3]
        a_lines, self.ay_sems, b_lines, self.by_sems = sems[3:6], sems[6], sems[7:10], sems[10]
        self.store_sems = sems[11]
        self.sends = Sends(send_sems)

        def pieces(buf, w, size):
            return lambda i: buf.at[w, pl.ds(i * size, size)]

        self.a_chains = [
            Chain(
                p,
                self.sends,
                pieces(self.a_own, w, ua),
                pieces(self.a_up, w, ua),
                pieces(self.a_down, w, ua),
                self.a_own.at[w, pl.ds(p.high * ua, ua)],
                functools.partial(self.a_out, w, p.low),
                [line.at[w] for line in a_lines],
            )
            for w in range(len(refs))
        ]
        self.b_chains = [
            Chain(
                p,
                self.sends,
                pieces(self.b_own, w, 2 * ub),
                pieces(self.b_up, w, 2 * ub),
                pieces(self.b_down, w, 2 * ub),
                self.b_done.at[w],
                functools.partial(self.b_out, w),
                [line.at[w] for line in b_lines],
            )
            for w in range(len(refs))
        ]

    @staticmethod
    def scratch(count, rounds, ua, ub, width):
        dma = pltpu.SemaphoreType.DMA

        def blocks(n):
            return pltpu.VMEM((count, n, 16, width), BF)

        bufs = [blocks(rounds * ua)] * 4 + [blocks(2 * rounds * ub)] * 3
        bufs += [blocks(ub), blocks(2 * ub)]
        sends = count * (10 * (rounds - 1) + 8)
        line = dma((count, rounds))
        sems = [dma((sends,)), dma((count, 2)), dma((count,)), line, line, line, line]
        sems += [line, line, line, dma((count, 2)), dma((count, 2))]
        return bufs, sems

    def a_out(self, w, low, i):
        return self.outs[w].at[pl.ds((low * self.p.rounds + i) * self.ua, self.ua)]

    def b_out(self, w, i):
        return self.outs[w].at[pl.ds(self.base + 2 * i * self.ub, 2 * self.ub)]

    def wait(self, ref, sem, device):
        arrived(ref, sem, self.sends.sems.at[0], device)

    def a_rows(self, w, low):
        size = self.p.rounds * self.ua
        return self.refs[w].at[pl.ds(low * size, size)]

    def load(self, w, n):
        if n == 0:
            src, dst = self.a_rows(w, self.p.low), self.a_own.at[w]
        else:
            src = self.refs[w].at[pl.ds(self.base, 2 * self.p.rounds * self.ub)]
            dst = self.b_own.at[w]
        return pltpu.make_async_copy(src, dst, self.own_sems.at[w, n])

    def store(self, w, n):
        p = self.p
        if n == 0:
            src, dst = self.a_chains[w].done, self.a_out(w, p.low, p.high)
        else:
            src, dst = self.b_done.at[w], self.b_out(w, p.high)
        return pltpu.make_async_copy(src, dst, self.store_sems.at[w, n])

    def begin(self, w):
        p = self.p
        self.sends.start(self.a_rows(w, 1 - p.low), self.a_y.at[w], self.y_sems.at[w], p.y)
        for n in range(2):
            self.load(w, n).start()

    def b_first(self, w):
        self.load(w, 1).wait()

    def a_first(self, w):
        self.load(w, 0).wait()
        self.wait(self.a_y.at[w], self.y_sems.at[w], self.p.y)
        own = self.a_own.at[w]
        own[...] = own[...] + self.a_y[w]

    def a_pass(self, w, i, valid, src=None):
        dst = self.a_out(w, self.p.low, i)
        self.sends.start(dst if src is None else src, dst, self.ay_sems.at[w, i], self.p.y, valid)

    def a_close(self, w):
        chain = self.a_chains[w]
        chain.close()
        chain.spread()
        self.a_pass(w, self.p.high, None, chain.done)
        self.store(w, 0).start()

    def b_close(self, w):
        p = self.p
        self.b_chains[w].close()
        half = self.b_own.at[w, pl.ds((2 * p.high + 1 - p.low) * self.ub, self.ub)]
        self.sends.start(half, self.b_y.at[w], self.by_sems.at[w, 0], p.y)

    def b_pair(self, w):
        p = self.p
        self.wait(self.b_y.at[w], self.by_sems.at[w, 0], p.y)
        half = self.b_own[w, pl.ds((2 * p.high + p.low) * self.ub, self.ub)]
        done = self.b_done.at[w, pl.ds(p.low * self.ub, self.ub)]
        done[...] = half + self.b_y[w]
        self.sends.start(done, done, self.by_sems.at[w, 1], p.y)

    def b_spread(self, w):
        p = self.p
        other = self.b_done.at[w, pl.ds((1 - p.low) * self.ub, self.ub)]
        self.wait(other, self.by_sems.at[w, 1], p.y)
        self.b_chains[w].spread()
        self.store(w, 1).start()

    def streams(self, w):
        n, part = self.p.rounds, functools.partial
        a, b = self.a_chains[w], self.b_chains[w]

        def hops(move, distances, *then):
            return [[part(move, k, way, *then) for way in (1, -1)] for k in distances]

        out, back = range(n - 1, 0, -1), range(1, n)
        b_steps = [[part(self.b_first, w)]] + hops(b.toward, out)
        b_steps += [[part(self.b_close, w)], [part(self.b_pair, w)], [part(self.b_spread, w)]]
        b_steps += hops(b.follow, back)
        a_steps = [[part(self.begin, w)], [part(self.a_first, w)]] + hops(a.toward, out)
        a_steps += [[part(self.a_close, w)]] + hops(a.follow, back, part(self.a_pass, w))
        return a_steps, b_steps

    def turns(self, apart):
        count = len(self.refs)
        turns = []
        for w in range(count):
            a_steps, b_steps = self.streams(w)
            for n, step in enumerate(a_steps):
                turns.append((apart * w + n, w, 0, step))
            for n, step in enumerate(b_steps):
                turns.append((apart * w + n + 1, w, 1, step))
        turns.sort(key=lambda m: m[:3])
        return [
            [step for turn in turns if turn[0] == n for step in turn[3]]
            for n in range(turns[-1][0] + 1)
        ]

    def steps(self):
        return [step for turn in self.turns(2) for step in turn]

    def finish(self):
        p = self.p
        for w in range(len(self.refs)):
            for i in range(p.rounds):
                self.wait(self.a_out(w, 1 - p.low, i), self.ay_sems.at[w, i], p.y)
            for n in range(2):
                self.store(w, n).wait()
        self.sends.finish()


def pieces(blocks, groups):
    first = blocks * 9 // 16 // groups
    return first, blocks // groups - first


class Small:
    def __init__(self, p, ref, out, bufs, sems):
        self.p, self.small, self.small_out = p, ref, out
        self.s_own, self.s_core, self.s_x, self.s_y, self.s_z = bufs
        send_sems, self.s_pair_sems, self.s_y_sem, self.s_z_sems, self.s_gather_sems = sems
        self.sends = Sends(send_sems)

    @staticmethod
    def scratch(rounds, rows, width):
        dma = pltpu.SemaphoreType.DMA
        whole = pltpu.VMEM((2, rounds, rows, width), F32)
        half = pltpu.VMEM((rounds, rows, width), F32)
        sems = [dma((3 * rounds + 1,)), dma((2,)), dma, dma((rounds,)), dma((2, rounds))]
        return [whole, whole, whole, half, half], sems

    def wait(self, ref, sem, device):
        arrived(ref, sem, self.sends.sems.at[0], device)

    def source(self, r):
        p = self.p
        high = lax.rem(p.high + r, p.rounds)
        return high, (2 * high + p.low, p.t)

    def small_pair(self):
        p = self.p
        self.sends.start(self.small, self.s_core, self.s_pair_sems.at[0], p.c)
        self.wait(self.s_core, self.s_pair_sems.at[0], p.c)
        self.s_own[...] = self.small[...] + self.s_core[...]
        self.sends.start(self.s_own, self.s_x, self.s_pair_sems.at[1], p.x)

    def small_x(self):
        p = self.p
        self.wait(self.s_x, self.s_pair_sems.at[1], p.x)
        self.s_x[...] = self.s_x[...] + self.s_own[...]
        self.sends.start(self.s_x.at[1 - p.low], self.s_y, self.s_y_sem, p.y)

    def small_y(self):
        p = self.p
        self.wait(self.s_y, self.s_y_sem, p.y)
        self.s_y[...] = self.s_y[...] + self.s_x[p.low]
        for r in range(1, p.rounds):
            self.sends.start(
                self.s_y.at[p.far(r)], self.s_z.at[r], self.s_z_sems.at[r], p.z(r)
            )

    def small_z(self):
        p = self.p
        total = self.s_y[p.high]
        for r in range(1, p.rounds):
            self.wait(self.s_z.at[r], self.s_z_sems.at[r], self.source(r)[1])
            total += self.s_z[r]
        self.small_out[p.low, p.high] = total
        piece = self.small_out.at[p.low, p.high]
        for device in [p.z(r) for r in range(1, p.rounds)] + [p.y]:
            self.sends.start(piece, piece, self.s_gather_sems.at[p.low, p.high], device)

    def small_pass(self):
        p = self.p
        for r in range(1, p.rounds):
            high, source = self.source(r)
            piece = self.small_out.at[p.low, high]
            self.wait(piece, self.s_gather_sems.at[p.low, high], source)
            self.sends.start(piece, piece, self.s_gather_sems.at[p.low, high], p.y)

    def finish(self):
        p = self.p
        for high in range(p.rounds):
            piece = self.small_out.at[1 - p.low, high]
            self.wait(piece, self.s_gather_sems.at[1 - p.low, high], p.y)
        self.sends.finish()

    def steps(self):
        return [self.small_pair, self.small_x, self.small_y, self.small_z, self.small_pass]


def reduce_kernel(count, ua, ub, *refs):
    refs = list(refs)

    def take(n):
        taken = refs[:n]
        del refs[:n]
        return taken

    w_refs, (rest, lg, part), inputs = take(count), take(3), take(5)
    outs, (small_out, mixed), w_outs = take(count), take(2), take(3)
    bufs, sems, m_bufs, m_sems, w_bufs, w_sems = (take(n) for n in (9, 12, 5, 5, 8, 2))
    small, router = take(2)
    s_bufs, s_sems = take(6), take(7)
    p = Place(inputs[0].shape[0])
    weights = Weights(inputs, lg, w_outs, router, w_bufs, w_sems)
    weights.start()
    p.greet([p.y, p.x, p.c] + [p.z(r) for r in range(1, p.rounds)])
    reduce = Reduce(p, w_refs, outs, ua, ub, bufs, sems)
    total = Small(p, small, small_out, m_bufs, m_sems)
    scatter = Scatter(p, s_bufs, s_sems)

    def fill():
        experts = small.shape[2]
        small[...] = jnp.zeros_like(small)
        for t in range(router.shape[0]):
            both = router[t, :, :experts] + router[t, :, experts:]
            small[t // p.rounds, t % p.rounds] = both.T
        last = router.shape[0]
        small[last // p.rounds, last % p.rounds] = rest[...]

    interleave(
        (0.0, 1.0, reduce.steps()),
        (0.0, 1.0, ScatterSteps(scatter, part).steps()),
        (0.0, 0.6, weights.steps(2)),
        (0.6, 1.0, [fill] + total.steps()),
    )
    reduce.finish()
    total.finish()
    scatter.finish(mixed)
    weights.finish()


def reduce_shared(weight_grads, rest, lg, part, inputs, cid):
    groups, tensors, tok, part_width = inputs[0].shape
    count, (rows, width) = len(weight_grads), weight_grads[0].shape
    local, ffe = inputs[2].shape[1], inputs[2].shape[3]
    full = tensors * part_width
    rounds = groups // 2
    blocks = rows // 16
    ua, ub = pieces(blocks, groups)
    shape = (blocks, 16, width)
    small_shape = (2, rounds) + rest.shape
    m_bufs, m_sems = Small.scratch(rounds, small_shape[2], width)
    bufs, sems = Reduce.scratch(count, rounds, ua, ub, width)
    w_bufs, w_sems = Weights.scratch(local, tok, ffe, part_width)
    s_bufs, s_sems = Scatter.scratch(groups, tok, part_width, tok // 8 * 7)
    outs = pl.pallas_call(
        functools.partial(reduce_kernel, count, ua, ub),
        name="reduce_shared",
        in_specs=[ANY] * count + [VMEM, VMEM] + [ANY] * 6,
        out_specs=[ANY] * count + [VMEM, VMEM, ANY, ANY, ANY],
        out_shape=[jax.ShapeDtypeStruct(shape, BF)] * count
        + [
            jax.ShapeDtypeStruct(small_shape, F32),
            jax.ShapeDtypeStruct((tok, part_width), F32),
            jax.ShapeDtypeStruct((local, full, ffe), F32),
            jax.ShapeDtypeStruct((local, full, ffe), F32),
            jax.ShapeDtypeStruct((local, ffe, full), F32),
        ],
        scratch_shapes=bufs
        + sems
        + m_bufs
        + m_sems
        + w_bufs
        + w_sems
        + [
            pltpu.VMEM(small_shape, F32),
            pltpu.VMEM((tensors, part_width, lg.shape[2]), F32),
        ]
        + s_bufs
        + s_sems,
        compiler_params=pltpu.CompilerParams(
            collective_id=cid, has_side_effects=True, vmem_limit_bytes=62 * 2**20
        ),
        cost_estimate=pl.CostEstimate(
            flops=6 * groups * tok * full * ffe * local,
            bytes_accessed=count * rows * width * 8,
            transcendentals=0,
        ),
    )(*[w.reshape(shape) for w in weight_grads], rest, lg, part, *inputs)
    weight_grads = [o.reshape(rows, width) for o in outs[:count]]
    small = outs[count].reshape((-1,) + rest.shape)
    return weight_grads, small, outs[count + 1], outs[count + 2 :]


def attention_kernel(
    tokens_ref,
    seg_row_ref,
    gain1_ref,
    wq_ref,
    wk_ref,
    wv_ref,
    wo_ref,
    qg_ref,
    kg_ref,
    gain2_ref,
    cos_ref,
    sin_ref,
    x_ref,
    normed_ref,
    q_ref,
    k_ref,
    q_rot_ref,
    k_rot_ref,
    v_ref,
    att_ref,
    res_ref,
    normed_two_ref,
    scales_ref,
    sent,
    from_c,
    from_x,
    squares,
    send_sems,
    x_sems,
    c_sems,
    x_sem,
    square_sems,
):
    tok, width = tokens_ref.shape
    parts = x_ref.shape[0]
    full = parts * width
    p = Place(2)
    opposite = (p.e, 2 * (1 - p.side) + 1 - p.core)
    sends = Sends(send_sems)
    p.greet([p.x, p.c, opposite])
    sends.start(tokens_ref, x_ref.at[p.t], x_sems.at[p.t], p.x)
    sends.start(tokens_ref, x_ref.at[p.t], x_sems.at[p.t], p.c)
    x_ref[p.t] = tokens_ref[...]

    def wait(ref, sem, device):
        arrived(ref, sem, send_sems.at[0], device)

    def squared(t):
        values = x_ref[t].astype(F32)
        return jnp.sum(values * values, axis=-1, keepdims=True)

    total = squared(p.t)
    tx, tc, to = p.x[1], p.c[1], opposite[1]
    wait(x_ref.at[tx], x_sems.at[tx], p.x)
    sends.start(x_ref.at[tx], x_ref.at[tx], x_sems.at[tx], p.c)
    total += squared(tx)
    wait(x_ref.at[tc], x_sems.at[tc], p.c)
    total += squared(tc)
    wait(x_ref.at[to], x_sems.at[to], p.c)
    total += squared(to)
    scale_one = lax.rsqrt(total / full + EPSILON)
    scales_ref[:, 0:1] = scale_one
    for t in range(parts):
        normed_ref[:, t * width : (t + 1) * width] = (
            x_ref[t].astype(F32) * scale_one * gain1_ref[:, t * width : (t + 1) * width]
        ).astype(BF)
    normed = normed_ref[...]
    q_ref[...] = dot(normed, wq_ref[...])
    k_ref[...] = dot(normed, wk_ref[...])
    v_ref[...] = dot(normed, wv_ref[...]).astype(BF)
    same = as_column(seg_row_ref[...]) == seg_row_ref[...].astype(F32)
    cosine, sine = cos_ref[...], sin_ref[...]

    def turned(values, gain):
        scale = lax.rsqrt(jnp.mean(values * values, axis=-1, keepdims=True) + EPSILON)
        scaled = values * scale * gain
        return (scaled * cosine + pltpu.roll(scaled, HEAD_DIM // 2, 1) * sine).astype(BF)

    for head in range(q_ref.shape[1] // HEAD_DIM):
        cols = slice(head * HEAD_DIM, (head + 1) * HEAD_DIM)
        q_rot = turned(q_ref[:, cols], qg_ref[...])
        k_rot = turned(k_ref[:, cols], kg_ref[...])
        q_rot_ref[:, cols] = q_rot
        k_rot_ref[:, cols] = k_rot
        scores = jnp.where(same, cols_product(q_rot, k_rot) * HEAD_DIM ** (-0.5), -1e30)
        weights = jnp.exp(scores - jnp.max(scores, axis=-1, keepdims=True))
        probs = (weights / jnp.sum(weights, axis=-1, keepdims=True)).astype(BF)
        att_ref[:, cols] = dot(probs, v_ref[:, cols]).astype(BF)

    attended = att_ref[...]

    def branch(side, core):
        t = 2 * side + core
        return dot(attended, wo_ref[:, pl.ds(pl.multiple_of(t * width, width), width)])

    for i, side in enumerate((1 - p.side, p.side)):
        sent[i] = branch(side, 1 - p.core).astype(BF)
        sends.start(sent.at[i], from_c.at[side], c_sems.at[side], p.c)
    part = branch(1 - p.side, p.core)
    wait(from_c.at[1 - p.side], c_sems.at[1 - p.side], p.c)
    sent[2] = (part + from_c[1 - p.side].astype(F32)).astype(BF)
    sends.start(sent.at[2], from_x, x_sem, p.x)
    part = branch(p.side, p.core) + tokens_ref[...].astype(F32)
    wait(from_c.at[p.side], c_sems.at[p.side], p.c)
    part += from_c[p.side].astype(F32)
    wait(from_x, x_sem, p.x)
    residual = part + from_x[...].astype(F32)
    res_ref[...] = residual
    total = jnp.sum(residual * residual, axis=-1, keepdims=True)
    squares[p.t] = jnp.broadcast_to(total, (tok, 128)).T[0:8, :]
    mine = pl.ds(pl.multiple_of(p.t * width, width), width)
    for device in (p.x, p.c, opposite):
        sends.start(squares.at[p.t], squares.at[p.t], square_sems.at[p.t], device)
    for device in (p.x, p.c, opposite):
        wait(squares.at[device[1]], square_sems.at[device[1]], device)
    whole = squares[0]
    for t in range(1, parts):
        whole += squares[t]
    whole = as_column(whole[0:1, :])
    scale_two = lax.rsqrt(whole / full + EPSILON)
    scales_ref[:, 1:2] = scale_two
    normed_two_ref[...] = (residual * scale_two * gain2_ref[:, mine]).astype(BF)
    sends.finish()


def attention(
    tokens, segments, norm1_gain, wq, wk, wv, wo, query_gain, key_gain, norm2_gain, tables, cid
):
    tok, width = tokens.shape
    full, here = wq.shape
    parts = full // width
    dma = pltpu.SemaphoreType.DMA

    def shape(*dims, dtype=BF):
        return jax.ShapeDtypeStruct(dims, dtype)

    return pl.pallas_call(
        attention_kernel,
        name="attention",
        in_specs=[VMEM] * 12,
        out_specs=[VMEM] * 11,
        out_shape=[
            shape(parts, tok, width),
            shape(tok, full),
            shape(tok, here, dtype=F32),
            shape(tok, here, dtype=F32),
            shape(tok, here),
            shape(tok, here),
            shape(tok, here),
            shape(tok, here),
            shape(tok, width, dtype=F32),
            shape(tok, width),
            shape(tok, 2, dtype=F32),
        ],
        scratch_shapes=[
            pltpu.VMEM((3, tok, width), BF),
            pltpu.VMEM((2, tok, width), BF),
            pltpu.VMEM((tok, width), BF),
            pltpu.VMEM((parts, 8, tok), F32),
            dma((9,)),
            dma((parts,)),
            dma((2,)),
            dma,
            dma((parts,)),
        ],
        compiler_params=pltpu.CompilerParams(
            collective_id=cid, has_side_effects=True, vmem_limit_bytes=56 * 2**20
        ),
        cost_estimate=pl.CostEstimate(
            flops=2 * tok * full * here * 4, bytes_accessed=24 * 2**20, transcendentals=0
        ),
    )(
        tokens,
        segments[None, :],
        norm1_gain[None, :],
        wq,
        wk,
        wv,
        wo,
        query_gain[None, :],
        key_gain[None, :],
        norm2_gain[None, :],
        *tables,
    )


def backward_kernel(
    groups,
    ua,
    ub,
    grad_ref,
    res_ref,
    cot_ref,
    tokens_ref,
    scales_ref,
    gain1_ref,
    gain2_ref,
    seg_row_ref,
    qg_ref,
    kg_ref,
    cos_ref,
    sin_ref,
    normed_ref,
    q_ref,
    k_ref,
    q_rot_ref,
    k_rot_ref,
    v_ref,
    att_ref,
    wq_ref,
    wk_ref,
    wv_ref,
    wo_ref,
    tokens_grad_ref,
    wq_grad_ref,
    wk_grad_ref,
    wv_grad_ref,
    wo_grad_ref,
    norm1_ref,
    norm2_ref,
    gains_ref,
    res_grad,
    low,
    att_grad,
    dq,
    dk,
    dv,
    sent,
    from_c,
    from_x,
    means,
    send_sems,
    low_sems,
    c_sems,
    x_sem,
    mean_sems,
    *reduce_refs,
):
    tok, width = tokens_ref.shape
    parts = low.shape[0]
    full = parts * width
    p = Place(groups)
    opposite = (p.e, 2 * (1 - p.side) + 1 - p.core)
    sends = Sends(send_sems)
    partners, turns = [p.x, p.c, opposite], []
    wo_part = wo_grad_ref
    if reduce_refs:
        wo_part, bufs, sems = reduce_refs[0], reduce_refs[1:10], reduce_refs[10:]
        half = wo_part.shape[0] // 2
        halves = [pl.ds(side * half, half) for side in (p.side, 1 - p.side)]
        parts_in = [wo_part.at[rows] for rows in halves]
        parts_out = [wo_grad_ref.at[rows] for rows in halves]
        reduce = Reduce(p, parts_in, parts_out, ua, ub, bufs, sems)
        turns = reduce.turns(1)
        partners += [p.y] + [p.z(r) for r in range(1, p.rounds)]
    p.greet(partners)

    def meanwhile(count):
        for _ in range(count):
            for step in turns.pop(0) if turns else []:
                step()

    def wait(ref, sem, device):
        arrived(ref, sem, send_sems.at[0], device)

    def mean_start(n, total):
        means[n, p.t] = jnp.broadcast_to(total, (tok, 128)).T[0:8, :]
        for device in (p.x, p.c, opposite):
            sends.start(means.at[n, p.t], means.at[n, p.t], mean_sems.at[n, p.t], device)

    def mean_end(n):
        for device in (p.x, p.c, opposite):
            wait(means.at[n, device[1]], mean_sems.at[n, device[1]], device)
        whole = means[n, 0]
        for t in range(1, parts):
            whole += means[n, t]
        return as_column(whole[0:1, :]) / full

    scale_one, scale_two = scales_ref[:, 0:1], scales_ref[:, 1:2]
    grad, residual = grad_ref[...], res_ref[...]
    mine = pl.ds(pl.multiple_of(p.t * width, width), width)
    h2 = grad * gain2_ref[:, mine]
    mean_start(0, jnp.sum(h2 * residual, axis=-1, keepdims=True))
    norm2_ref[...] = jnp.sum(grad * residual * scale_two, axis=0, keepdims=True)
    upstream = cot_ref[...].astype(F32)
    res_grad[...] = upstream + scale_two * (
        h2 - residual * scale_two * scale_two * mean_end(0)
    )
    low[p.t] = res_grad[...].astype(BF)
    sends.start(low.at[p.t], low.at[p.t], low_sems.at[p.t], p.x)
    sends.start(low.at[p.t], low.at[p.t], low_sems.at[p.t], p.c)
    attended = att_ref[...]

    def through_out(t, first=False):
        blocks = wo_part.shape[0] // parts
        product = rows_product(attended, low[t]).astype(BF)
        wo_part[pl.ds(t * blocks, blocks)] = product.reshape(blocks, 16, width)
        cols = pl.ds(pl.multiple_of(t * width, width), width)
        product = cols_product(low[t], wo_ref[:, cols])
        att_grad[...] = product if first else att_grad[...] + product

    through_out(p.t, True)
    tx, tc, to = p.x[1], p.c[1], opposite[1]
    wait(low.at[tc], low_sems.at[tc], p.c)
    through_out(tc)
    meanwhile(1)
    wait(low.at[tx], low_sems.at[tx], p.x)
    sends.start(low.at[tx], low.at[tx], low_sems.at[tx], p.c)
    through_out(tx)
    wait(low.at[to], low_sems.at[to], p.c)
    through_out(to)
    meanwhile(1)

    same = as_column(seg_row_ref[...]) == seg_row_ref[...].astype(F32)
    cosine, sine = cos_ref[...], sin_ref[...]
    factor = HEAD_DIM ** (-0.5)

    def to_pre(rot_grad, pre, gain):
        normed_grad = rot_grad * cosine - pltpu.roll(rot_grad, HEAD_DIM // 2, 1) * sine
        scale = lax.rsqrt(jnp.mean(pre * pre, axis=-1, keepdims=True) + EPSILON)
        gain_grad = jnp.sum(normed_grad * pre * scale, axis=0, keepdims=True)
        return rms_backward(pre, scale, normed_grad * gain).astype(BF), gain_grad

    query_gain, key_gain = jnp.zeros((1, HEAD_DIM), F32), jnp.zeros((1, HEAD_DIM), F32)
    for head in range(q_ref.shape[1] // HEAD_DIM):
        cols = slice(head * HEAD_DIM, (head + 1) * HEAD_DIM)
        q_rot, k_rot, value = q_rot_ref[:, cols], k_rot_ref[:, cols], v_ref[:, cols]
        scores = jnp.where(same, cols_product(q_rot, k_rot) * factor, -1e30)
        weights = jnp.exp(scores - jnp.max(scores, axis=-1, keepdims=True))
        probs = weights / jnp.sum(weights, axis=-1, keepdims=True)
        out_grad = att_grad[:, cols].astype(BF)
        dv[:, cols] = rows_product(probs.astype(BF), out_grad).astype(BF)
        prob_grad = cols_product(out_grad, value)
        score_grad = (
            probs * (prob_grad - jnp.sum(probs * prob_grad, axis=-1, keepdims=True))
        ).astype(BF)
        dq[:, cols], gain_grad = to_pre(dot(score_grad, k_rot) * factor, q_ref[:, cols], qg_ref[...])
        query_gain += gain_grad
        dk[:, cols], gain_grad = to_pre(
            rows_product(score_grad, q_rot) * factor, k_ref[:, cols], kg_ref[...]
        )
        key_gain += gain_grad
        meanwhile(1)
    gains_ref[:, :HEAD_DIM] = query_gain
    gains_ref[:, HEAD_DIM:] = key_gain

    def normed_part(side, core):
        rows = pl.ds(pl.multiple_of((2 * side + core) * width, width), width)
        return (
            cols_product(dq[...], wq_ref[rows, :])
            + cols_product(dk[...], wk_ref[rows, :])
            + cols_product(dv[...], wv_ref[rows, :])
        )

    for i, side in enumerate((1 - p.side, p.side)):
        sent[i] = normed_part(side, 1 - p.core).astype(BF)
        sends.start(sent.at[i], from_c.at[side], c_sems.at[side], p.c)
    part = normed_part(1 - p.side, p.core)
    wait(from_c.at[1 - p.side], c_sems.at[1 - p.side], p.c)
    sent[2] = (part + from_c[1 - p.side].astype(F32)).astype(BF)
    sends.start(sent.at[2], from_x, x_sem, p.x)
    part = normed_part(p.side, p.core)
    meanwhile(1)
    for t in range(parts):
        rows = slice(t * width, (t + 1) * width)
        wq_grad_ref[rows, :] = rows_product(normed_ref[:, rows], dq[...]).astype(BF)
    meanwhile(1)
    wait(from_c.at[p.side], c_sems.at[p.side], p.c)
    part += from_c[p.side].astype(F32)
    wait(from_x, x_sem, p.x)
    part += from_x[...].astype(F32)
    own = tokens_ref[...].astype(F32)
    h1 = part * gain1_ref[:, mine]
    mean_start(1, jnp.sum(h1 * own, axis=-1, keepdims=True))
    norm1_ref[...] = jnp.sum(part * own * scale_one, axis=0, keepdims=True)
    meanwhile(1)
    for t in range(parts):
        rows = slice(t * width, (t + 1) * width)
        wk_grad_ref[rows, :] = rows_product(normed_ref[:, rows], dk[...]).astype(BF)
    meanwhile(1)
    for t in range(parts):
        rows = slice(t * width, (t + 1) * width)
        wv_grad_ref[rows, :] = rows_product(normed_ref[:, rows], dv[...]).astype(BF)
    tokens_grad_ref[...] = res_grad[...] + scale_one * (
        h1 - own * scale_one * scale_one * mean_end(1)
    )
    meanwhile(len(turns))
    if reduce_refs:
        reduce.finish()
    sends.finish()


def backward(groups, direct, cid, *arrays):
    tok, width = arrays[3].shape
    full, here = arrays[19].shape
    parts = full // width
    dma = pltpu.SemaphoreType.DMA

    def shape(*dims, dtype=BF):
        return jax.ShapeDtypeStruct(dims, dtype)

    outs = [
        shape(tok, width, dtype=F32),
        shape(full, here),
        shape(full, here),
        shape(full, here),
        shape(full // 16, 16, here),
        shape(1, width, dtype=F32),
        shape(1, width, dtype=F32),
        shape(1, 2 * HEAD_DIM, dtype=F32),
    ]
    scratch = [
        pltpu.VMEM((tok, width), F32),
        pltpu.VMEM((parts, tok, width), BF),
        pltpu.VMEM((tok, here), F32),
        pltpu.VMEM((tok, here), BF),
        pltpu.VMEM((tok, here), BF),
        pltpu.VMEM((tok, here), BF),
        pltpu.VMEM((3, tok, width), BF),
        pltpu.VMEM((2, tok, width), BF),
        pltpu.VMEM((tok, width), BF),
        pltpu.VMEM((2, parts, 8, tok), F32),
        dma((12,)),
        dma((parts,)),
        dma((2,)),
        dma,
        dma((2, parts)),
    ]
    out_specs = [VMEM] * len(outs)
    ua, ub = pieces(full // 32, groups)
    if direct:
        out_specs[4] = ANY
        bufs, sems = Reduce.scratch(2, groups // 2, ua, ub, width)
        scratch += [pltpu.VMEM(outs[4].shape, BF)] + bufs + sems
    return pl.pallas_call(
        functools.partial(backward_kernel, groups, ua, ub),
        name="backward",
        in_specs=[VMEM] * len(arrays),
        out_specs=out_specs,
        out_shape=outs,
        scratch_shapes=scratch,
        compiler_params=pltpu.CompilerParams(
            collective_id=cid, has_side_effects=True, vmem_limit_bytes=62 * 2**20
        ),
        cost_estimate=pl.CostEstimate(
            flops=2 * tok * full * here * 8, bytes_accessed=36 * 2**20, transcendentals=0
        ),
    )(*arrays)


def chosen_here(chosen, rank, local, j):
    columns = lax.broadcasted_iota(jnp.int32, chosen.shape, 1)
    return jnp.where(columns == rank * local + j, chosen, 0.0)


def sigmoid(values):
    return 1.0 / (1.0 + jnp.exp(-values))


def softmax(values):
    weights = jnp.exp(values - jnp.max(values, axis=-1, keepdims=True))
    return weights / jnp.sum(weights, axis=-1, keepdims=True)


def expert_backward(gate, here, g, u, v):
    s = sigmoid(g)
    gs = g * s
    hidden = (gs * u).astype(BF).astype(F32)
    gate_grad = here * jnp.sum(hidden * v, axis=-1, keepdims=True)
    hidden_grad = gate * v
    uga = (hidden_grad * gs).astype(BF)
    gga = (hidden_grad * u * s * (1.0 + g * (1.0 - s))).astype(BF)
    return gga, uga, gate_grad


def router_backward(probs, prob_grad):
    logit_grad = probs * (prob_grad - jnp.sum(probs * prob_grad, axis=-1, keepdims=True))
    high = logit_grad.astype(BF)
    return high, (logit_grad - high.astype(F32)).astype(BF)


def plain_experts(rank, x_all, up_all, mask_all, router_t, w_gate, w_up, w_down):
    local = w_gate.shape[0]

    def joined(quarters):
        return quarters.transpose(1, 0, 2).reshape(quarters.shape[1], -1)

    def quarters(values, parts):
        return values.reshape(values.shape[0], parts, -1).transpose(1, 0, 2).astype(BF)

    def block(sums, pieces):
        x_parts, up_parts, mask = pieces
        x, up, chosen = joined(x_parts), joined(up_parts), mask.astype(F32).T
        probs = softmax(cols_product(x, router_t))
        out = grad = 0.0
        prob_grad = jnp.zeros_like(probs)
        grads = [[], [], []]
        for j in range(local):
            here = chosen_here(chosen, rank, local, j)
            gate = jnp.sum(here * probs, axis=-1, keepdims=True)
            g, u, v = dot(x, w_gate[j]), dot(x, w_up[j]), cols_product(up, w_down[j])
            hidden = (gate * (g * sigmoid(g) * u).astype(BF).astype(F32)).astype(BF)
            gga, uga, gate_grad = expert_backward(gate, here, g, u, v)
            prob_grad += gate_grad
            out += dot(hidden, w_down[j])
            grad += cols_product(gga, w_gate[j]) + cols_product(uga, w_up[j])
            for n, (left, right) in enumerate(((x, gga), (x, uga), (hidden, up))):
                grads[n].append(rows_product(left, right))
        high, low = router_backward(probs, prob_grad)
        grad += dot(high, router_t) + dot(low, router_t)
        grads = [jnp.stack(g) for g in grads] + [rows_product(high, x) + rows_product(low, x)]
        parts = x_parts.shape[0]
        sums = [total + more for total, more in zip(sums, grads)]
        return sums, (quarters(out, parts), quarters(grad, parts))

    zeros = [jnp.zeros(w.shape, F32) for w in (w_gate, w_up, w_down, router_t)]
    sums, (out_part, grad_part) = lax.scan(block, zeros, (x_all, up_all, mask_all))
    return out_part, grad_part, sums[:3], sums[3]


def expert_scatter_kernel(
    x_ref,
    up_ref,
    mask_ref,
    router_t_ref,
    wg_ref,
    wu_ref,
    wd_ref,
    grad_ref,
    out_ref,
    hid_ref,
    gga_ref,
    uga_ref,
    lg_ref,
    *refs,
):
    bufs, sems = refs[:6], refs[6:13]
    x_buf, up_buf, out_buf, out_other, from_c, other, mine, hid, acts = refs[13:22]
    joined, products, probs_ref, load_sems, store_sems, weight_sems = refs[22:28]
    out_send_sems, out_sems = refs[28:]
    groups, parts, tok, width = x_ref.shape
    experts = router_t_ref.shape[0]
    local, full, ffe = wg_ref.shape
    hidden_units = local * ffe
    last = 2 * hidden_units
    p = Place(groups)
    rounds = p.rounds
    scatter = Scatter(p, bufs, sems)

    def round_of(k):
        return lax.rem(k + 1, rounds)

    def loads(k, i):
        e = scatter.block(round_of(k), i)
        return [
            pltpu.make_async_copy(
                ref.at[e, t], buf.at[i, :, pl.ds(t * width, width)], load_sems.at[n, i, t]
            )
            for t in range(parts)
            for n, (ref, buf) in enumerate(((x_ref, x_buf), (up_ref, up_buf)))
        ]

    def columns(n, j):
        return pl.ds(n * hidden_units + j * ffe, ffe)

    def weight_loads():
        return [
            pltpu.make_async_copy(ref.at[j], joined.at[:, columns(n, j)], weight_sems.at[n, j])
            for j in range(local)
            for n, ref in enumerate((wg_ref, wu_ref))
        ]

    def stores(k, i):
        e = scatter.block(round_of(k), i)
        copies = []
        for j in range(local):
            pairs = (
                (hid.at[i, :, columns(0, j)], hid_ref.at[e, j]),
                (acts.at[i, :, columns(0, j)], gga_ref.at[e, j]),
                (acts.at[i, :, columns(1, j)], uga_ref.at[e, j]),
            )
            for n, (src, dst) in enumerate(pairs):
                copies.append(pltpu.make_async_copy(src, dst, store_sems.at[n, j, i]))
        for j, side in enumerate(scatter.sides):
            src, dst = out_buf.at[i, j], out_ref.at[e, side]
            copies.append(pltpu.make_async_copy(src, dst, store_sems.at[3, j, i]))
        return copies

    def out_send(i, j):
        return remote(
            out_other.at[i, j], from_c.at[i, j], out_send_sems.at[i, j], out_sems.at[i, j], p.c
        )

    def ended(k, i):
        for copy in stores(k, i):
            copy.wait()
        for j in range(2):
            scatter.core_sent(round_of(k), i, j, other.at[i, j])
            out_send(i, j).wait_send()

    def exchanged(k, i):
        for j in range(2):
            scatter.core_add(round_of(k), i, j, mine[i, j])
            scatter.first(round_of(k), i, j)

    def compute(k, i):
        r = round_of(k)
        e = scatter.block(r, i)
        for copy in loads(k, i):
            copy.wait()

        @pl.when(k > 0)
        def _():
            ended(k - 1, i)

        chosen = mask_ref[e].astype(F32).T
        products[...] = dot(x_buf[i], joined[...])
        probs_ref[...] = softmax(products[:, last : last + experts])
        for j in range(local):
            gate = jnp.sum(
                chosen_here(chosen, p.e, local, j) * probs_ref[...], axis=-1, keepdims=True
            )
            g, u = products[:, columns(0, j)], products[:, columns(1, j)]
            hidden = (g * sigmoid(g) * u).astype(BF).astype(F32)
            hid[i, :, columns(0, j)] = (gate * hidden).astype(BF)
        if i == 0:
            pl.when(k > 0)(lambda: exchanged(k - 1, 1))
        else:
            exchanged(k, 0)

        def outputs(t):
            return dot(hid[i], wd_ref[:, pl.ds(pl.multiple_of(t * width, width), width)])

        for j, side in enumerate(scatter.sides):
            out_other[i, j] = outputs(2 * side + 1 - p.core).astype(BF)
            out_send(i, j).start()
        probs = probs_ref[...]
        prob_grad = jnp.zeros_like(probs)
        for j in range(local):
            here = chosen_here(chosen, p.e, local, j)
            gate = jnp.sum(here * probs, axis=-1, keepdims=True)
            v = cols_product(up_buf[i], wd_ref[pl.ds(j * ffe, ffe), :])
            g, u = products[:, columns(0, j)], products[:, columns(1, j)]
            gga, uga, gate_grad = expert_backward(gate, here, g, u, v)
            acts[i, :, columns(0, j)] = gga
            acts[i, :, columns(1, j)] = uga
            prob_grad += gate_grad
        high, low = router_backward(probs, prob_grad)
        both = jnp.concatenate([high, low], axis=-1)
        lg_ref[e] = both
        acts[i, :, last : last + 2 * experts] = both

        def gradients(t):
            rows = pl.ds(pl.multiple_of(t * width, width), width)
            return cols_product(acts[i], joined[rows, :]).astype(BF)

        for j, side in enumerate(scatter.sides):
            other[i, j] = gradients(2 * side + 1 - p.core)
            scatter.core(r, i, j, other.at[i, j])
        for j, side in enumerate(scatter.sides):
            total = outputs(2 * side + p.core)
            out_send(i, j).wait_recv()
            out_buf[i, j] = (total + from_c[i, j].astype(F32)).astype(BF)
        for j, side in enumerate(scatter.sides):
            mine[i, j] = gradients(2 * side + p.core)
        for copy in stores(k, i):
            copy.start()

        @pl.when(k + 1 < rounds)
        def _():
            for copy in loads(k + 1, i):
                copy.start()

    for copy in weight_loads():
        copy.start()
    for i in range(2):
        for copy in loads(0, i):
            copy.start()
        acts[i, :, last:] = jnp.zeros((tok, acts.shape[2] - last), BF)
    spare = jnp.zeros((acts.shape[2] - last - 2 * experts, full), F32)
    router = router_t_ref[...].astype(F32)
    joined[:, last:] = jnp.concatenate([router, router, spare], axis=0).T.astype(BF)
    p.greet([p.y, p.x, p.c] + [p.z(r) for r in range(1, rounds)])
    for copy in weight_loads():
        copy.wait()

    def body(k, carry):
        r1, r2 = round_of(k + rounds - 1), round_of(k + rounds - 2)

        @pl.when(k < rounds)
        def _():
            compute(k, 0)

        pl.when(k == rounds)(lambda: exchanged(rounds - 1, 1))

        @pl.when(k >= 2)
        def _():
            for h in range(2):
                scatter.third(r2, h)

        @pl.when(k < rounds)
        def _():
            compute(k, 1)

        @pl.when(jnp.logical_and(k >= 1, k <= rounds))
        def _():
            for i in range(2):
                scatter.second0(r1, i)
                scatter.second1(r1, i)

        return carry

    lax.fori_loop(0, rounds + 2, body, 0)
    scatter.finish(grad_ref)
    for i in range(2):
        ended(rounds - 1, i)


def expert_scatter(x_all, up_all, mask_all, router_t, w_gate, w_up, w_down, cid):
    groups, parts, tok, width = x_all.shape
    local, full, ffe = w_gate.shape
    experts = router_t.shape[0]
    dma = pltpu.SemaphoreType.DMA
    bufs, sems = Scatter.scratch(groups, tok, width, tok // 2)
    act = jax.ShapeDtypeStruct((groups, local, tok, ffe), BF)
    block = pltpu.VMEM((2, tok, full), BF)
    shards = pltpu.VMEM((2, 2, tok, width), BF)
    wide = 2 * local * ffe + 128
    return pl.pallas_call(
        expert_scatter_kernel,
        name="experts_scatter",
        in_specs=[ANY, ANY, VMEM, VMEM, ANY, ANY, VMEM],
        out_specs=[VMEM] + [ANY] * 4 + [VMEM],
        out_shape=[
            jax.ShapeDtypeStruct((tok, width), F32),
            jax.ShapeDtypeStruct((groups, 2, tok, width), BF),
            act,
            act,
            act,
            jax.ShapeDtypeStruct((groups, tok, 2 * experts), BF),
        ],
        scratch_shapes=bufs
        + sems
        + [block, block, shards, shards, shards, shards, shards]
        + [
            pltpu.VMEM((2, tok, local * ffe), BF),
            pltpu.VMEM((2, tok, wide), BF),
            pltpu.VMEM((full, wide), BF),
            pltpu.VMEM((tok, wide), F32),
            pltpu.VMEM((tok, experts), F32),
        ]
        + [dma((2, 2, parts)), dma((4, 2, 2)), dma((2, local)), dma((2, 2)), dma((2, 2))],
        compiler_params=pltpu.CompilerParams(
            collective_id=cid, has_side_effects=True, vmem_limit_bytes=62 * 2**20
        ),
        cost_estimate=pl.CostEstimate(
            flops=12 * groups * tok * full * ffe * local,
            bytes_accessed=groups * tok * full * 8,
            transcendentals=0,
        ),
    )(x_all, up_all, mask_all, router_t, w_gate, w_up, w_down.reshape(local * ffe, full))


def per_device(
    tokens,
    segments,
    routes,
    norm1_gain,
    w_query,
    w_key,
    w_value,
    w_out,
    query_gain,
    key_gain,
    norm2_gain,
    router,
    w_gate,
    w_up,
    w_down,
    cotangent,
):
    tok, quarter = tokens.shape
    experts = router.shape[1]
    tensors = lax.axis_size("tensor")
    groups = lax.axis_size("expert")
    tensor_rank = lax.axis_index("tensor")
    full = quarter * tensors
    direct = tensors == 4 and groups == 8 and 16 <= experts <= 32

    up_all = lax.all_gather(cotangent, BOTH, axis=0).reshape(groups, tensors, tok, quarter)
    expert_ids = jnp.arange(experts, dtype=jnp.int32)
    chosen = jnp.any(routes.T[None, :, :] == expert_ids[:, None, None], axis=1).astype(BF)

    cosine_row, sine_row = rope_tables(tok, HEAD_DIM)
    tables = (
        jnp.concatenate([cosine_row, cosine_row], axis=-1),
        jnp.concatenate([-sine_row, sine_row], axis=-1),
    )
    (
        _,
        normed,
        query_pre,
        key_pre,
        query_rot,
        key_rot,
        value_low,
        attended,
        residual,
        normed_two,
        scales,
    ) = attention(
        tokens,
        segments,
        norm1_gain,
        w_query,
        w_key,
        w_value,
        w_out,
        query_gain,
        key_gain,
        norm2_gain,
        tables,
        4,
    )
    if direct:
        x_all, mask_all = gather_all(normed_two, chosen, groups, tensors, 1)
    else:
        mask_all = lax.all_gather(chosen, "expert", axis=0)
        x_all = lax.all_gather(normed_two, BOTH, axis=0).reshape(groups, tensors, tok, quarter)

    def to_home(values):
        return lax.psum_scatter(
            values.reshape(groups * tensors, tok, quarter), BOTH, scatter_dimension=0
        ).astype(F32)

    expert_args = (x_all, up_all, mask_all, router.T, w_gate, w_up, w_down)
    if direct:
        normed_two_grad, out_part, hid, gga, uga, lg = expert_scatter(
            *expert_args, cid=2
        )
    else:
        out_part, grad_part, expert_grads, router_part = plain_experts(
            lax.axis_index("expert"), *expert_args
        )
        normed_two_grad = to_home(grad_part)

    (
        tokens_grad,
        query_w_grad,
        key_w_grad,
        value_w_grad,
        out_w_grad,
        norm1_grad,
        norm2_grad,
        gains,
    ) = backward(
        groups,
        direct,
        5,
        normed_two_grad,
        residual,
        cotangent,
        tokens,
        scales,
        norm1_gain[None, :],
        norm2_gain[None, :],
        segments[None, :],
        query_gain[None, :],
        key_gain[None, :],
        *tables,
        normed,
        query_pre,
        key_pre,
        query_rot,
        key_rot,
        value_low,
        attended,
        w_query,
        w_key,
        w_value,
        w_out,
    )

    def spread(part):
        mine = jnp.arange(tensors)[:, None] == tensor_rank
        return jnp.where(mine, part, 0.0)

    rest = jnp.concatenate(
        [
            spread(norm1_grad),
            spread(norm2_grad),
            jnp.pad(gains, ((0, 0), (0, quarter - gains.shape[1]))),
        ]
    )
    rest = jnp.pad(rest, ((0, -rest.shape[0] % 8), (0, 0)))
    weight_grads = [query_w_grad, key_w_grad, value_w_grad]
    out_w_grad = out_w_grad.reshape(full, quarter)
    if direct:
        rest = jnp.pad(rest, ((0, experts - rest.shape[0]), (0, 0)))
        weight_grads, small, moe_out, expert_grads = reduce_shared(
            weight_grads, rest, lg, out_part, (x_all, up_all, hid, gga, uga), 3
        )
        router_sum, rest = small[:tensors], small[tensors]
    else:
        moe_out = to_home(out_part)
        *weight_grads, out_w_grad = [
            lax.psum(part, "expert") for part in weight_grads + [out_w_grad]
        ]
        router_sum, rest = lax.psum(
            (router_part.reshape(experts, tensors, quarter).transpose(1, 0, 2), rest), BOTH
        )
    mixed = (residual + moe_out).astype(BF)
    weight_grads = [part.astype(F32) for part in weight_grads]
    router_sum = router_sum.transpose(0, 2, 1).reshape(full, experts)
    norm1_sum = rest[:tensors].reshape(full)
    norm2_sum = rest[tensors : 2 * tensors].reshape(full)
    query_gain_sum = rest[2 * tensors, :HEAD_DIM]
    key_gain_sum = rest[2 * tensors, HEAD_DIM : 2 * HEAD_DIM]
    out_w_sum = out_w_grad.astype(F32).reshape(tensors, quarter, quarter).transpose(1, 0, 2)
    return (
        mixed,
        tokens_grad,
        norm1_sum,
        weight_grads[0],
        weight_grads[1],
        weight_grads[2],
        out_w_sum.reshape(quarter, full),
        query_gain_sum,
        key_gain_sum,
        norm2_sum,
        router_sum,
        *expert_grads,
    )


def solution(mesh):
    return jax.shard_map(
        per_device,
        mesh=mesh,
        in_specs=(
            P("expert", "tensor"),
            P("expert"),
            P("expert", None),
            P(),
            P(None, "tensor"),
            P(None, "tensor"),
            P(None, "tensor"),
            P("tensor", None),
            P(),
            P(),
            P(),
            P(),
            P("expert", None, "tensor"),
            P("expert", None, "tensor"),
            P("expert", "tensor", None),
            P("expert", "tensor"),
        ),
        out_specs=(
            P("expert", "tensor"),
            P("expert", "tensor"),
            P(),
            P(None, "tensor"),
            P(None, "tensor"),
            P(None, "tensor"),
            P("tensor", None),
            P(),
            P(),
            P(),
            P(),
            P("expert", None, "tensor"),
            P("expert", None, "tensor"),
            P("expert", "tensor", None),
        ),
        check_vma=False,
    )
```

```python
import functools

import jax
import jax.numpy as jnp
from jax import lax
from jax.experimental import pallas as pl
from jax.experimental.pallas import tpu as pltpu
from jax.sharding import PartitionSpec as P

HEAD_DIM = 128
EPSILON = 1e-06
ROPE_BASE = 50000.0
BF = jnp.bfloat16
F32 = jnp.float32
BOTH = ("expert", "tensor")


def rms_backward(values, scale_row, grad_out):
    return scale_row * (
        grad_out
        - values * scale_row * scale_row * jnp.mean(grad_out * values, axis=-1, keepdims=True)
    )


def rope_tables(length, head_dim):
    half_dim = head_dim // 2
    frequency = ROPE_BASE ** (-jnp.arange(half_dim, dtype=F32) * 2.0 / head_dim)
    angles = jnp.arange(length, dtype=F32)[:, None] * frequency[None, :]
    return jnp.cos(angles), jnp.sin(angles)


def rows_product(left, right):
    return lax.dot_general(left, right, (((0,), (0,)), ((), ())), preferred_element_type=F32)


def cols_product(left, right):
    return lax.dot_general(left, right, (((1,), (1,)), ((), ())), preferred_element_type=F32)


def as_column(row):
    return jnp.broadcast_to(row.astype(F32), (128, row.shape[1])).T[:, 0:1]


def dot(left, right):
    return jnp.dot(left, right, preferred_element_type=F32)


ANY = pl.BlockSpec(memory_space=pl.ANY)
VMEM = pl.BlockSpec(memory_space=pltpu.VMEM)


class Place:
    def __init__(self, groups):
        self.e, self.t = lax.axis_index("expert"), lax.axis_index("tensor")
        self.rounds = groups // 2
        self.high, self.low = self.e // 2, self.e % 2
        self.side, self.core = self.t // 2, self.t % 2
        self.y = (2 * self.high + 1 - self.low, self.t)
        self.x = (self.e, 2 * (1 - self.side) + self.core)
        self.c = (self.e, 2 * self.side + 1 - self.core)

    def far(self, r):
        return lax.rem(self.high + self.rounds - r, self.rounds)

    def z(self, r):
        return (2 * self.far(r) + self.low, self.t)

    def greet(self, partners):
        barrier = pltpu.get_barrier_semaphore()
        for partner in partners:
            pl.semaphore_signal(
                barrier, inc=1, device_id=partner, device_id_type=pl.DeviceIdType.MESH
            )
        pl.semaphore_wait(barrier, len(partners))


class Sends:
    def __init__(self, sems):
        self.sems, self.copies = sems, []

    def start(self, src, dst, recv_sem, device, when=None):
        copy = remote(src, dst, self.sems.at[len(self.copies)], recv_sem, device)
        if when is None:
            copy.start()
        else:
            pl.when(when)(copy.start)
        self.copies.append((copy, when))

    def finish(self):
        for copy, when in self.copies:
            if when is None:
                copy.wait_send()
            else:
                pl.when(when)(copy.wait_send)


def remote(src, dst, send_sem, recv_sem, device):
    return pltpu.make_async_remote_copy(
        src_ref=src,
        dst_ref=dst,
        send_sem=send_sem,
        recv_sem=recv_sem,
        device_id=device,
        device_id_type=pl.DeviceIdType.MESH,
    )


def arrived(ref, recv_sem, send_sem, device):
    remote(ref, ref, send_sem, recv_sem, device).wait_recv()


def departed(ref, recv_sem, send_sem, device):
    remote(ref, ref, send_sem, recv_sem, device).wait_send()


class Moves:
    def __init__(self, pairs, sems):
        self.pairs, self.sems = pairs, sems

    def copy(self, n):
        return pltpu.make_async_copy(*self.pairs[n], self.sems.at[n])

    def start(self, *which):
        for n in which:
            self.copy(n).start()

    def wait(self, *which):
        for n in which:
            self.copy(n).wait()


def gather_kernel(
    x_ref,
    mask_ref,
    out_ref,
    masks_ref,
    send_sems,
    recv_sems,
    mask_sems,
    own_sem,
):
    groups, tok = out_ref.shape[0], out_ref.shape[2]
    half = tok // 2
    p = Place(groups)
    rounds = p.rounds
    p.greet([p.y, p.x, p.c] + [p.z(r) for r in range(1, rounds)])
    sends = Sends(send_sems)
    low2, side2 = 1 - p.low, 1 - p.side

    def shard(h, e, t):
        return out_ref.at[e, t, pl.ds(h * half, half)]

    def send(h, e, t, device, src=None):
        dst = shard(h, e, t)
        sends.start(dst if src is None else src, dst, recv_sems.at[h, e, t], device)

    def wait(h, e, t, device):
        arrived(shard(h, e, t), recv_sems.at[h, e, t], send_sems.at[0], device)

    own = pltpu.make_async_copy(x_ref, out_ref.at[p.e, p.t], own_sem)
    own.start()

    def send_mask(e, device):
        sends.start(masks_ref.at[e], masks_ref.at[e], mask_sems.at[e], device)

    masks_ref[p.e] = mask_ref[...]

    def first(r):
        e = 2 * p.far(r) + p.low
        if r > 0:
            arrived(masks_ref.at[e], mask_sems.at[e], send_sems.at[0], p.z(r))
        send_mask(e, p.y)
        for h in range(2):
            src = x_ref.at[pl.ds(h * half, half)] if r == 0 else None
            if r > 0:
                wait(h, e, p.t, p.z(r))
            send(h, e, p.t, p.x if h else p.y, src)
            send(h, e, p.t, p.y if h else p.x, src)
            send(h, e, p.t, p.c, src)

    def second(r):
        e, e2 = 2 * p.far(r) + p.low, 2 * p.far(r) + low2
        wait(0, e2, p.t, p.y)
        send(0, e2, p.t, p.x)
        send(0, e2, p.t, p.c)
        t2 = 2 * side2 + p.core
        wait(1, e, t2, p.x)
        send(1, e, t2, p.y)
        send(1, e, t2, p.c)

    def third(r):
        e, e2 = 2 * p.far(r) + p.low, 2 * p.far(r) + low2
        t2 = 2 * side2 + p.core
        wait(0, e, t2, p.x)
        send(0, e, t2, p.c)
        wait(1, e2, p.t, p.y)
        send(1, e2, p.t, p.c)
        wait(0, e2, t2, p.x)
        send(0, e2, t2, p.c)
        wait(1, e2, t2, p.y)
        send(1, e2, t2, p.c)

    for r in range(1, rounds):
        to = (2 * lax.rem(p.high + r, rounds) + p.low, p.t)
        send_mask(p.e, to)
        for h in range(2):
            send(h, p.e, p.t, to, x_ref.at[pl.ds(h * half, half)])
    for r in range(rounds + 2):
        if r < rounds:
            first(r)
        if 0 <= r - 1 < rounds:
            second(r - 1)
        if 0 <= r - 2 < rounds:
            third(r - 2)
    other = 1 - p.core
    for r in range(rounds):
        e2 = 2 * p.far(r) + low2
        arrived(masks_ref.at[e2], mask_sems.at[e2], send_sems.at[0], p.y)
        for e in (2 * p.far(r) + p.low, 2 * p.far(r) + low2):
            for t in (2 * p.side + other, 2 * side2 + other):
                for h in range(2):
                    wait(h, e, t, p.c)
    own.wait()
    sends.finish()


def gather_all(x, mask, groups, tensors, collective_id):
    tok, width = x.shape
    rounds = groups // 2
    count = 3 * (rounds - 1) + 7 * rounds + 4 * rounds + 4 * rounds
    return pl.pallas_call(
        gather_kernel,
        name="gather_all",
        in_specs=[ANY, VMEM],
        out_specs=[ANY, VMEM],
        out_shape=[
            jax.ShapeDtypeStruct((groups, tensors, tok, width), x.dtype),
            jax.ShapeDtypeStruct((groups,) + mask.shape, mask.dtype),
        ],
        scratch_shapes=[
            pltpu.SemaphoreType.DMA((count,)),
            pltpu.SemaphoreType.DMA((2, groups, tensors)),
            pltpu.SemaphoreType.DMA((groups,)),
            pltpu.SemaphoreType.DMA,
        ],
        compiler_params=pltpu.CompilerParams(
            collective_id=collective_id, has_side_effects=True, vmem_limit_bytes=62 * 2**20
        ),
        cost_estimate=pl.CostEstimate(
            flops=0, bytes_accessed=groups * tensors * tok * width * 2, transcendentals=0
        ),
    )(x, mask)


class Scatter:
    def __init__(self, p, bufs, sems):
        self.p = p
        self.total, self.from_x0, self.from_y0, self.from_x1, self.from_y1, self.from_z = bufs
        self.send_sems, self.core_sems, self.x0_sems, self.y0_sems = sems[:4]
        self.x1_sems, self.y1_sems, self.z_sems = sems[4:]
        self.tok, cut = self.total.shape[2], self.from_x0.shape[1]
        self.halves = (pl.ds(0, cut), pl.ds(cut, self.tok - cut))
        self.lows = (1 - p.low, p.low)
        self.sides = (1 - p.side, p.side)

    @staticmethod
    def scratch(groups, tok, width, cut):
        rounds, rest = groups // 2, tok - cut
        dma = pltpu.SemaphoreType.DMA
        bufs = [
            pltpu.VMEM((groups, 2, tok, width), BF),
            pltpu.VMEM((groups, cut, width), BF),
            pltpu.VMEM((rounds, cut, width), BF),
            pltpu.VMEM((rounds, rest, width), BF),
            pltpu.VMEM((rounds, 2, rest, width), BF),
            pltpu.VMEM((rounds, tok, width), BF),
        ]
        sems = [
            dma((12, rounds)),
            dma((groups, 2)),
            dma((groups,)),
            dma((rounds,)),
            dma((rounds,)),
            dma((rounds, 2)),
            dma((rounds, 2)),
        ]
        return bufs, sems

    def order(self, k):
        return (k + 1) % self.p.rounds

    def block(self, r, i):
        return 2 * self.p.far(r) + self.lows[i]

    def wait(self, ref, sem, device):
        arrived(ref, sem, self.send_sems.at[0, 0], device)

    def send(self, n, r, src, dst, sem, device):
        remote(src, dst, self.send_sems.at[n, r], sem, device).start()

    def add(self, target, received):
        self.total[target] = self.total[target] + received

    def core(self, r, i, j, src):
        e, side = self.block(r, i), self.sides[j]
        dst, sem = self.total.at[e, side], self.core_sems.at[e, side]
        self.send(2 * i + j, r, src, dst, sem, self.p.c)

    def core_sent(self, r, i, j, src):
        departed(src, self.core_sems.at[0, 0], self.send_sems.at[2 * i + j, r], self.p.c)

    def core_add(self, r, i, j, mine):
        e, side = self.block(r, i), self.sides[j]
        self.wait(self.total.at[e, side], self.core_sems.at[e, side], self.p.c)
        self.total[e, side] = self.total[e, side] + mine

    def first(self, r, i, j):
        p, (h0, h1) = self.p, self.halves
        e, far, side = self.block(r, i), p.far(r), self.sides[j]
        if j == 0:
            src = self.total.at[e, side, h0]
            self.send(4 + i, r, src, self.from_x0.at[e], self.x0_sems.at[e], p.x)
        if i == 0:
            src, dst = self.total.at[e, side, h1], self.from_y1.at[far, side]
            self.send(6 + j, r, src, dst, self.y1_sems.at[far, side], p.y)

    def second0(self, r, i):
        p, far, e = self.p, self.p.far(r), self.block(r, i)
        rows = self.halves[0]
        self.wait(self.from_x0.at[e], self.x0_sems.at[e], p.x)
        self.add((e, p.side, rows), self.from_x0[e])
        if i == 0:
            src = self.total.at[e, p.side, rows]
            self.send(8, r, src, self.from_y0.at[far], self.y0_sems.at[far], p.y)

    def second1(self, r, j):
        p, far, side = self.p, self.p.far(r), self.sides[j]
        e, rows = 2 * far + p.low, self.halves[1]
        self.wait(self.from_y1.at[far, side], self.y1_sems.at[far, side], p.y)
        self.add((e, side, rows), self.from_y1[far, side])
        if j == 0:
            src = self.total.at[e, side, rows]
            self.send(9, r, src, self.from_x1.at[far], self.x1_sems.at[far], p.x)

    def third(self, r, h):
        p, far = self.p, self.p.far(r)
        e, rows = 2 * far + p.low, self.halves[h]
        if h == 0:
            received, sem, device = self.from_y0, self.y0_sems, p.y
        else:
            received, sem, device = self.from_x1, self.x1_sems, p.x
        self.wait(received.at[far], sem.at[far], device)
        self.add((e, p.side, rows), received[far])

        @pl.when(r > 0)
        def _():
            src, dst = self.total.at[e, p.side, rows], self.from_z.at[r, rows]
            self.send(10 + h, r, src, dst, self.z_sems.at[r, h], p.z(r))

    def finish(self, out_ref):
        p = self.p
        for h, rows in enumerate(self.halves):
            total = self.total[p.e, p.side, rows].astype(F32)
            for r in range(1, p.rounds):
                source = (2 * lax.rem(p.high + r, p.rounds) + p.low, p.t)
                self.wait(self.from_z.at[r, rows], self.z_sems.at[r, h], source)
                total += self.from_z[r, rows].astype(F32)
            out_ref[rows, :] = total
        h0, h1 = self.halves
        for r in range(p.rounds):
            ends = [(4, h0, p.x), (5, h0, p.x), (6, h1, p.y), (7, h1, p.y), (8, h0, p.y)]
            ends += [(9, h1, p.x)]
            if r > 0:
                ends += [(10, h0, p.z(r)), (11, h1, p.z(r))]
            for n, rows, device in ends:
                departed(
                    self.total.at[0, 0, rows],
                    self.core_sems.at[0, 0],
                    self.send_sems.at[n, r],
                    device,
                )


class ScatterSteps:
    def __init__(self, scatter, part_ref):
        self.scatter, self.part = scatter, part_ref

    def load(self, k, i, j):
        s = self.scatter
        at = (s.block(s.order(k), i), s.sides[j])
        return pltpu.make_async_copy(self.part.at[at], s.total.at[at], s.core_sems.at[at])

    def start(self, k):
        for i in range(2):
            for j in range(2):
                self.load(k, i, j).start()

    def first(self, k, i, j):
        self.load(k, i, j).wait()
        self.scatter.first(self.scatter.order(k), i, j)

    def steps(self):
        s, part = self.scatter, functools.partial
        rounds = s.p.rounds
        out = [part(self.start, k) for k in range(rounds)]
        for k in range(rounds + 2):
            if k < rounds:
                out += [part(self.first, k, i, j) for i in range(2) for j in range(2)]
            if 0 <= k - 1 < rounds:
                for i in range(2):
                    out.append(part(s.second0, s.order(k - 1), i))
                    out.append(part(s.second1, s.order(k - 1), i))
            if 0 <= k - 2 < rounds:
                out += [part(s.third, s.order(k - 2), h) for h in range(2)]
        return out


def interleave(*groups):
    marked = []
    for n, (low, high, steps) in enumerate(groups):
        for i, step in enumerate(steps):
            marked.append((low + (high - low) * (i + 0.5) / len(steps), n, step))
    for _, _, step in sorted(marked, key=lambda m: (m[0], m[1])):
        step()


class Weights:
    def __init__(self, inputs, lg_ref, outs, router, bufs, sems):
        self.inputs, self.lg, self.outs, self.router = inputs, lg_ref, outs, router
        self.held, self.sums = bufs[:5], bufs[5:]
        self.load_sems, self.store_sems = sems
        self.groups, self.parts, self.tok, self.width = inputs[0].shape

    @staticmethod
    def scratch(local, tok, ffe, width):
        dma = pltpu.SemaphoreType.DMA
        act = pltpu.VMEM((2, local, tok, ffe), BF)
        bufs = [pltpu.VMEM((2, tok, width), BF)] * 2 + [act] * 3
        bufs += [pltpu.VMEM((2, local, width, ffe), F32)] * 2
        return bufs + [pltpu.VMEM((2, local, ffe, width), F32)], [dma((5, 2)), dma((3, 2))]

    def loads(self, step):
        t, e, slot = step // self.groups, step % self.groups, step % 2
        return [
            pltpu.make_async_copy(
                ref.at[e, t] if n < 2 else ref.at[e],
                self.held[n].at[slot],
                self.load_sems.at[n, slot],
            )
            for n, ref in enumerate(self.inputs)
        ]

    def stores(self, t):
        cols = pl.ds(pl.multiple_of(t * self.width, self.width), self.width)
        targets = (
            self.outs[0].at[:, cols, :],
            self.outs[1].at[:, cols, :],
            self.outs[2].at[:, :, cols],
        )
        return [
            pltpu.make_async_copy(total.at[t % 2], target, self.store_sems.at[i, t % 2])
            for i, (total, target) in enumerate(zip(self.sums, targets))
        ]

    def start(self):
        for copy in self.loads(0):
            copy.start()
        self.router[...] = jnp.zeros_like(self.router)

    def step(self, s):
        t, e, slot = s // self.groups, s % self.groups, s % 2
        for copy in self.loads(s):
            copy.wait()

        @pl.when(s + 1 < self.groups * self.parts)
        def _():
            for copy in self.loads(s + 1):
                copy.start()

        @pl.when(jnp.logical_and(e == 0, t >= 2))
        def _():
            for copy in self.stores(t - 2):
                copy.wait()

        @pl.when(e == 0)
        def _():
            for total in self.sums:
                total[t % 2] = jnp.zeros(total.shape[1:], F32)

        x, up, hid, gga, uga = (ref[slot] for ref in self.held)
        for j in range(hid.shape[0]):
            self.sums[0][t % 2, j] += rows_product(x, gga[j])
            self.sums[1][t % 2, j] += rows_product(x, uga[j])
            self.sums[2][t % 2, j] += rows_product(hid[j], up)
        self.router[t] += rows_product(x, self.lg[e])

        @pl.when(e == self.groups - 1)
        def _():
            for copy in self.stores(t):
                copy.start()

    def steps(self, size):
        total = self.groups * self.parts

        def chunk(first):
            def body(s, carry):
                self.step(s)
                return carry

            lax.fori_loop(first, min(first + size, total), body, 0)

        return [functools.partial(chunk, first) for first in range(0, total, size)]

    def finish(self):
        for t in (self.parts - 2, self.parts - 1):
            for copy in self.stores(t):
                copy.wait()


class Chain:
    def __init__(self, p, sends, held, up, down, done, out, sems):
        self.p, self.sends = p, sends
        self.held, self.up, self.down, self.done, self.out = held, up, down, done, out
        self.up_sems, self.down_sems, self.out_sems = sems

    def step(self, way):
        p = self.p
        high = jnp.clip(p.high + way, 0, p.rounds - 1)
        return p.high + way == high, (2 * high + p.low, p.t)

    def wait(self, ref, sem, device):
        arrived(ref, sem, self.sends.sems.at[0], device)

    def piece(self, i):
        valid = jnp.logical_and(i >= 0, i < self.p.rounds)
        return valid, jnp.clip(i, 0, self.p.rounds - 1)

    def receive(self, i, way, valid):
        buf, sems = (self.up, self.up_sems) if way > 0 else (self.down, self.down_sems)
        behind, source = self.step(-way)

        @pl.when(jnp.logical_and(valid, behind))
        def _():
            received, held = buf(i), self.held(i)
            self.wait(received, sems.at[i], source)
            held[...] = held[...] + received[...]

    def toward(self, k, way):
        valid, i = self.piece(self.p.high + way * k)
        self.receive(i, way, valid)
        buf, sems = (self.up, self.up_sems) if way > 0 else (self.down, self.down_sems)
        self.sends.start(self.held(i), buf(i), sems.at[i], self.step(way)[1], valid)

    def close(self):
        for way in (1, -1):
            self.receive(self.p.high, way, True)

    def spread(self):
        high = self.p.high
        for way in (1, -1):
            there, ahead = self.step(way)
            self.sends.start(self.done, self.out(high), self.out_sems.at[high], ahead, there)

    def follow(self, k, way, then=None):
        valid, i = self.piece(self.p.high - way * k)
        piece, sem = self.out(i), self.out_sems.at[i]

        @pl.when(valid)
        def _():
            self.wait(piece, sem, self.step(-way)[1])

        there, ahead = self.step(way)
        self.sends.start(piece, piece, sem, ahead, jnp.logical_and(valid, there))
        if then is not None:
            then(i, valid)


class Reduce:
    def __init__(self, p, refs, outs, ua, ub, bufs, sems):
        self.p, self.refs, self.outs, self.ua, self.ub = p, refs, outs, ua, ub
        self.base = 2 * p.rounds * ua
        self.a_own, self.a_y, self.a_up, self.a_down = bufs[:4]
        self.b_own, self.b_up, self.b_down, self.b_y, self.b_done = bufs[4:]
        send_sems, self.own_sems, self.y_sems = sems[:3]
        a_lines, self.ay_sems, b_lines, self.by_sems = sems[3:6], sems[6], sems[7:10], sems[10]
        self.store_sems = sems[11]
        self.sends = Sends(send_sems)

        def pieces(buf, w, size):
            return lambda i: buf.at[w, pl.ds(i * size, size)]

        self.a_chains = [
            Chain(
                p,
                self.sends,
                pieces(self.a_own, w, ua),
                pieces(self.a_up, w, ua),
                pieces(self.a_down, w, ua),
                self.a_own.at[w, pl.ds(p.high * ua, ua)],
                functools.partial(self.a_out, w, p.low),
                [line.at[w] for line in a_lines],
            )
            for w in range(len(refs))
        ]
        self.b_chains = [
            Chain(
                p,
                self.sends,
                pieces(self.b_own, w, 2 * ub),
                pieces(self.b_up, w, 2 * ub),
                pieces(self.b_down, w, 2 * ub),
                self.b_done.at[w],
                functools.partial(self.b_out, w),
                [line.at[w] for line in b_lines],
            )
            for w in range(len(refs))
        ]

    @staticmethod
    def scratch(count, rounds, ua, ub, width):
        dma = pltpu.SemaphoreType.DMA

        def blocks(n):
            return pltpu.VMEM((count, n, 16, width), BF)

        bufs = [blocks(rounds * ua)] * 4 + [blocks(2 * rounds * ub)] * 3
        bufs += [blocks(ub), blocks(2 * ub)]
        sends = count * (10 * (rounds - 1) + 8)
        line = dma((count, rounds))
        sems = [dma((sends,)), dma((count, 2)), dma((count,)), line, line, line, line]
        sems += [line, line, line, dma((count, 2)), dma((count, 2))]
        return bufs, sems

    def a_out(self, w, low, i):
        return self.outs[w].at[pl.ds((low * self.p.rounds + i) * self.ua, self.ua)]

    def b_out(self, w, i):
        return self.outs[w].at[pl.ds(self.base + 2 * i * self.ub, 2 * self.ub)]

    def wait(self, ref, sem, device):
        arrived(ref, sem, self.sends.sems.at[0], device)

    def a_rows(self, w, low):
        size = self.p.rounds * self.ua
        return self.refs[w].at[pl.ds(low * size, size)]

    def load(self, w, n):
        if n == 0:
            src, dst = self.a_rows(w, self.p.low), self.a_own.at[w]
        else:
            src = self.refs[w].at[pl.ds(self.base, 2 * self.p.rounds * self.ub)]
            dst = self.b_own.at[w]
        return pltpu.make_async_copy(src, dst, self.own_sems.at[w, n])

    def store(self, w, n):
        p = self.p
        if n == 0:
            src, dst = self.a_chains[w].done, self.a_out(w, p.low, p.high)
        else:
            src, dst = self.b_done.at[w], self.b_out(w, p.high)
        return pltpu.make_async_copy(src, dst, self.store_sems.at[w, n])

    def begin(self, w):
        p = self.p
        self.sends.start(self.a_rows(w, 1 - p.low), self.a_y.at[w], self.y_sems.at[w], p.y)
        for n in range(2):
            self.load(w, n).start()

    def b_first(self, w):
        self.load(w, 1).wait()

    def a_first(self, w):
        self.load(w, 0).wait()
        self.wait(self.a_y.at[w], self.y_sems.at[w], self.p.y)
        own = self.a_own.at[w]
        own[...] = own[...] + self.a_y[w]

    def a_pass(self, w, i, valid, src=None):
        dst = self.a_out(w, self.p.low, i)
        self.sends.start(dst if src is None else src, dst, self.ay_sems.at[w, i], self.p.y, valid)

    def a_close(self, w):
        chain = self.a_chains[w]
        chain.close()
        chain.spread()
        self.a_pass(w, self.p.high, None, chain.done)
        self.store(w, 0).start()

    def b_close(self, w):
        p = self.p
        self.b_chains[w].close()
        half = self.b_own.at[w, pl.ds((2 * p.high + 1 - p.low) * self.ub, self.ub)]
        self.sends.start(half, self.b_y.at[w], self.by_sems.at[w, 0], p.y)

    def b_pair(self, w):
        p = self.p
        self.wait(self.b_y.at[w], self.by_sems.at[w, 0], p.y)
        half = self.b_own[w, pl.ds((2 * p.high + p.low) * self.ub, self.ub)]
        done = self.b_done.at[w, pl.ds(p.low * self.ub, self.ub)]
        done[...] = half + self.b_y[w]
        self.sends.start(done, done, self.by_sems.at[w, 1], p.y)

    def b_spread(self, w):
        p = self.p
        other = self.b_done.at[w, pl.ds((1 - p.low) * self.ub, self.ub)]
        self.wait(other, self.by_sems.at[w, 1], p.y)
        self.b_chains[w].spread()
        self.store(w, 1).start()

    def streams(self, w):
        n, part = self.p.rounds, functools.partial
        a, b = self.a_chains[w], self.b_chains[w]

        def hops(move, distances, *then):
            return [[part(move, k, way, *then) for way in (1, -1)] for k in distances]

        out, back = range(n - 1, 0, -1), range(1, n)
        b_steps = [[part(self.b_first, w)]] + hops(b.toward, out)
        b_steps += [[part(self.b_close, w)], [part(self.b_pair, w)], [part(self.b_spread, w)]]
        b_steps += hops(b.follow, back)
        a_steps = [[part(self.begin, w)], [part(self.a_first, w)]] + hops(a.toward, out)
        a_steps += [[part(self.a_close, w)]] + hops(a.follow, back, part(self.a_pass, w))
        return a_steps, b_steps

    def turns(self, apart):
        count = len(self.refs)
        turns = []
        for w in range(count):
            a_steps, b_steps = self.streams(w)
            for n, step in enumerate(a_steps):
                turns.append((apart * w + n, w, 0, step))
            for n, step in enumerate(b_steps):
                turns.append((apart * w + n + 1, w, 1, step))
        turns.sort(key=lambda m: m[:3])
        return [
            [step for turn in turns if turn[0] == n for step in turn[3]]
            for n in range(turns[-1][0] + 1)
        ]

    def steps(self):
        return [step for turn in self.turns(2) for step in turn]

    def finish(self):
        p = self.p
        for w in range(len(self.refs)):
            for i in range(p.rounds):
                self.wait(self.a_out(w, 1 - p.low, i), self.ay_sems.at[w, i], p.y)
            for n in range(2):
                self.store(w, n).wait()
        self.sends.finish()


def pieces(blocks, groups):
    first = blocks * 9 // 16 // groups
    return first, blocks // groups - first


class Small:
    def __init__(self, p, ref, out, bufs, sems):
        self.p, self.small, self.small_out = p, ref, out
        self.s_own, self.s_core, self.s_x, self.s_y, self.s_z = bufs
        send_sems, self.s_pair_sems, self.s_y_sem, self.s_z_sems, self.s_gather_sems = sems
        self.sends = Sends(send_sems)

    @staticmethod
    def scratch(rounds, rows, width):
        dma = pltpu.SemaphoreType.DMA
        whole = pltpu.VMEM((2, rounds, rows, width), F32)
        half = pltpu.VMEM((rounds, rows, width), F32)
        sems = [dma((3 * rounds + 1,)), dma((2,)), dma, dma((rounds,)), dma((2, rounds))]
        return [whole, whole, whole, half, half], sems

    def wait(self, ref, sem, device):
        arrived(ref, sem, self.sends.sems.at[0], device)

    def source(self, r):
        p = self.p
        high = lax.rem(p.high + r, p.rounds)
        return high, (2 * high + p.low, p.t)

    def small_pair(self):
        p = self.p
        self.sends.start(self.small, self.s_core, self.s_pair_sems.at[0], p.c)
        self.wait(self.s_core, self.s_pair_sems.at[0], p.c)
        self.s_own[...] = self.small[...] + self.s_core[...]
        self.sends.start(self.s_own, self.s_x, self.s_pair_sems.at[1], p.x)

    def small_x(self):
        p = self.p
        self.wait(self.s_x, self.s_pair_sems.at[1], p.x)
        self.s_x[...] = self.s_x[...] + self.s_own[...]
        self.sends.start(self.s_x.at[1 - p.low], self.s_y, self.s_y_sem, p.y)

    def small_y(self):
        p = self.p
        self.wait(self.s_y, self.s_y_sem, p.y)
        self.s_y[...] = self.s_y[...] + self.s_x[p.low]
        for r in range(1, p.rounds):
            self.sends.start(
                self.s_y.at[p.far(r)], self.s_z.at[r], self.s_z_sems.at[r], p.z(r)
            )

    def small_z(self):
        p = self.p
        total = self.s_y[p.high]
        for r in range(1, p.rounds):
            self.wait(self.s_z.at[r], self.s_z_sems.at[r], self.source(r)[1])
            total += self.s_z[r]
        self.small_out[p.low, p.high] = total
        piece = self.small_out.at[p.low, p.high]
        for device in [p.z(r) for r in range(1, p.rounds)] + [p.y]:
            self.sends.start(piece, piece, self.s_gather_sems.at[p.low, p.high], device)

    def small_pass(self):
        p = self.p
        for r in range(1, p.rounds):
            high, source = self.source(r)
            piece = self.small_out.at[p.low, high]
            self.wait(piece, self.s_gather_sems.at[p.low, high], source)
            self.sends.start(piece, piece, self.s_gather_sems.at[p.low, high], p.y)

    def finish(self):
        p = self.p
        for high in range(p.rounds):
            piece = self.small_out.at[1 - p.low, high]
            self.wait(piece, self.s_gather_sems.at[1 - p.low, high], p.y)
        self.sends.finish()

    def steps(self):
        return [self.small_pair, self.small_x, self.small_y, self.small_z, self.small_pass]


def reduce_kernel(count, ua, ub, *refs):
    refs = list(refs)

    def take(n):
        taken = refs[:n]
        del refs[:n]
        return taken

    w_refs, (rest, lg, part), inputs = take(count), take(3), take(5)
    outs, (small_out, mixed), w_outs = take(count), take(2), take(3)
    bufs, sems, m_bufs, m_sems, w_bufs, w_sems = (take(n) for n in (9, 12, 5, 5, 8, 2))
    small, router = take(2)
    s_bufs, s_sems = take(6), take(7)
    p = Place(inputs[0].shape[0])
    weights = Weights(inputs, lg, w_outs, router, w_bufs, w_sems)
    weights.start()
    p.greet([p.y, p.x, p.c] + [p.z(r) for r in range(1, p.rounds)])
    reduce = Reduce(p, w_refs, outs, ua, ub, bufs, sems)
    total = Small(p, small, small_out, m_bufs, m_sems)
    scatter = Scatter(p, s_bufs, s_sems)

    def fill():
        experts = small.shape[2]
        small[...] = jnp.zeros_like(small)
        for t in range(router.shape[0]):
            both = router[t, :, :experts] + router[t, :, experts:]
            small[t // p.rounds, t % p.rounds] = both.T
        last = router.shape[0]
        small[last // p.rounds, last % p.rounds] = rest[...]

    interleave(
        (0.0, 1.0, reduce.steps()),
        (0.0, 1.0, ScatterSteps(scatter, part).steps()),
        (0.0, 0.6, weights.steps(2)),
        (0.6, 1.0, [fill] + total.steps()),
    )
    reduce.finish()
    total.finish()
    scatter.finish(mixed)
    weights.finish()


def reduce_shared(weight_grads, rest, lg, part, inputs, cid):
    groups, tensors, tok, part_width = inputs[0].shape
    count, (rows, width) = len(weight_grads), weight_grads[0].shape
    local, ffe = inputs[2].shape[1], inputs[2].shape[3]
    full = tensors * part_width
    rounds = groups // 2
    blocks = rows // 16
    ua, ub = pieces(blocks, groups)
    shape = (blocks, 16, width)
    small_shape = (2, rounds) + rest.shape
    m_bufs, m_sems = Small.scratch(rounds, small_shape[2], width)
    bufs, sems = Reduce.scratch(count, rounds, ua, ub, width)
    w_bufs, w_sems = Weights.scratch(local, tok, ffe, part_width)
    s_bufs, s_sems = Scatter.scratch(groups, tok, part_width, tok // 8 * 7)
    outs = pl.pallas_call(
        functools.partial(reduce_kernel, count, ua, ub),
        name="reduce_shared",
        in_specs=[ANY] * count + [VMEM, VMEM] + [ANY] * 6,
        out_specs=[ANY] * count + [VMEM, VMEM, ANY, ANY, ANY],
        out_shape=[jax.ShapeDtypeStruct(shape, BF)] * count
        + [
            jax.ShapeDtypeStruct(small_shape, F32),
            jax.ShapeDtypeStruct((tok, part_width), F32),
            jax.ShapeDtypeStruct((local, full, ffe), F32),
            jax.ShapeDtypeStruct((local, full, ffe), F32),
            jax.ShapeDtypeStruct((local, ffe, full), F32),
        ],
        scratch_shapes=bufs
        + sems
        + m_bufs
        + m_sems
        + w_bufs
        + w_sems
        + [
            pltpu.VMEM(small_shape, F32),
            pltpu.VMEM((tensors, part_width, lg.shape[2]), F32),
        ]
        + s_bufs
        + s_sems,
        compiler_params=pltpu.CompilerParams(
            collective_id=cid, has_side_effects=True, vmem_limit_bytes=62 * 2**20
        ),
        cost_estimate=pl.CostEstimate(
            flops=6 * groups * tok * full * ffe * local,
            bytes_accessed=count * rows * width * 8,
            transcendentals=0,
        ),
    )(*[w.reshape(shape) for w in weight_grads], rest, lg, part, *inputs)
    weight_grads = [o.reshape(rows, width) for o in outs[:count]]
    small = outs[count].reshape((-1,) + rest.shape)
    return weight_grads, small, outs[count + 1], outs[count + 2 :]


def attention_kernel(
    tokens_ref,
    seg_row_ref,
    gain1_ref,
    wq_hbm,
    wk_hbm,
    wv_hbm,
    wo_hbm,
    qg_ref,
    kg_ref,
    gain2_ref,
    cos_ref,
    sin_ref,
    normed_hbm,
    q_hbm,
    k_hbm,
    q_rot_hbm,
    k_rot_hbm,
    v_hbm,
    att_hbm,
    res_ref,
    normed_two_ref,
    scales_ref,
    x_ref,
    wq_ref,
    wk_ref,
    wv_ref,
    wo_ref,
    normed_ref,
    q_ref,
    k_ref,
    q_rot_ref,
    k_rot_ref,
    v_ref,
    att_ref,
    move_sems,
    sent,
    from_c,
    from_x,
    squares,
    send_sems,
    x_sems,
    c_sems,
    x_sem,
    square_sems,
):
    tok, width = tokens_ref.shape
    parts = x_ref.shape[0]
    full = parts * width
    p = Place(2)
    opposite = (p.e, 2 * (1 - p.side) + 1 - p.core)
    sends = Sends(send_sems)
    moves = Moves(
        [
            (wq_hbm, wq_ref),
            (wk_hbm, wk_ref),
            (wv_hbm, wv_ref),
            (wo_hbm, wo_ref),
            (normed_ref, normed_hbm),
            (q_ref, q_hbm),
            (k_ref, k_hbm),
            (v_ref, v_hbm),
            (q_rot_ref, q_rot_hbm),
            (k_rot_ref, k_rot_hbm),
            (att_ref, att_hbm),
        ],
        move_sems,
    )
    moves.start(0, 1, 2, 3)
    p.greet([p.x, p.c, opposite])
    sends.start(tokens_ref, x_ref.at[p.t], x_sems.at[p.t], p.x)
    sends.start(tokens_ref, x_ref.at[p.t], x_sems.at[p.t], p.c)
    x_ref[p.t] = tokens_ref[...]

    def wait(ref, sem, device):
        arrived(ref, sem, send_sems.at[0], device)

    def squared(t):
        values = x_ref[t].astype(F32)
        return jnp.sum(values * values, axis=-1, keepdims=True)

    total = squared(p.t)
    tx, tc, to = p.x[1], p.c[1], opposite[1]
    wait(x_ref.at[tx], x_sems.at[tx], p.x)
    sends.start(x_ref.at[tx], x_ref.at[tx], x_sems.at[tx], p.c)
    total += squared(tx)
    wait(x_ref.at[tc], x_sems.at[tc], p.c)
    total += squared(tc)
    wait(x_ref.at[to], x_sems.at[to], p.c)
    total += squared(to)
    scale_one = lax.rsqrt(total / full + EPSILON)
    scales_ref[:, 0:1] = scale_one
    for t in range(parts):
        normed_ref[:, t * width : (t + 1) * width] = (
            x_ref[t].astype(F32) * scale_one * gain1_ref[:, t * width : (t + 1) * width]
        ).astype(BF)
    moves.start(4)
    normed = normed_ref[...]
    moves.wait(0, 1, 2)
    q_ref[...] = dot(normed, wq_ref[...])
    k_ref[...] = dot(normed, wk_ref[...])
    v_ref[...] = dot(normed, wv_ref[...]).astype(BF)
    moves.start(5, 6, 7)
    same = as_column(seg_row_ref[...]) == seg_row_ref[...].astype(F32)
    cosine, sine = cos_ref[...], sin_ref[...]

    def turned(values, gain):
        scale = lax.rsqrt(jnp.mean(values * values, axis=-1, keepdims=True) + EPSILON)
        scaled = values * scale * gain
        return (scaled * cosine + pltpu.roll(scaled, HEAD_DIM // 2, 1) * sine).astype(BF)

    for head in range(q_ref.shape[1] // HEAD_DIM):
        cols = slice(head * HEAD_DIM, (head + 1) * HEAD_DIM)
        q_rot = turned(q_ref[:, cols], qg_ref[...])
        k_rot = turned(k_ref[:, cols], kg_ref[...])
        q_rot_ref[:, cols] = q_rot
        k_rot_ref[:, cols] = k_rot
        scores = jnp.where(same, cols_product(q_rot, k_rot) * HEAD_DIM ** (-0.5), -1e30)
        weights = jnp.exp(scores - jnp.max(scores, axis=-1, keepdims=True))
        probs = (weights / jnp.sum(weights, axis=-1, keepdims=True)).astype(BF)
        att_ref[:, cols] = dot(probs, v_ref[:, cols]).astype(BF)

    moves.start(8, 9, 10)
    moves.wait(3)
    attended = att_ref[...]

    def branch(side, core):
        t = 2 * side + core
        return dot(attended, wo_ref[:, pl.ds(pl.multiple_of(t * width, width), width)])

    for i, side in enumerate((1 - p.side, p.side)):
        sent[i] = branch(side, 1 - p.core).astype(BF)
        sends.start(sent.at[i], from_c.at[side], c_sems.at[side], p.c)
    part = branch(1 - p.side, p.core)
    wait(from_c.at[1 - p.side], c_sems.at[1 - p.side], p.c)
    sent[2] = (part + from_c[1 - p.side].astype(F32)).astype(BF)
    sends.start(sent.at[2], from_x, x_sem, p.x)
    part = branch(p.side, p.core) + tokens_ref[...].astype(F32)
    wait(from_c.at[p.side], c_sems.at[p.side], p.c)
    part += from_c[p.side].astype(F32)
    wait(from_x, x_sem, p.x)
    residual = part + from_x[...].astype(F32)
    res_ref[...] = residual
    total = jnp.sum(residual * residual, axis=-1, keepdims=True)
    squares[p.t] = jnp.broadcast_to(total, (tok, 128)).T[0:8, :]
    mine = pl.ds(pl.multiple_of(p.t * width, width), width)
    for device in (p.x, p.c, opposite):
        sends.start(squares.at[p.t], squares.at[p.t], square_sems.at[p.t], device)
    for device in (p.x, p.c, opposite):
        wait(squares.at[device[1]], square_sems.at[device[1]], device)
    whole = squares[0]
    for t in range(1, parts):
        whole += squares[t]
    whole = as_column(whole[0:1, :])
    scale_two = lax.rsqrt(whole / full + EPSILON)
    scales_ref[:, 1:2] = scale_two
    normed_two_ref[...] = (residual * scale_two * gain2_ref[:, mine]).astype(BF)
    moves.wait(4, 5, 6, 7, 8, 9, 10)
    sends.finish()


def attention(
    tokens, segments, norm1_gain, wq, wk, wv, wo, query_gain, key_gain, norm2_gain, tables, cid
):
    tok, width = tokens.shape
    full, here = wq.shape
    parts = full // width
    dma = pltpu.SemaphoreType.DMA

    def shape(*dims, dtype=BF):
        return jax.ShapeDtypeStruct(dims, dtype)

    return pl.pallas_call(
        attention_kernel,
        name="attention",
        in_specs=[VMEM] * 3 + [ANY] * 4 + [VMEM] * 5,
        out_specs=[ANY] * 7 + [VMEM] * 3,
        out_shape=[
            shape(tok, full),
            shape(tok, here, dtype=F32),
            shape(tok, here, dtype=F32),
            shape(tok, here),
            shape(tok, here),
            shape(tok, here),
            shape(tok, here),
            shape(tok, width, dtype=F32),
            shape(tok, width),
            shape(tok, 2, dtype=F32),
        ],
        scratch_shapes=[
            pltpu.VMEM((parts, tok, width), BF),
            pltpu.VMEM((full, here), BF),
            pltpu.VMEM((full, here), BF),
            pltpu.VMEM((full, here), BF),
            pltpu.VMEM((here, full), BF),
            pltpu.VMEM((tok, full), BF),
            pltpu.VMEM((tok, here), F32),
            pltpu.VMEM((tok, here), F32),
            pltpu.VMEM((tok, here), BF),
            pltpu.VMEM((tok, here), BF),
            pltpu.VMEM((tok, here), BF),
            pltpu.VMEM((tok, here), BF),
            dma((11,)),
            pltpu.VMEM((3, tok, width), BF),
            pltpu.VMEM((2, tok, width), BF),
            pltpu.VMEM((tok, width), BF),
            pltpu.VMEM((parts, 8, tok), F32),
            dma((9,)),
            dma((parts,)),
            dma((2,)),
            dma,
            dma((parts,)),
        ],
        compiler_params=pltpu.CompilerParams(
            collective_id=cid, has_side_effects=True, vmem_limit_bytes=56 * 2**20
        ),
        cost_estimate=pl.CostEstimate(
            flops=2 * tok * full * here * 4, bytes_accessed=24 * 2**20, transcendentals=0
        ),
    )(
        tokens,
        segments[None, :],
        norm1_gain[None, :],
        wq,
        wk,
        wv,
        wo,
        query_gain[None, :],
        key_gain[None, :],
        norm2_gain[None, :],
        *tables,
    )


def backward_kernel(
    groups,
    ua,
    ub,
    grad_ref,
    res_ref,
    cot_ref,
    tokens_ref,
    scales_ref,
    gain1_ref,
    gain2_ref,
    seg_row_ref,
    qg_ref,
    kg_ref,
    cos_ref,
    sin_ref,
    normed_hbm,
    q_hbm,
    k_hbm,
    q_rot_hbm,
    k_rot_hbm,
    v_hbm,
    att_hbm,
    wq_hbm,
    wk_hbm,
    wv_hbm,
    wo_hbm,
    tokens_grad_ref,
    wq_grad_hbm,
    wk_grad_hbm,
    wv_grad_hbm,
    wo_grad_ref,
    norm1_ref,
    norm2_ref,
    gains_ref,
    res_grad,
    low,
    att_grad,
    dq,
    dk,
    dv,
    sent,
    from_c,
    from_x,
    means,
    send_sems,
    low_sems,
    c_sems,
    x_sem,
    mean_sems,
    normed_ref,
    q_ref,
    k_ref,
    q_rot_ref,
    k_rot_ref,
    v_ref,
    att_ref,
    wq_ref,
    wk_ref,
    wv_ref,
    wo_ref,
    wq_grad_ref,
    wk_grad_ref,
    wv_grad_ref,
    move_sems,
    *reduce_refs,
):
    tok, width = tokens_ref.shape
    parts = low.shape[0]
    full = parts * width
    p = Place(groups)
    opposite = (p.e, 2 * (1 - p.side) + 1 - p.core)
    sends = Sends(send_sems)
    partners, turns = [p.x, p.c, opposite], []
    wo_part = wo_grad_ref
    if reduce_refs:
        wo_part, bufs, sems = reduce_refs[0], reduce_refs[1:10], reduce_refs[10:]
        half = wo_part.shape[0] // 2
        halves = [pl.ds(side * half, half) for side in (p.side, 1 - p.side)]
        parts_in = [wo_part.at[rows] for rows in halves]
        parts_out = [wo_grad_ref.at[rows] for rows in halves]
        reduce = Reduce(p, parts_in, parts_out, ua, ub, bufs, sems)
        turns = reduce.turns(1)
        partners += [p.y] + [p.z(r) for r in range(1, p.rounds)]
    moves = Moves(
        [
            (att_hbm, att_ref),
            (wo_hbm, wo_ref),
            (q_rot_hbm, q_rot_ref),
            (k_rot_hbm, k_rot_ref),
            (v_hbm, v_ref),
            (q_hbm, q_ref),
            (k_hbm, k_ref),
            (wq_hbm, wq_ref),
            (wk_hbm, wk_ref),
            (wv_hbm, wv_ref),
            (normed_hbm, normed_ref),
            (wq_grad_ref, wq_grad_hbm),
            (wk_grad_ref, wk_grad_hbm),
            (wv_grad_ref, wv_grad_hbm),
        ],
        move_sems,
    )
    moves.start(*range(11))
    p.greet(partners)

    def meanwhile(count):
        for _ in range(count):
            for step in turns.pop(0) if turns else []:
                step()

    def wait(ref, sem, device):
        arrived(ref, sem, send_sems.at[0], device)

    def mean_start(n, total):
        means[n, p.t] = jnp.broadcast_to(total, (tok, 128)).T[0:8, :]
        for device in (p.x, p.c, opposite):
            sends.start(means.at[n, p.t], means.at[n, p.t], mean_sems.at[n, p.t], device)

    def mean_end(n):
        for device in (p.x, p.c, opposite):
            wait(means.at[n, device[1]], mean_sems.at[n, device[1]], device)
        whole = means[n, 0]
        for t in range(1, parts):
            whole += means[n, t]
        return as_column(whole[0:1, :]) / full

    scale_one, scale_two = scales_ref[:, 0:1], scales_ref[:, 1:2]
    grad, residual = grad_ref[...], res_ref[...]
    mine = pl.ds(pl.multiple_of(p.t * width, width), width)
    h2 = grad * gain2_ref[:, mine]
    mean_start(0, jnp.sum(h2 * residual, axis=-1, keepdims=True))
    norm2_ref[...] = jnp.sum(grad * residual * scale_two, axis=0, keepdims=True)
    upstream = cot_ref[...].astype(F32)
    res_grad[...] = upstream + scale_two * (
        h2 - residual * scale_two * scale_two * mean_end(0)
    )
    low[p.t] = res_grad[...].astype(BF)
    sends.start(low.at[p.t], low.at[p.t], low_sems.at[p.t], p.x)
    sends.start(low.at[p.t], low.at[p.t], low_sems.at[p.t], p.c)
    moves.wait(0, 1)
    attended = att_ref[...]

    def through_out(t, first=False):
        blocks = wo_part.shape[0] // parts
        product = rows_product(attended, low[t]).astype(BF)
        wo_part[pl.ds(t * blocks, blocks)] = product.reshape(blocks, 16, width)
        cols = pl.ds(pl.multiple_of(t * width, width), width)
        product = cols_product(low[t], wo_ref[:, cols])
        att_grad[...] = product if first else att_grad[...] + product

    through_out(p.t, True)
    tx, tc, to = p.x[1], p.c[1], opposite[1]
    wait(low.at[tc], low_sems.at[tc], p.c)
    through_out(tc)
    meanwhile(1)
    wait(low.at[tx], low_sems.at[tx], p.x)
    sends.start(low.at[tx], low.at[tx], low_sems.at[tx], p.c)
    through_out(tx)
    wait(low.at[to], low_sems.at[to], p.c)
    through_out(to)
    meanwhile(1)

    same = as_column(seg_row_ref[...]) == seg_row_ref[...].astype(F32)
    cosine, sine = cos_ref[...], sin_ref[...]
    factor = HEAD_DIM ** (-0.5)
    moves.wait(2, 3, 4, 5, 6)

    def to_pre(rot_grad, pre, gain):
        normed_grad = rot_grad * cosine - pltpu.roll(rot_grad, HEAD_DIM // 2, 1) * sine
        scale = lax.rsqrt(jnp.mean(pre * pre, axis=-1, keepdims=True) + EPSILON)
        gain_grad = jnp.sum(normed_grad * pre * scale, axis=0, keepdims=True)
        return rms_backward(pre, scale, normed_grad * gain).astype(BF), gain_grad

    query_gain, key_gain = jnp.zeros((1, HEAD_DIM), F32), jnp.zeros((1, HEAD_DIM), F32)
    for head in range(q_ref.shape[1] // HEAD_DIM):
        cols = slice(head * HEAD_DIM, (head + 1) * HEAD_DIM)
        q_rot, k_rot, value = q_rot_ref[:, cols], k_rot_ref[:, cols], v_ref[:, cols]
        scores = jnp.where(same, cols_product(q_rot, k_rot) * factor, -1e30)
        weights = jnp.exp(scores - jnp.max(scores, axis=-1, keepdims=True))
        probs = weights / jnp.sum(weights, axis=-1, keepdims=True)
        out_grad = att_grad[:, cols].astype(BF)
        dv[:, cols] = rows_product(probs.astype(BF), out_grad).astype(BF)
        prob_grad = cols_product(out_grad, value)
        score_grad = (
            probs * (prob_grad - jnp.sum(probs * prob_grad, axis=-1, keepdims=True))
        ).astype(BF)
        dq[:, cols], gain_grad = to_pre(dot(score_grad, k_rot) * factor, q_ref[:, cols], qg_ref[...])
        query_gain += gain_grad
        dk[:, cols], gain_grad = to_pre(
            rows_product(score_grad, q_rot) * factor, k_ref[:, cols], kg_ref[...]
        )
        key_gain += gain_grad
        meanwhile(1)
    gains_ref[:, :HEAD_DIM] = query_gain
    gains_ref[:, HEAD_DIM:] = key_gain
    moves.wait(7, 8, 9, 10)

    def normed_part(side, core):
        rows = pl.ds(pl.multiple_of((2 * side + core) * width, width), width)
        return (
            cols_product(dq[...], wq_ref[rows, :])
            + cols_product(dk[...], wk_ref[rows, :])
            + cols_product(dv[...], wv_ref[rows, :])
        )

    for i, side in enumerate((1 - p.side, p.side)):
        sent[i] = normed_part(side, 1 - p.core).astype(BF)
        sends.start(sent.at[i], from_c.at[side], c_sems.at[side], p.c)
    part = normed_part(1 - p.side, p.core)
    wait(from_c.at[1 - p.side], c_sems.at[1 - p.side], p.c)
    sent[2] = (part + from_c[1 - p.side].astype(F32)).astype(BF)
    sends.start(sent.at[2], from_x, x_sem, p.x)
    part = normed_part(p.side, p.core)
    meanwhile(1)
    for t in range(parts):
        rows = slice(t * width, (t + 1) * width)
        wq_grad_ref[rows, :] = rows_product(normed_ref[:, rows], dq[...]).astype(BF)
    moves.start(11)
    meanwhile(1)
    wait(from_c.at[p.side], c_sems.at[p.side], p.c)
    part += from_c[p.side].astype(F32)
    wait(from_x, x_sem, p.x)
    part += from_x[...].astype(F32)
    own = tokens_ref[...].astype(F32)
    h1 = part * gain1_ref[:, mine]
    mean_start(1, jnp.sum(h1 * own, axis=-1, keepdims=True))
    norm1_ref[...] = jnp.sum(part * own * scale_one, axis=0, keepdims=True)
    meanwhile(1)
    for t in range(parts):
        rows = slice(t * width, (t + 1) * width)
        wk_grad_ref[rows, :] = rows_product(normed_ref[:, rows], dk[...]).astype(BF)
    moves.start(12)
    meanwhile(1)
    for t in range(parts):
        rows = slice(t * width, (t + 1) * width)
        wv_grad_ref[rows, :] = rows_product(normed_ref[:, rows], dv[...]).astype(BF)
    moves.start(13)
    tokens_grad_ref[...] = res_grad[...] + scale_one * (
        h1 - own * scale_one * scale_one * mean_end(1)
    )
    meanwhile(len(turns))
    moves.wait(11, 12, 13)
    if reduce_refs:
        reduce.finish()
    sends.finish()


def backward(groups, direct, cid, *arrays):
    tok, width = arrays[3].shape
    full, here = arrays[19].shape
    parts = full // width
    dma = pltpu.SemaphoreType.DMA

    def shape(*dims, dtype=BF):
        return jax.ShapeDtypeStruct(dims, dtype)

    outs = [
        shape(tok, width, dtype=F32),
        shape(full, here),
        shape(full, here),
        shape(full, here),
        shape(full // 16, 16, here),
        shape(1, width, dtype=F32),
        shape(1, width, dtype=F32),
        shape(1, 2 * HEAD_DIM, dtype=F32),
    ]
    scratch = [
        pltpu.VMEM((tok, width), F32),
        pltpu.VMEM((parts, tok, width), BF),
        pltpu.VMEM((tok, here), F32),
        pltpu.VMEM((tok, here), BF),
        pltpu.VMEM((tok, here), BF),
        pltpu.VMEM((tok, here), BF),
        pltpu.VMEM((3, tok, width), BF),
        pltpu.VMEM((2, tok, width), BF),
        pltpu.VMEM((tok, width), BF),
        pltpu.VMEM((2, parts, 8, tok), F32),
        dma((12,)),
        dma((parts,)),
        dma((2,)),
        dma,
        dma((2, parts)),
    ]
    scratch += [pltpu.VMEM(a.shape, a.dtype) for a in arrays[12:]]
    scratch += [pltpu.VMEM((full, here), BF)] * 3 + [dma((14,))]
    out_specs = [VMEM] + [ANY] * 3 + [VMEM] * 4
    ua, ub = pieces(full // 32, groups)
    if direct:
        out_specs[4] = ANY
        bufs, sems = Reduce.scratch(2, groups // 2, ua, ub, width)
        scratch += [pltpu.VMEM(outs[4].shape, BF)] + bufs + sems
    return pl.pallas_call(
        functools.partial(backward_kernel, groups, ua, ub),
        name="backward",
        in_specs=[VMEM] * 12 + [ANY] * 11,
        out_specs=out_specs,
        out_shape=outs,
        scratch_shapes=scratch,
        compiler_params=pltpu.CompilerParams(
            collective_id=cid, has_side_effects=True, vmem_limit_bytes=62 * 2**20
        ),
        cost_estimate=pl.CostEstimate(
            flops=2 * tok * full * here * 8, bytes_accessed=36 * 2**20, transcendentals=0
        ),
    )(*arrays)


def chosen_here(chosen, rank, local, j):
    columns = lax.broadcasted_iota(jnp.int32, chosen.shape, 1)
    return jnp.where(columns == rank * local + j, chosen, 0.0)


def sigmoid(values):
    return 1.0 / (1.0 + jnp.exp(-values))


def softmax(values):
    weights = jnp.exp(values - jnp.max(values, axis=-1, keepdims=True))
    return weights / jnp.sum(weights, axis=-1, keepdims=True)


def expert_backward(gate, here, g, u, v):
    s = sigmoid(g)
    gs = g * s
    hidden = (gs * u).astype(BF).astype(F32)
    gate_grad = here * jnp.sum(hidden * v, axis=-1, keepdims=True)
    hidden_grad = gate * v
    uga = (hidden_grad * gs).astype(BF)
    gga = (hidden_grad * u * s * (1.0 + g * (1.0 - s))).astype(BF)
    return gga, uga, gate_grad


def router_backward(probs, prob_grad):
    logit_grad = probs * (prob_grad - jnp.sum(probs * prob_grad, axis=-1, keepdims=True))
    high = logit_grad.astype(BF)
    return high, (logit_grad - high.astype(F32)).astype(BF)


def plain_experts(rank, x_all, up_all, mask_all, router_t, w_gate, w_up, w_down):
    local = w_gate.shape[0]

    def joined(quarters):
        return quarters.transpose(1, 0, 2).reshape(quarters.shape[1], -1)

    def quarters(values, parts):
        return values.reshape(values.shape[0], parts, -1).transpose(1, 0, 2).astype(BF)

    def block(sums, pieces):
        x_parts, up_parts, mask = pieces
        x, up, chosen = joined(x_parts), joined(up_parts), mask.astype(F32).T
        probs = softmax(cols_product(x, router_t))
        out = grad = 0.0
        prob_grad = jnp.zeros_like(probs)
        grads = [[], [], []]
        for j in range(local):
            here = chosen_here(chosen, rank, local, j)
            gate = jnp.sum(here * probs, axis=-1, keepdims=True)
            g, u, v = dot(x, w_gate[j]), dot(x, w_up[j]), cols_product(up, w_down[j])
            hidden = (gate * (g * sigmoid(g) * u).astype(BF).astype(F32)).astype(BF)
            gga, uga, gate_grad = expert_backward(gate, here, g, u, v)
            prob_grad += gate_grad
            out += dot(hidden, w_down[j])
            grad += cols_product(gga, w_gate[j]) + cols_product(uga, w_up[j])
            for n, (left, right) in enumerate(((x, gga), (x, uga), (hidden, up))):
                grads[n].append(rows_product(left, right))
        high, low = router_backward(probs, prob_grad)
        grad += dot(high, router_t) + dot(low, router_t)
        grads = [jnp.stack(g) for g in grads] + [rows_product(high, x) + rows_product(low, x)]
        parts = x_parts.shape[0]
        sums = [total + more for total, more in zip(sums, grads)]
        return sums, (quarters(out, parts), quarters(grad, parts))

    zeros = [jnp.zeros(w.shape, F32) for w in (w_gate, w_up, w_down, router_t)]
    sums, (out_part, grad_part) = lax.scan(block, zeros, (x_all, up_all, mask_all))
    return out_part, grad_part, sums[:3], sums[3]


def expert_scatter_kernel(
    x_ref,
    up_ref,
    mask_ref,
    router_t_ref,
    wg_ref,
    wu_ref,
    wd_ref,
    grad_ref,
    out_ref,
    hid_ref,
    gga_ref,
    uga_ref,
    lg_ref,
    *refs,
):
    bufs, sems = refs[:6], refs[6:13]
    x_buf, up_buf, out_buf, out_other, from_c, other, mine, hid, acts = refs[13:22]
    joined, products, probs_ref, load_sems, store_sems, weight_sems = refs[22:28]
    out_send_sems, out_sems = refs[28:]
    groups, parts, tok, width = x_ref.shape
    experts = router_t_ref.shape[0]
    local, full, ffe = wg_ref.shape
    hidden_units = local * ffe
    last = 2 * hidden_units
    p = Place(groups)
    rounds = p.rounds
    scatter = Scatter(p, bufs, sems)

    def round_of(k):
        return lax.rem(k + 1, rounds)

    def loads(k, i):
        e = scatter.block(round_of(k), i)
        return [
            pltpu.make_async_copy(
                ref.at[e, t], buf.at[i, :, pl.ds(t * width, width)], load_sems.at[n, i, t]
            )
            for t in range(parts)
            for n, (ref, buf) in enumerate(((x_ref, x_buf), (up_ref, up_buf)))
        ]

    def columns(n, j):
        return pl.ds(n * hidden_units + j * ffe, ffe)

    def weight_loads():
        return [
            pltpu.make_async_copy(ref.at[j], joined.at[:, columns(n, j)], weight_sems.at[n, j])
            for j in range(local)
            for n, ref in enumerate((wg_ref, wu_ref))
        ]

    def stores(k, i):
        e = scatter.block(round_of(k), i)
        copies = []
        for j in range(local):
            pairs = (
                (hid.at[i, :, columns(0, j)], hid_ref.at[e, j]),
                (acts.at[i, :, columns(0, j)], gga_ref.at[e, j]),
                (acts.at[i, :, columns(1, j)], uga_ref.at[e, j]),
            )
            for n, (src, dst) in enumerate(pairs):
                copies.append(pltpu.make_async_copy(src, dst, store_sems.at[n, j, i]))
        for j, side in enumerate(scatter.sides):
            src, dst = out_buf.at[i, j], out_ref.at[e, side]
            copies.append(pltpu.make_async_copy(src, dst, store_sems.at[3, j, i]))
        return copies

    def out_send(i, j):
        return remote(
            out_other.at[i, j], from_c.at[i, j], out_send_sems.at[i, j], out_sems.at[i, j], p.c
        )

    def ended(k, i):
        for copy in stores(k, i):
            copy.wait()
        for j in range(2):
            scatter.core_sent(round_of(k), i, j, other.at[i, j])
            out_send(i, j).wait_send()

    def exchanged(k, i):
        for j in range(2):
            scatter.core_add(round_of(k), i, j, mine[i, j])
            scatter.first(round_of(k), i, j)

    def compute(k, i):
        r = round_of(k)
        e = scatter.block(r, i)
        for copy in loads(k, i):
            copy.wait()

        @pl.when(k > 0)
        def _():
            ended(k - 1, i)

        chosen = mask_ref[e].astype(F32).T
        products[...] = dot(x_buf[i], joined[...])
        probs_ref[...] = softmax(products[:, last : last + experts])
        for j in range(local):
            gate = jnp.sum(
                chosen_here(chosen, p.e, local, j) * probs_ref[...], axis=-1, keepdims=True
            )
            g, u = products[:, columns(0, j)], products[:, columns(1, j)]
            hidden = (g * sigmoid(g) * u).astype(BF).astype(F32)
            hid[i, :, columns(0, j)] = (gate * hidden).astype(BF)
        if i == 0:
            pl.when(k > 0)(lambda: exchanged(k - 1, 1))
        else:
            exchanged(k, 0)

        def outputs(t):
            return dot(hid[i], wd_ref[:, pl.ds(pl.multiple_of(t * width, width), width)])

        for j, side in enumerate(scatter.sides):
            out_other[i, j] = outputs(2 * side + 1 - p.core).astype(BF)
            out_send(i, j).start()
        probs = probs_ref[...]
        prob_grad = jnp.zeros_like(probs)
        for j in range(local):
            here = chosen_here(chosen, p.e, local, j)
            gate = jnp.sum(here * probs, axis=-1, keepdims=True)
            v = cols_product(up_buf[i], wd_ref[pl.ds(j * ffe, ffe), :])
            g, u = products[:, columns(0, j)], products[:, columns(1, j)]
            gga, uga, gate_grad = expert_backward(gate, here, g, u, v)
            acts[i, :, columns(0, j)] = gga
            acts[i, :, columns(1, j)] = uga
            prob_grad += gate_grad
        high, low = router_backward(probs, prob_grad)
        both = jnp.concatenate([high, low], axis=-1)
        lg_ref[e] = both
        acts[i, :, last : last + 2 * experts] = both

        def gradients(t):
            rows = pl.ds(pl.multiple_of(t * width, width), width)
            return cols_product(acts[i], joined[rows, :]).astype(BF)

        for j, side in enumerate(scatter.sides):
            other[i, j] = gradients(2 * side + 1 - p.core)
            scatter.core(r, i, j, other.at[i, j])
        for j, side in enumerate(scatter.sides):
            total = outputs(2 * side + p.core)
            out_send(i, j).wait_recv()
            out_buf[i, j] = (total + from_c[i, j].astype(F32)).astype(BF)
        for j, side in enumerate(scatter.sides):
            mine[i, j] = gradients(2 * side + p.core)
        for copy in stores(k, i):
            copy.start()

        @pl.when(k + 1 < rounds)
        def _():
            for copy in loads(k + 1, i):
                copy.start()

    for copy in weight_loads():
        copy.start()
    for i in range(2):
        for copy in loads(0, i):
            copy.start()
        acts[i, :, last:] = jnp.zeros((tok, acts.shape[2] - last), BF)
    spare = jnp.zeros((acts.shape[2] - last - 2 * experts, full), F32)
    router = router_t_ref[...].astype(F32)
    joined[:, last:] = jnp.concatenate([router, router, spare], axis=0).T.astype(BF)
    p.greet([p.y, p.x, p.c] + [p.z(r) for r in range(1, rounds)])
    for copy in weight_loads():
        copy.wait()

    def body(k, carry):
        r1, r2 = round_of(k + rounds - 1), round_of(k + rounds - 2)

        @pl.when(k < rounds)
        def _():
            compute(k, 0)

        pl.when(k == rounds)(lambda: exchanged(rounds - 1, 1))

        @pl.when(k >= 2)
        def _():
            for h in range(2):
                scatter.third(r2, h)

        @pl.when(k < rounds)
        def _():
            compute(k, 1)

        @pl.when(jnp.logical_and(k >= 1, k <= rounds))
        def _():
            for i in range(2):
                scatter.second0(r1, i)
                scatter.second1(r1, i)

        return carry

    lax.fori_loop(0, rounds + 2, body, 0)
    scatter.finish(grad_ref)
    for i in range(2):
        ended(rounds - 1, i)


def expert_scatter(x_all, up_all, mask_all, router_t, w_gate, w_up, w_down, cid):
    groups, parts, tok, width = x_all.shape
    local, full, ffe = w_gate.shape
    experts = router_t.shape[0]
    dma = pltpu.SemaphoreType.DMA
    bufs, sems = Scatter.scratch(groups, tok, width, tok // 2)
    act = jax.ShapeDtypeStruct((groups, local, tok, ffe), BF)
    block = pltpu.VMEM((2, tok, full), BF)
    shards = pltpu.VMEM((2, 2, tok, width), BF)
    wide = 2 * local * ffe + 128
    return pl.pallas_call(
        expert_scatter_kernel,
        name="experts_scatter",
        in_specs=[ANY, ANY, VMEM, VMEM, ANY, ANY, VMEM],
        out_specs=[VMEM] + [ANY] * 4 + [VMEM],
        out_shape=[
            jax.ShapeDtypeStruct((tok, width), F32),
            jax.ShapeDtypeStruct((groups, 2, tok, width), BF),
            act,
            act,
            act,
            jax.ShapeDtypeStruct((groups, tok, 2 * experts), BF),
        ],
        scratch_shapes=bufs
        + sems
        + [block, block, shards, shards, shards, shards, shards]
        + [
            pltpu.VMEM((2, tok, local * ffe), BF),
            pltpu.VMEM((2, tok, wide), BF),
            pltpu.VMEM((full, wide), BF),
            pltpu.VMEM((tok, wide), F32),
            pltpu.VMEM((tok, experts), F32),
        ]
        + [dma((2, 2, parts)), dma((4, 2, 2)), dma((2, local)), dma((2, 2)), dma((2, 2))],
        compiler_params=pltpu.CompilerParams(
            collective_id=cid, has_side_effects=True, vmem_limit_bytes=62 * 2**20
        ),
        cost_estimate=pl.CostEstimate(
            flops=12 * groups * tok * full * ffe * local,
            bytes_accessed=groups * tok * full * 8,
            transcendentals=0,
        ),
    )(x_all, up_all, mask_all, router_t, w_gate, w_up, w_down.reshape(local * ffe, full))


def per_device(
    tokens,
    segments,
    routes,
    norm1_gain,
    w_query,
    w_key,
    w_value,
    w_out,
    query_gain,
    key_gain,
    norm2_gain,
    router,
    w_gate,
    w_up,
    w_down,
    cotangent,
):
    tok, quarter = tokens.shape
    experts = router.shape[1]
    tensors = lax.axis_size("tensor")
    groups = lax.axis_size("expert")
    tensor_rank = lax.axis_index("tensor")
    full = quarter * tensors
    direct = tensors == 4 and groups == 8 and 16 <= experts <= 32

    up_all = lax.all_gather(cotangent, BOTH, axis=0).reshape(groups, tensors, tok, quarter)
    expert_ids = jnp.arange(experts, dtype=jnp.int32)
    chosen = jnp.any(routes.T[None, :, :] == expert_ids[:, None, None], axis=1).astype(BF)

    cosine_row, sine_row = rope_tables(tok, HEAD_DIM)
    tables = (
        jnp.concatenate([cosine_row, cosine_row], axis=-1),
        jnp.concatenate([-sine_row, sine_row], axis=-1),
    )
    (
        normed,
        query_pre,
        key_pre,
        query_rot,
        key_rot,
        value_low,
        attended,
        residual,
        normed_two,
        scales,
    ) = attention(
        tokens,
        segments,
        norm1_gain,
        w_query,
        w_key,
        w_value,
        w_out,
        query_gain,
        key_gain,
        norm2_gain,
        tables,
        4,
    )
    if direct:
        x_all, mask_all = gather_all(normed_two, chosen, groups, tensors, 1)
    else:
        mask_all = lax.all_gather(chosen, "expert", axis=0)
        x_all = lax.all_gather(normed_two, BOTH, axis=0).reshape(groups, tensors, tok, quarter)

    def to_home(values):
        return lax.psum_scatter(
            values.reshape(groups * tensors, tok, quarter), BOTH, scatter_dimension=0
        ).astype(F32)

    expert_args = (x_all, up_all, mask_all, router.T, w_gate, w_up, w_down)
    if direct:
        normed_two_grad, out_part, hid, gga, uga, lg = expert_scatter(
            *expert_args, cid=2
        )
    else:
        out_part, grad_part, expert_grads, router_part = plain_experts(
            lax.axis_index("expert"), *expert_args
        )
        normed_two_grad = to_home(grad_part)

    (
        tokens_grad,
        query_w_grad,
        key_w_grad,
        value_w_grad,
        out_w_grad,
        norm1_grad,
        norm2_grad,
        gains,
    ) = backward(
        groups,
        direct,
        5,
        normed_two_grad,
        residual,
        cotangent,
        tokens,
        scales,
        norm1_gain[None, :],
        norm2_gain[None, :],
        segments[None, :],
        query_gain[None, :],
        key_gain[None, :],
        *tables,
        normed,
        query_pre,
        key_pre,
        query_rot,
        key_rot,
        value_low,
        attended,
        w_query,
        w_key,
        w_value,
        w_out,
    )

    def spread(part):
        mine = jnp.arange(tensors)[:, None] == tensor_rank
        return jnp.where(mine, part, 0.0)

    rest = jnp.concatenate(
        [
            spread(norm1_grad),
            spread(norm2_grad),
            jnp.pad(gains, ((0, 0), (0, quarter - gains.shape[1]))),
        ]
    )
    rest = jnp.pad(rest, ((0, -rest.shape[0] % 8), (0, 0)))
    weight_grads = [query_w_grad, key_w_grad, value_w_grad]
    out_w_grad = out_w_grad.reshape(full, quarter)
    if direct:
        rest = jnp.pad(rest, ((0, experts - rest.shape[0]), (0, 0)))
        weight_grads, small, moe_out, expert_grads = reduce_shared(
            weight_grads, rest, lg, out_part, (x_all, up_all, hid, gga, uga), 3
        )
        router_sum, rest = small[:tensors], small[tensors]
    else:
        moe_out = to_home(out_part)
        *weight_grads, out_w_grad = [
            lax.psum(part, "expert") for part in weight_grads + [out_w_grad]
        ]
        router_sum, rest = lax.psum(
            (router_part.reshape(experts, tensors, quarter).transpose(1, 0, 2), rest), BOTH
        )
    mixed = (residual + moe_out).astype(BF)
    weight_grads = [part.astype(F32) for part in weight_grads]
    router_sum = router_sum.transpose(0, 2, 1).reshape(full, experts)
    norm1_sum = rest[:tensors].reshape(full)
    norm2_sum = rest[tensors : 2 * tensors].reshape(full)
    query_gain_sum = rest[2 * tensors, :HEAD_DIM]
    key_gain_sum = rest[2 * tensors, HEAD_DIM : 2 * HEAD_DIM]
    out_w_sum = out_w_grad.astype(F32).reshape(tensors, quarter, quarter).transpose(1, 0, 2)
    return (
        mixed,
        tokens_grad,
        norm1_sum,
        weight_grads[0],
        weight_grads[1],
        weight_grads[2],
        out_w_sum.reshape(quarter, full),
        query_gain_sum,
        key_gain_sum,
        norm2_sum,
        router_sum,
        *expert_grads,
    )


def solution(mesh):
    return jax.shard_map(
        per_device,
        mesh=mesh,
        in_specs=(
            P("expert", "tensor"),
            P("expert"),
            P("expert", None),
            P(),
            P(None, "tensor"),
            P(None, "tensor"),
            P(None, "tensor"),
            P("tensor", None),
            P(),
            P(),
            P(),
            P(),
            P("expert", None, "tensor"),
            P("expert", None, "tensor"),
            P("expert", "tensor", None),
            P("expert", "tensor"),
        ),
        out_specs=(
            P("expert", "tensor"),
            P("expert", "tensor"),
            P(),
            P(None, "tensor"),
            P(None, "tensor"),
            P(None, "tensor"),
            P("tensor", None),
            P(),
            P(),
            P(),
            P(),
            P("expert", None, "tensor"),
            P("expert", None, "tensor"),
            P("expert", "tensor", None),
        ),
        check_vma=False,
    )
```

```python
import functools

import jax
import jax.numpy as jnp
from jax import lax
from jax.experimental import pallas as pl
from jax.experimental.pallas import tpu as pltpu
from jax.sharding import PartitionSpec as P

HEAD_DIM = 128
EPSILON = 1e-06
ROPE_BASE = 50000.0
BF = jnp.bfloat16
F32 = jnp.float32
BOTH = ("expert", "tensor")


def rms_backward(values, scale_row, grad_out):
    return scale_row * (
        grad_out
        - values * scale_row * scale_row * jnp.mean(grad_out * values, axis=-1, keepdims=True)
    )


def rope_tables(length, head_dim):
    half_dim = head_dim // 2
    frequency = ROPE_BASE ** (-jnp.arange(half_dim, dtype=F32) * 2.0 / head_dim)
    angles = jnp.arange(length, dtype=F32)[:, None] * frequency[None, :]
    return jnp.cos(angles), jnp.sin(angles)


def rows_product(left, right):
    return lax.dot_general(left, right, (((0,), (0,)), ((), ())), preferred_element_type=F32)


def cols_product(left, right):
    return lax.dot_general(left, right, (((1,), (1,)), ((), ())), preferred_element_type=F32)


def as_column(row):
    return jnp.broadcast_to(row.astype(F32), (128, row.shape[1])).T[:, 0:1]


def dot(left, right):
    return jnp.dot(left, right, preferred_element_type=F32)


ANY = pl.BlockSpec(memory_space=pl.ANY)
VMEM = pl.BlockSpec(memory_space=pltpu.VMEM)


class Place:
    def __init__(self, groups):
        self.e, self.t = lax.axis_index("expert"), lax.axis_index("tensor")
        self.rounds = groups // 2
        self.high, self.low = self.e // 2, self.e % 2
        self.side, self.core = self.t // 2, self.t % 2
        self.y = (2 * self.high + 1 - self.low, self.t)
        self.x = (self.e, 2 * (1 - self.side) + self.core)
        self.c = (self.e, 2 * self.side + 1 - self.core)

    def far(self, r):
        return lax.rem(self.high + self.rounds - r, self.rounds)

    def z(self, r):
        return (2 * self.far(r) + self.low, self.t)

    def greet(self, partners):
        barrier = pltpu.get_barrier_semaphore()
        for partner in partners:
            pl.semaphore_signal(
                barrier, inc=1, device_id=partner, device_id_type=pl.DeviceIdType.MESH
            )
        pl.semaphore_wait(barrier, len(partners))


class Sends:
    def __init__(self, sems):
        self.sems, self.copies = sems, []

    def start(self, src, dst, recv_sem, device, when=None):
        copy = remote(src, dst, self.sems.at[len(self.copies)], recv_sem, device)
        if when is None:
            copy.start()
        else:
            pl.when(when)(copy.start)
        self.copies.append((copy, when))

    def finish(self):
        for copy, when in self.copies:
            if when is None:
                copy.wait_send()
            else:
                pl.when(when)(copy.wait_send)


def remote(src, dst, send_sem, recv_sem, device):
    return pltpu.make_async_remote_copy(
        src_ref=src,
        dst_ref=dst,
        send_sem=send_sem,
        recv_sem=recv_sem,
        device_id=device,
        device_id_type=pl.DeviceIdType.MESH,
    )


def arrived(ref, recv_sem, send_sem, device):
    remote(ref, ref, send_sem, recv_sem, device).wait_recv()


def departed(ref, recv_sem, send_sem, device):
    remote(ref, ref, send_sem, recv_sem, device).wait_send()


class Moves:
    def __init__(self, pairs, sems):
        self.pairs, self.sems = pairs, sems

    def copy(self, n):
        return pltpu.make_async_copy(*self.pairs[n], self.sems.at[n])

    def start(self, *which):
        for n in which:
            self.copy(n).start()

    def wait(self, *which):
        for n in which:
            self.copy(n).wait()


def gather_kernel(
    x_ref,
    mask_ref,
    router_t_ref,
    out_ref,
    masks_ref,
    router_ref,
    send_sems,
    recv_sems,
    mask_sems,
    own_sem,
):
    groups, tok = out_ref.shape[0], out_ref.shape[2]
    half = tok // 2
    p = Place(groups)
    rounds = p.rounds
    p.greet([p.y, p.x, p.c] + [p.z(r) for r in range(1, rounds)])
    sends = Sends(send_sems)
    low2, side2 = 1 - p.low, 1 - p.side

    def shard(h, e, t):
        return out_ref.at[e, t, pl.ds(h * half, half)]

    def send(h, e, t, device, src=None):
        dst = shard(h, e, t)
        sends.start(dst if src is None else src, dst, recv_sems.at[h, e, t], device)

    def wait(h, e, t, device):
        arrived(shard(h, e, t), recv_sems.at[h, e, t], send_sems.at[0], device)

    own = pltpu.make_async_copy(x_ref, out_ref.at[p.e, p.t], own_sem)
    own.start()

    def send_mask(e, device):
        sends.start(masks_ref.at[e], masks_ref.at[e], mask_sems.at[e], device)

    masks_ref[p.e] = mask_ref[...]

    def first(r):
        e = 2 * p.far(r) + p.low
        if r > 0:
            arrived(masks_ref.at[e], mask_sems.at[e], send_sems.at[0], p.z(r))
        send_mask(e, p.y)
        for h in range(2):
            src = x_ref.at[pl.ds(h * half, half)] if r == 0 else None
            if r > 0:
                wait(h, e, p.t, p.z(r))
            send(h, e, p.t, p.x if h else p.y, src)
            send(h, e, p.t, p.y if h else p.x, src)
            send(h, e, p.t, p.c, src)

    def second(r):
        e, e2 = 2 * p.far(r) + p.low, 2 * p.far(r) + low2
        wait(0, e2, p.t, p.y)
        send(0, e2, p.t, p.x)
        send(0, e2, p.t, p.c)
        t2 = 2 * side2 + p.core
        wait(1, e, t2, p.x)
        send(1, e, t2, p.y)
        send(1, e, t2, p.c)

    def third(r):
        e, e2 = 2 * p.far(r) + p.low, 2 * p.far(r) + low2
        t2 = 2 * side2 + p.core
        wait(0, e, t2, p.x)
        send(0, e, t2, p.c)
        wait(1, e2, p.t, p.y)
        send(1, e2, p.t, p.c)
        wait(0, e2, t2, p.x)
        send(0, e2, t2, p.c)
        wait(1, e2, t2, p.y)
        send(1, e2, t2, p.c)

    for r in range(1, rounds):
        to = (2 * lax.rem(p.high + r, rounds) + p.low, p.t)
        send_mask(p.e, to)
        for h in range(2):
            send(h, p.e, p.t, to, x_ref.at[pl.ds(h * half, half)])
    for r in range(rounds + 2):
        if r == 2:
            router = router_t_ref[...].astype(F32)
            spare = router_ref.shape[1] - 2 * router.shape[0]
            spare = jnp.zeros((spare, router.shape[1]), F32)
            router_ref[...] = jnp.concatenate([router, router, spare], axis=0).T.astype(BF)
        if r < rounds:
            first(r)
        if 0 <= r - 1 < rounds:
            second(r - 1)
        if 0 <= r - 2 < rounds:
            third(r - 2)
    other = 1 - p.core
    for r in range(rounds):
        e2 = 2 * p.far(r) + low2
        arrived(masks_ref.at[e2], mask_sems.at[e2], send_sems.at[0], p.y)
        for e in (2 * p.far(r) + p.low, 2 * p.far(r) + low2):
            for t in (2 * p.side + other, 2 * side2 + other):
                for h in range(2):
                    wait(h, e, t, p.c)
    own.wait()
    sends.finish()


def gather_all(x, mask, router_t, groups, tensors, collective_id):
    tok, width = x.shape
    rounds = groups // 2
    count = 3 * (rounds - 1) + 7 * rounds + 4 * rounds + 4 * rounds
    return pl.pallas_call(
        gather_kernel,
        name="gather_all",
        in_specs=[ANY, VMEM, VMEM],
        out_specs=[ANY, VMEM, VMEM],
        out_shape=[
            jax.ShapeDtypeStruct((groups, tensors, tok, width), x.dtype),
            jax.ShapeDtypeStruct((groups,) + mask.shape, mask.dtype),
            jax.ShapeDtypeStruct((router_t.shape[1], 128), router_t.dtype),
        ],
        scratch_shapes=[
            pltpu.SemaphoreType.DMA((count,)),
            pltpu.SemaphoreType.DMA((2, groups, tensors)),
            pltpu.SemaphoreType.DMA((groups,)),
            pltpu.SemaphoreType.DMA,
        ],
        compiler_params=pltpu.CompilerParams(
            collective_id=collective_id, has_side_effects=True, vmem_limit_bytes=62 * 2**20
        ),
        cost_estimate=pl.CostEstimate(
            flops=0, bytes_accessed=groups * tensors * tok * width * 2, transcendentals=0
        ),
    )(x, mask, router_t)


class Scatter:
    def __init__(self, p, bufs, sems):
        self.p = p
        self.total, self.from_x0, self.from_y0, self.from_x1, self.from_y1, self.from_z = bufs
        self.send_sems, self.core_sems, self.x0_sems, self.y0_sems = sems[:4]
        self.x1_sems, self.y1_sems, self.z_sems = sems[4:]
        self.tok, cut = self.total.shape[2], self.from_x0.shape[1]
        self.halves = (pl.ds(0, cut), pl.ds(cut, self.tok - cut))
        self.lows = (1 - p.low, p.low)
        self.sides = (1 - p.side, p.side)

    @staticmethod
    def scratch(groups, tok, width, cut):
        rounds, rest = groups // 2, tok - cut
        dma = pltpu.SemaphoreType.DMA
        bufs = [
            pltpu.VMEM((groups, 2, tok, width), BF),
            pltpu.VMEM((groups, cut, width), BF),
            pltpu.VMEM((rounds, cut, width), BF),
            pltpu.VMEM((rounds, rest, width), BF),
            pltpu.VMEM((rounds, 2, rest, width), BF),
            pltpu.VMEM((rounds, tok, width), BF),
        ]
        sems = [
            dma((12, rounds)),
            dma((groups, 2)),
            dma((groups,)),
            dma((rounds,)),
            dma((rounds,)),
            dma((rounds, 2)),
            dma((rounds, 2)),
        ]
        return bufs, sems

    def order(self, k):
        return (k + 1) % self.p.rounds

    def block(self, r, i):
        return 2 * self.p.far(r) + self.lows[i]

    def wait(self, ref, sem, device):
        arrived(ref, sem, self.send_sems.at[0, 0], device)

    def send(self, n, r, src, dst, sem, device):
        remote(src, dst, self.send_sems.at[n, r], sem, device).start()

    def add(self, target, received):
        self.total[target] = self.total[target] + received

    def core(self, r, i, j, src):
        e, side = self.block(r, i), self.sides[j]
        dst, sem = self.total.at[e, side], self.core_sems.at[e, side]
        self.send(2 * i + j, r, src, dst, sem, self.p.c)

    def core_sent(self, r, i, j, src):
        departed(src, self.core_sems.at[0, 0], self.send_sems.at[2 * i + j, r], self.p.c)

    def core_add(self, r, i, j, mine):
        e, side = self.block(r, i), self.sides[j]
        self.wait(self.total.at[e, side], self.core_sems.at[e, side], self.p.c)
        self.total[e, side] = self.total[e, side] + mine

    def first(self, r, i, j):
        p, (h0, h1) = self.p, self.halves
        e, far, side = self.block(r, i), p.far(r), self.sides[j]
        if j == 0:
            src = self.total.at[e, side, h0]
            self.send(4 + i, r, src, self.from_x0.at[e], self.x0_sems.at[e], p.x)
        if i == 0:
            src, dst = self.total.at[e, side, h1], self.from_y1.at[far, side]
            self.send(6 + j, r, src, dst, self.y1_sems.at[far, side], p.y)

    def second0(self, r, i):
        p, far, e = self.p, self.p.far(r), self.block(r, i)
        rows = self.halves[0]
        self.wait(self.from_x0.at[e], self.x0_sems.at[e], p.x)
        self.add((e, p.side, rows), self.from_x0[e])
        if i == 0:
            src = self.total.at[e, p.side, rows]
            self.send(8, r, src, self.from_y0.at[far], self.y0_sems.at[far], p.y)

    def second1(self, r, j):
        p, far, side = self.p, self.p.far(r), self.sides[j]
        e, rows = 2 * far + p.low, self.halves[1]
        self.wait(self.from_y1.at[far, side], self.y1_sems.at[far, side], p.y)
        self.add((e, side, rows), self.from_y1[far, side])
        if j == 0:
            src = self.total.at[e, side, rows]
            self.send(9, r, src, self.from_x1.at[far], self.x1_sems.at[far], p.x)

    def third(self, r, h):
        p, far = self.p, self.p.far(r)
        e, rows = 2 * far + p.low, self.halves[h]
        if h == 0:
            received, sem, device = self.from_y0, self.y0_sems, p.y
        else:
            received, sem, device = self.from_x1, self.x1_sems, p.x
        self.wait(received.at[far], sem.at[far], device)
        self.add((e, p.side, rows), received[far])

        @pl.when(r > 0)
        def _():
            src, dst = self.total.at[e, p.side, rows], self.from_z.at[r, rows]
            self.send(10 + h, r, src, dst, self.z_sems.at[r, h], p.z(r))

    def finish(self, out_ref):
        p = self.p
        for h, rows in enumerate(self.halves):
            total = self.total[p.e, p.side, rows].astype(F32)
            for r in range(1, p.rounds):
                source = (2 * lax.rem(p.high + r, p.rounds) + p.low, p.t)
                self.wait(self.from_z.at[r, rows], self.z_sems.at[r, h], source)
                total += self.from_z[r, rows].astype(F32)
            out_ref[rows, :] = total
        h0, h1 = self.halves
        for r in range(p.rounds):
            ends = [(4, h0, p.x), (5, h0, p.x), (6, h1, p.y), (7, h1, p.y), (8, h0, p.y)]
            ends += [(9, h1, p.x)]
            if r > 0:
                ends += [(10, h0, p.z(r)), (11, h1, p.z(r))]
            for n, rows, device in ends:
                departed(
                    self.total.at[0, 0, rows],
                    self.core_sems.at[0, 0],
                    self.send_sems.at[n, r],
                    device,
                )


class ScatterSteps:
    def __init__(self, scatter, part_ref):
        self.scatter, self.part = scatter, part_ref

    def load(self, k, i, j):
        s = self.scatter
        at = (s.block(s.order(k), i), s.sides[j])
        return pltpu.make_async_copy(self.part.at[at], s.total.at[at], s.core_sems.at[at])

    def start(self, k):
        for i in range(2):
            for j in range(2):
                self.load(k, i, j).start()

    def first(self, k, i, j):
        self.load(k, i, j).wait()
        self.scatter.first(self.scatter.order(k), i, j)

    def steps(self):
        s, part = self.scatter, functools.partial
        rounds = s.p.rounds
        out = [part(self.start, k) for k in range(rounds)]
        for k in range(rounds + 2):
            if k < rounds:
                out += [part(self.first, k, i, j) for i in range(2) for j in range(2)]
            if 0 <= k - 1 < rounds:
                for i in range(2):
                    out.append(part(s.second0, s.order(k - 1), i))
                    out.append(part(s.second1, s.order(k - 1), i))
            if 0 <= k - 2 < rounds:
                out += [part(s.third, s.order(k - 2), h) for h in range(2)]
        return out


def interleave(*groups):
    marked = []
    for n, (low, high, steps) in enumerate(groups):
        for i, step in enumerate(steps):
            marked.append((low + (high - low) * (i + 0.5) / len(steps), n, step))
    for _, _, step in sorted(marked, key=lambda m: (m[0], m[1])):
        step()


class Weights:
    def __init__(self, inputs, lg_ref, outs, router, bufs, sems):
        self.inputs, self.lg, self.outs, self.router = inputs, lg_ref, outs, router
        self.held, self.sums = bufs[:5], bufs[5:]
        self.load_sems, self.store_sems = sems
        self.groups, self.parts, self.tok, self.width = inputs[0].shape

    @staticmethod
    def scratch(local, tok, ffe, width):
        dma = pltpu.SemaphoreType.DMA
        act = pltpu.VMEM((2, local, tok, ffe), BF)
        bufs = [pltpu.VMEM((2, tok, width), BF)] * 2 + [act] * 3
        bufs += [pltpu.VMEM((2, local, width, ffe), F32)] * 2
        return bufs + [pltpu.VMEM((2, local, ffe, width), F32)], [dma((5, 2)), dma((3, 2))]

    def loads(self, step):
        t, e, slot = step // self.groups, step % self.groups, step % 2
        return [
            pltpu.make_async_copy(
                ref.at[e, t] if n < 2 else ref.at[e],
                self.held[n].at[slot],
                self.load_sems.at[n, slot],
            )
            for n, ref in enumerate(self.inputs)
        ]

    def stores(self, t):
        cols = pl.ds(pl.multiple_of(t * self.width, self.width), self.width)
        targets = (
            self.outs[0].at[:, cols, :],
            self.outs[1].at[:, cols, :],
            self.outs[2].at[:, :, cols],
        )
        return [
            pltpu.make_async_copy(total.at[t % 2], target, self.store_sems.at[i, t % 2])
            for i, (total, target) in enumerate(zip(self.sums, targets))
        ]

    def start(self):
        for copy in self.loads(0):
            copy.start()
        self.router[...] = jnp.zeros_like(self.router)

    def step(self, s):
        t, e, slot = s // self.groups, s % self.groups, s % 2
        for copy in self.loads(s):
            copy.wait()

        @pl.when(s + 1 < self.groups * self.parts)
        def _():
            for copy in self.loads(s + 1):
                copy.start()

        @pl.when(jnp.logical_and(e == 0, t >= 2))
        def _():
            for copy in self.stores(t - 2):
                copy.wait()

        @pl.when(e == 0)
        def _():
            for total in self.sums:
                total[t % 2] = jnp.zeros(total.shape[1:], F32)

        x, up, hid, gga, uga = (ref[slot] for ref in self.held)
        for j in range(hid.shape[0]):
            self.sums[0][t % 2, j] += rows_product(x, gga[j])
            self.sums[1][t % 2, j] += rows_product(x, uga[j])
            self.sums[2][t % 2, j] += rows_product(hid[j], up)
        self.router[t] += rows_product(x, self.lg[e])

        @pl.when(e == self.groups - 1)
        def _():
            for copy in self.stores(t):
                copy.start()

    def steps(self, size):
        total = self.groups * self.parts

        def chunk(first):
            def body(s, carry):
                self.step(s)
                return carry

            lax.fori_loop(first, min(first + size, total), body, 0)

        return [functools.partial(chunk, first) for first in range(0, total, size)]

    def finish(self):
        for t in (self.parts - 2, self.parts - 1):
            for copy in self.stores(t):
                copy.wait()


class Chain:
    def __init__(self, p, sends, held, up, down, done, out, sems):
        self.p, self.sends = p, sends
        self.held, self.up, self.down, self.done, self.out = held, up, down, done, out
        self.up_sems, self.down_sems, self.out_sems = sems

    def step(self, way):
        p = self.p
        high = jnp.clip(p.high + way, 0, p.rounds - 1)
        return p.high + way == high, (2 * high + p.low, p.t)

    def wait(self, ref, sem, device):
        arrived(ref, sem, self.sends.sems.at[0], device)

    def piece(self, i):
        valid = jnp.logical_and(i >= 0, i < self.p.rounds)
        return valid, jnp.clip(i, 0, self.p.rounds - 1)

    def receive(self, i, way, valid):
        buf, sems = (self.up, self.up_sems) if way > 0 else (self.down, self.down_sems)
        behind, source = self.step(-way)

        @pl.when(jnp.logical_and(valid, behind))
        def _():
            received, held = buf(i), self.held(i)
            self.wait(received, sems.at[i], source)
            held[...] = held[...] + received[...]

    def toward(self, k, way):
        valid, i = self.piece(self.p.high + way * k)
        self.receive(i, way, valid)
        buf, sems = (self.up, self.up_sems) if way > 0 else (self.down, self.down_sems)
        self.sends.start(self.held(i), buf(i), sems.at[i], self.step(way)[1], valid)

    def close(self):
        for way in (1, -1):
            self.receive(self.p.high, way, True)

    def spread(self):
        high = self.p.high
        for way in (1, -1):
            there, ahead = self.step(way)
            self.sends.start(self.done, self.out(high), self.out_sems.at[high], ahead, there)

    def follow(self, k, way, then=None):
        valid, i = self.piece(self.p.high - way * k)
        piece, sem = self.out(i), self.out_sems.at[i]

        @pl.when(valid)
        def _():
            self.wait(piece, sem, self.step(-way)[1])

        there, ahead = self.step(way)
        self.sends.start(piece, piece, sem, ahead, jnp.logical_and(valid, there))
        if then is not None:
            then(i, valid)


class Reduce:
    def __init__(self, p, refs, outs, ua, ub, bufs, sems):
        self.p, self.refs, self.outs, self.ua, self.ub = p, refs, outs, ua, ub
        self.base = 2 * p.rounds * ua
        self.a_own, self.a_y, self.a_up, self.a_down = bufs[:4]
        self.b_own, self.b_up, self.b_down, self.b_y, self.b_done = bufs[4:]
        send_sems, self.own_sems, self.y_sems = sems[:3]
        a_lines, self.ay_sems, b_lines, self.by_sems = sems[3:6], sems[6], sems[7:10], sems[10]
        self.store_sems = sems[11]
        self.sends = Sends(send_sems)

        def pieces(buf, w, size):
            return lambda i: buf.at[w, pl.ds(i * size, size)]

        self.a_chains = [
            Chain(
                p,
                self.sends,
                pieces(self.a_own, w, ua),
                pieces(self.a_up, w, ua),
                pieces(self.a_down, w, ua),
                self.a_own.at[w, pl.ds(p.high * ua, ua)],
                functools.partial(self.a_out, w, p.low),
                [line.at[w] for line in a_lines],
            )
            for w in range(len(refs))
        ]
        self.b_chains = [
            Chain(
                p,
                self.sends,
                pieces(self.b_own, w, 2 * ub),
                pieces(self.b_up, w, 2 * ub),
                pieces(self.b_down, w, 2 * ub),
                self.b_done.at[w],
                functools.partial(self.b_out, w),
                [line.at[w] for line in b_lines],
            )
            for w in range(len(refs))
        ]

    @staticmethod
    def scratch(count, rounds, ua, ub, width):
        dma = pltpu.SemaphoreType.DMA

        def blocks(n):
            return pltpu.VMEM((count, n, 16, width), BF)

        bufs = [blocks(rounds * ua)] * 4 + [blocks(2 * rounds * ub)] * 3
        bufs += [blocks(ub), blocks(2 * ub)]
        sends = count * (10 * (rounds - 1) + 8)
        line = dma((count, rounds))
        sems = [dma((sends,)), dma((count, 2)), dma((count,)), line, line, line, line]
        sems += [line, line, line, dma((count, 2)), dma((count, 2))]
        return bufs, sems

    def a_out(self, w, low, i):
        return self.outs[w].at[pl.ds((low * self.p.rounds + i) * self.ua, self.ua)]

    def b_out(self, w, i):
        return self.outs[w].at[pl.ds(self.base + 2 * i * self.ub, 2 * self.ub)]

    def wait(self, ref, sem, device):
        arrived(ref, sem, self.sends.sems.at[0], device)

    def a_rows(self, w, low):
        size = self.p.rounds * self.ua
        return self.refs[w].at[pl.ds(low * size, size)]

    def load(self, w, n):
        if n == 0:
            src, dst = self.a_rows(w, self.p.low), self.a_own.at[w]
        else:
            src = self.refs[w].at[pl.ds(self.base, 2 * self.p.rounds * self.ub)]
            dst = self.b_own.at[w]
        return pltpu.make_async_copy(src, dst, self.own_sems.at[w, n])

    def store(self, w, n):
        p = self.p
        if n == 0:
            src, dst = self.a_chains[w].done, self.a_out(w, p.low, p.high)
        else:
            src, dst = self.b_done.at[w], self.b_out(w, p.high)
        return pltpu.make_async_copy(src, dst, self.store_sems.at[w, n])

    def begin(self, w):
        p = self.p
        self.sends.start(self.a_rows(w, 1 - p.low), self.a_y.at[w], self.y_sems.at[w], p.y)
        for n in range(2):
            self.load(w, n).start()

    def b_first(self, w):
        self.load(w, 1).wait()

    def a_first(self, w):
        self.load(w, 0).wait()
        self.wait(self.a_y.at[w], self.y_sems.at[w], self.p.y)
        own = self.a_own.at[w]
        own[...] = own[...] + self.a_y[w]

    def a_pass(self, w, i, valid, src=None):
        dst = self.a_out(w, self.p.low, i)
        self.sends.start(dst if src is None else src, dst, self.ay_sems.at[w, i], self.p.y, valid)

    def a_close(self, w):
        chain = self.a_chains[w]
        chain.close()
        chain.spread()
        self.a_pass(w, self.p.high, None, chain.done)
        self.store(w, 0).start()

    def b_close(self, w):
        p = self.p
        self.b_chains[w].close()
        half = self.b_own.at[w, pl.ds((2 * p.high + 1 - p.low) * self.ub, self.ub)]
        self.sends.start(half, self.b_y.at[w], self.by_sems.at[w, 0], p.y)

    def b_pair(self, w):
        p = self.p
        self.wait(self.b_y.at[w], self.by_sems.at[w, 0], p.y)
        half = self.b_own[w, pl.ds((2 * p.high + p.low) * self.ub, self.ub)]
        done = self.b_done.at[w, pl.ds(p.low * self.ub, self.ub)]
        done[...] = half + self.b_y[w]
        self.sends.start(done, done, self.by_sems.at[w, 1], p.y)

    def b_spread(self, w):
        p = self.p
        other = self.b_done.at[w, pl.ds((1 - p.low) * self.ub, self.ub)]
        self.wait(other, self.by_sems.at[w, 1], p.y)
        self.b_chains[w].spread()
        self.store(w, 1).start()

    def streams(self, w):
        n, part = self.p.rounds, functools.partial
        a, b = self.a_chains[w], self.b_chains[w]

        def hops(move, distances, *then):
            return [[part(move, k, way, *then) for way in (1, -1)] for k in distances]

        out, back = range(n - 1, 0, -1), range(1, n)
        b_steps = [[part(self.b_first, w)]] + hops(b.toward, out)
        b_steps += [[part(self.b_close, w)], [part(self.b_pair, w)], [part(self.b_spread, w)]]
        b_steps += hops(b.follow, back)
        a_steps = [[part(self.begin, w)], [part(self.a_first, w)]] + hops(a.toward, out)
        a_steps += [[part(self.a_close, w)]] + hops(a.follow, back, part(self.a_pass, w))
        return a_steps, b_steps

    def turns(self, apart):
        count = len(self.refs)
        turns = []
        for w in range(count):
            a_steps, b_steps = self.streams(w)
            for n, step in enumerate(a_steps):
                turns.append((apart * w + n, w, 0, step))
            for n, step in enumerate(b_steps):
                turns.append((apart * w + n + 1, w, 1, step))
        turns.sort(key=lambda m: m[:3])
        return [
            [step for turn in turns if turn[0] == n for step in turn[3]]
            for n in range(turns[-1][0] + 1)
        ]

    def steps(self):
        return [step for turn in self.turns(1) for step in turn]

    def finish(self):
        p = self.p
        for w in range(len(self.refs)):
            for i in range(p.rounds):
                self.wait(self.a_out(w, 1 - p.low, i), self.ay_sems.at[w, i], p.y)
            for n in range(2):
                self.store(w, n).wait()
        self.sends.finish()


def pieces(blocks, groups):
    first = blocks * 9 // 16 // groups
    return first, blocks // groups - first


class Small:
    def __init__(self, p, ref, out, bufs, sems):
        self.p, self.small, self.small_out = p, ref, out
        self.s_own, self.s_core, self.s_x, self.s_y, self.s_z = bufs
        send_sems, self.s_pair_sems, self.s_y_sem, self.s_z_sems, self.s_gather_sems = sems
        self.sends = Sends(send_sems)

    @staticmethod
    def scratch(rounds, rows, width):
        dma = pltpu.SemaphoreType.DMA
        whole = pltpu.VMEM((2, rounds, rows, width), F32)
        half = pltpu.VMEM((rounds, rows, width), F32)
        sems = [dma((3 * rounds + 1,)), dma((2,)), dma, dma((rounds,)), dma((2, rounds))]
        return [whole, whole, whole, half, half], sems

    def wait(self, ref, sem, device):
        arrived(ref, sem, self.sends.sems.at[0], device)

    def source(self, r):
        p = self.p
        high = lax.rem(p.high + r, p.rounds)
        return high, (2 * high + p.low, p.t)

    def small_pair(self):
        p = self.p
        self.sends.start(self.small, self.s_core, self.s_pair_sems.at[0], p.c)
        self.wait(self.s_core, self.s_pair_sems.at[0], p.c)
        self.s_own[...] = self.small[...] + self.s_core[...]
        self.sends.start(self.s_own, self.s_x, self.s_pair_sems.at[1], p.x)

    def small_x(self):
        p = self.p
        self.wait(self.s_x, self.s_pair_sems.at[1], p.x)
        self.s_x[...] = self.s_x[...] + self.s_own[...]
        self.sends.start(self.s_x.at[1 - p.low], self.s_y, self.s_y_sem, p.y)

    def small_y(self):
        p = self.p
        self.wait(self.s_y, self.s_y_sem, p.y)
        self.s_y[...] = self.s_y[...] + self.s_x[p.low]
        for r in range(1, p.rounds):
            self.sends.start(
                self.s_y.at[p.far(r)], self.s_z.at[r], self.s_z_sems.at[r], p.z(r)
            )

    def small_z(self):
        p = self.p
        total = self.s_y[p.high]
        for r in range(1, p.rounds):
            self.wait(self.s_z.at[r], self.s_z_sems.at[r], self.source(r)[1])
            total += self.s_z[r]
        self.small_out[p.low, p.high] = total
        piece = self.small_out.at[p.low, p.high]
        for device in [p.z(r) for r in range(1, p.rounds)] + [p.y]:
            self.sends.start(piece, piece, self.s_gather_sems.at[p.low, p.high], device)

    def small_pass(self):
        p = self.p
        for r in range(1, p.rounds):
            high, source = self.source(r)
            piece = self.small_out.at[p.low, high]
            self.wait(piece, self.s_gather_sems.at[p.low, high], source)
            self.sends.start(piece, piece, self.s_gather_sems.at[p.low, high], p.y)

    def finish(self):
        p = self.p
        for high in range(p.rounds):
            piece = self.small_out.at[1 - p.low, high]
            self.wait(piece, self.s_gather_sems.at[1 - p.low, high], p.y)
        self.sends.finish()

    def steps(self):
        return [self.small_pair, self.small_x, self.small_y, self.small_z, self.small_pass]


def reduce_kernel(count, ua, ub, *refs):
    refs = list(refs)

    def take(n):
        taken = refs[:n]
        del refs[:n]
        return taken

    w_refs, (rest, lg, part), inputs = take(count), take(3), take(5)
    outs, (small_out, mixed), w_outs = take(count), take(2), take(3)
    bufs, sems, m_bufs, m_sems, w_bufs, w_sems = (take(n) for n in (9, 12, 5, 5, 8, 2))
    small, router = take(2)
    s_bufs, s_sems = take(6), take(7)
    p = Place(inputs[0].shape[0])
    weights = Weights(inputs, lg, w_outs, router, w_bufs, w_sems)
    weights.start()
    p.greet([p.y, p.x, p.c] + [p.z(r) for r in range(1, p.rounds)])
    reduce = Reduce(p, w_refs, outs, ua, ub, bufs, sems)
    total = Small(p, small, small_out, m_bufs, m_sems)
    scatter = Scatter(p, s_bufs, s_sems)

    def fill():
        experts = small.shape[2]
        small[...] = jnp.zeros_like(small)
        for t in range(router.shape[0]):
            both = router[t, :, :experts] + router[t, :, experts:]
            small[t // p.rounds, t % p.rounds] = both.T
        last = router.shape[0]
        small[last // p.rounds, last % p.rounds] = rest[...]

    interleave(
        (0.0, 1.0, reduce.steps()),
        (0.0, 1.0, ScatterSteps(scatter, part).steps()),
        (0.0, 0.6, weights.steps(2)),
        (0.6, 1.0, [fill] + total.steps()),
    )
    reduce.finish()
    total.finish()
    scatter.finish(mixed)
    weights.finish()


def reduce_shared(weight_grads, rest, lg, part, inputs, cid):
    groups, tensors, tok, part_width = inputs[0].shape
    count, (rows, width) = len(weight_grads), weight_grads[0].shape
    local, ffe = inputs[2].shape[1], inputs[2].shape[3]
    full = tensors * part_width
    rounds = groups // 2
    blocks = rows // 16
    ua, ub = pieces(blocks, groups)
    shape = (blocks, 16, width)
    small_shape = (2, rounds) + rest.shape
    m_bufs, m_sems = Small.scratch(rounds, small_shape[2], width)
    bufs, sems = Reduce.scratch(count, rounds, ua, ub, width)
    w_bufs, w_sems = Weights.scratch(local, tok, ffe, part_width)
    s_bufs, s_sems = Scatter.scratch(groups, tok, part_width, tok // 8 * 7)
    outs = pl.pallas_call(
        functools.partial(reduce_kernel, count, ua, ub),
        name="reduce_shared",
        in_specs=[ANY] * count + [VMEM, VMEM] + [ANY] * 6,
        out_specs=[ANY] * count + [VMEM, VMEM, ANY, ANY, ANY],
        out_shape=[jax.ShapeDtypeStruct(shape, BF)] * count
        + [
            jax.ShapeDtypeStruct(small_shape, F32),
            jax.ShapeDtypeStruct((tok, part_width), F32),
            jax.ShapeDtypeStruct((local, full, ffe), F32),
            jax.ShapeDtypeStruct((local, full, ffe), F32),
            jax.ShapeDtypeStruct((local, ffe, full), F32),
        ],
        scratch_shapes=bufs
        + sems
        + m_bufs
        + m_sems
        + w_bufs
        + w_sems
        + [
            pltpu.VMEM(small_shape, F32),
            pltpu.VMEM((tensors, part_width, lg.shape[2]), F32),
        ]
        + s_bufs
        + s_sems,
        compiler_params=pltpu.CompilerParams(
            collective_id=cid, has_side_effects=True, vmem_limit_bytes=62 * 2**20
        ),
        cost_estimate=pl.CostEstimate(
            flops=6 * groups * tok * full * ffe * local,
            bytes_accessed=count * rows * width * 8,
            transcendentals=0,
        ),
    )(*[w.reshape(shape) for w in weight_grads], rest, lg, part, *inputs)
    weight_grads = [o.reshape(rows, width) for o in outs[:count]]
    small = outs[count].reshape((-1,) + rest.shape)
    return weight_grads, small, outs[count + 1], outs[count + 2 :]


def attention_kernel(
    tokens_ref,
    seg_row_ref,
    gain1_ref,
    wq_hbm,
    wk_hbm,
    wv_hbm,
    wo_hbm,
    qg_ref,
    kg_ref,
    gain2_ref,
    cos_ref,
    sin_ref,
    normed_hbm,
    q_hbm,
    k_hbm,
    q_rot_hbm,
    k_rot_hbm,
    v_hbm,
    att_hbm,
    res_ref,
    normed_two_ref,
    scales_ref,
    x_ref,
    wq_ref,
    wk_ref,
    wv_ref,
    wo_ref,
    normed_ref,
    q_ref,
    k_ref,
    q_rot_ref,
    k_rot_ref,
    v_ref,
    att_ref,
    move_sems,
    sent,
    from_c,
    from_x,
    squares,
    send_sems,
    x_sems,
    c_sems,
    x_sem,
    square_sems,
):
    tok, width = tokens_ref.shape
    parts = x_ref.shape[0]
    full = parts * width
    p = Place(2)
    opposite = (p.e, 2 * (1 - p.side) + 1 - p.core)
    sends = Sends(send_sems)
    moves = Moves(
        [
            (wq_hbm, wq_ref),
            (wk_hbm, wk_ref),
            (wv_hbm, wv_ref),
            (wo_hbm, wo_ref),
            (normed_ref, normed_hbm),
            (q_ref, q_hbm),
            (k_ref, k_hbm),
            (v_ref, v_hbm),
            (q_rot_ref, q_rot_hbm),
            (k_rot_ref, k_rot_hbm),
            (att_ref, att_hbm),
        ],
        move_sems,
    )
    moves.start(0, 1, 2, 3)
    p.greet([p.x, p.c, opposite])
    sends.start(tokens_ref, x_ref.at[p.t], x_sems.at[p.t], p.x)
    sends.start(tokens_ref, x_ref.at[p.t], x_sems.at[p.t], p.c)
    x_ref[p.t] = tokens_ref[...]

    def wait(ref, sem, device):
        arrived(ref, sem, send_sems.at[0], device)

    def squared(t):
        values = x_ref[t].astype(F32)
        return jnp.sum(values * values, axis=-1, keepdims=True)

    total = squared(p.t)
    tx, tc, to = p.x[1], p.c[1], opposite[1]
    wait(x_ref.at[tx], x_sems.at[tx], p.x)
    sends.start(x_ref.at[tx], x_ref.at[tx], x_sems.at[tx], p.c)
    total += squared(tx)
    wait(x_ref.at[tc], x_sems.at[tc], p.c)
    total += squared(tc)
    wait(x_ref.at[to], x_sems.at[to], p.c)
    total += squared(to)
    scale_one = lax.rsqrt(total / full + EPSILON)
    scales_ref[:, 0:1] = scale_one
    for t in range(parts):
        normed_ref[:, t * width : (t + 1) * width] = (
            x_ref[t].astype(F32) * scale_one * gain1_ref[:, t * width : (t + 1) * width]
        ).astype(BF)
    moves.start(4)
    normed = normed_ref[...]
    moves.wait(0, 1, 2)
    q_ref[...] = dot(normed, wq_ref[...])
    k_ref[...] = dot(normed, wk_ref[...])
    v_ref[...] = dot(normed, wv_ref[...]).astype(BF)
    moves.start(5, 6, 7)
    same = as_column(seg_row_ref[...]) == seg_row_ref[...].astype(F32)
    cosine, sine = cos_ref[...], sin_ref[...]

    def turned(values, gain):
        scale = lax.rsqrt(jnp.mean(values * values, axis=-1, keepdims=True) + EPSILON)
        scaled = values * scale * gain
        return (scaled * cosine + pltpu.roll(scaled, HEAD_DIM // 2, 1) * sine).astype(BF)

    for head in range(q_ref.shape[1] // HEAD_DIM):
        cols = slice(head * HEAD_DIM, (head + 1) * HEAD_DIM)
        q_rot = turned(q_ref[:, cols], qg_ref[...])
        k_rot = turned(k_ref[:, cols], kg_ref[...])
        q_rot_ref[:, cols] = q_rot
        k_rot_ref[:, cols] = k_rot
        scores = jnp.where(same, cols_product(q_rot, k_rot) * HEAD_DIM ** (-0.5), -1e30)
        weights = jnp.exp(scores - jnp.max(scores, axis=-1, keepdims=True))
        probs = (weights / jnp.sum(weights, axis=-1, keepdims=True)).astype(BF)
        att_ref[:, cols] = dot(probs, v_ref[:, cols]).astype(BF)

    moves.start(8, 9, 10)
    moves.wait(3)
    attended = att_ref[...]

    def branch(side, core):
        t = 2 * side + core
        return dot(attended, wo_ref[:, pl.ds(pl.multiple_of(t * width, width), width)])

    for i, side in enumerate((1 - p.side, p.side)):
        sent[i] = branch(side, 1 - p.core).astype(BF)
        sends.start(sent.at[i], from_c.at[side], c_sems.at[side], p.c)
    part = branch(1 - p.side, p.core)
    wait(from_c.at[1 - p.side], c_sems.at[1 - p.side], p.c)
    sent[2] = (part + from_c[1 - p.side].astype(F32)).astype(BF)
    sends.start(sent.at[2], from_x, x_sem, p.x)
    part = branch(p.side, p.core) + tokens_ref[...].astype(F32)
    wait(from_c.at[p.side], c_sems.at[p.side], p.c)
    part += from_c[p.side].astype(F32)
    wait(from_x, x_sem, p.x)
    residual = part + from_x[...].astype(F32)
    res_ref[...] = residual
    total = jnp.sum(residual * residual, axis=-1, keepdims=True)
    squares[p.t] = jnp.broadcast_to(total, (tok, 128)).T[0:8, :]
    mine = pl.ds(pl.multiple_of(p.t * width, width), width)
    for device in (p.x, p.c, opposite):
        sends.start(squares.at[p.t], squares.at[p.t], square_sems.at[p.t], device)
    for device in (p.x, p.c, opposite):
        wait(squares.at[device[1]], square_sems.at[device[1]], device)
    whole = squares[0]
    for t in range(1, parts):
        whole += squares[t]
    whole = as_column(whole[0:1, :])
    scale_two = lax.rsqrt(whole / full + EPSILON)
    scales_ref[:, 1:2] = scale_two
    normed_two_ref[...] = (residual * scale_two * gain2_ref[:, mine]).astype(BF)
    moves.wait(4, 5, 6, 7, 8, 9, 10)
    sends.finish()


def attention(
    tokens, segments, norm1_gain, wq, wk, wv, wo, query_gain, key_gain, norm2_gain, tables, cid
):
    tok, width = tokens.shape
    full, here = wq.shape
    parts = full // width
    dma = pltpu.SemaphoreType.DMA

    def shape(*dims, dtype=BF):
        return jax.ShapeDtypeStruct(dims, dtype)

    return pl.pallas_call(
        attention_kernel,
        name="attention",
        in_specs=[VMEM] * 3 + [ANY] * 4 + [VMEM] * 5,
        out_specs=[ANY] * 7 + [VMEM] * 3,
        out_shape=[
            shape(tok, full),
            shape(tok, here, dtype=F32),
            shape(tok, here, dtype=F32),
            shape(tok, here),
            shape(tok, here),
            shape(tok, here),
            shape(tok, here),
            shape(tok, width, dtype=F32),
            shape(tok, width),
            shape(tok, 2, dtype=F32),
        ],
        scratch_shapes=[
            pltpu.VMEM((parts, tok, width), BF),
            pltpu.VMEM((full, here), BF),
            pltpu.VMEM((full, here), BF),
            pltpu.VMEM((full, here), BF),
            pltpu.VMEM((here, full), BF),
            pltpu.VMEM((tok, full), BF),
            pltpu.VMEM((tok, here), F32),
            pltpu.VMEM((tok, here), F32),
            pltpu.VMEM((tok, here), BF),
            pltpu.VMEM((tok, here), BF),
            pltpu.VMEM((tok, here), BF),
            pltpu.VMEM((tok, here), BF),
            dma((11,)),
            pltpu.VMEM((3, tok, width), BF),
            pltpu.VMEM((2, tok, width), BF),
            pltpu.VMEM((tok, width), BF),
            pltpu.VMEM((parts, 8, tok), F32),
            dma((9,)),
            dma((parts,)),
            dma((2,)),
            dma,
            dma((parts,)),
        ],
        compiler_params=pltpu.CompilerParams(
            collective_id=cid, has_side_effects=True, vmem_limit_bytes=56 * 2**20
        ),
        cost_estimate=pl.CostEstimate(
            flops=2 * tok * full * here * 4, bytes_accessed=24 * 2**20, transcendentals=0
        ),
    )(
        tokens,
        segments[None, :],
        norm1_gain[None, :],
        wq,
        wk,
        wv,
        wo,
        query_gain[None, :],
        key_gain[None, :],
        norm2_gain[None, :],
        *tables,
    )


def backward_kernel(
    groups,
    ua,
    ub,
    grad_ref,
    res_ref,
    cot_ref,
    tokens_ref,
    scales_ref,
    gain1_ref,
    gain2_ref,
    seg_row_ref,
    qg_ref,
    kg_ref,
    cos_ref,
    sin_ref,
    normed_hbm,
    q_hbm,
    k_hbm,
    q_rot_hbm,
    k_rot_hbm,
    v_hbm,
    att_hbm,
    wq_hbm,
    wk_hbm,
    wv_hbm,
    wo_hbm,
    tokens_grad_ref,
    wq_grad_hbm,
    wk_grad_hbm,
    wv_grad_hbm,
    wo_grad_ref,
    norm1_ref,
    norm2_ref,
    gains_ref,
    res_grad,
    low,
    att_grad,
    dq,
    dk,
    dv,
    sent,
    from_c,
    from_x,
    means,
    send_sems,
    low_sems,
    c_sems,
    x_sem,
    mean_sems,
    normed_ref,
    q_ref,
    k_ref,
    q_rot_ref,
    k_rot_ref,
    v_ref,
    att_ref,
    wq_ref,
    wk_ref,
    wv_ref,
    wo_ref,
    wq_grad_ref,
    wk_grad_ref,
    wv_grad_ref,
    move_sems,
    *reduce_refs,
):
    tok, width = tokens_ref.shape
    parts = low.shape[0]
    full = parts * width
    p = Place(groups)
    opposite = (p.e, 2 * (1 - p.side) + 1 - p.core)
    sends = Sends(send_sems)
    partners, turns = [p.x, p.c, opposite], []
    wo_part = wo_grad_ref
    if reduce_refs:
        wo_part, bufs, sems = reduce_refs[0], reduce_refs[1:10], reduce_refs[10:]
        half = wo_part.shape[0] // 2
        halves = [pl.ds(side * half, half) for side in (p.side, 1 - p.side)]
        parts_in = [wo_part.at[rows] for rows in halves]
        parts_out = [wo_grad_ref.at[rows] for rows in halves]
        reduce = Reduce(p, parts_in, parts_out, ua, ub, bufs, sems)
        turns = reduce.turns(1)
        partners += [p.y] + [p.z(r) for r in range(1, p.rounds)]
    moves = Moves(
        [
            (att_hbm, att_ref),
            (wo_hbm, wo_ref),
            (q_rot_hbm, q_rot_ref),
            (k_rot_hbm, k_rot_ref),
            (v_hbm, v_ref),
            (q_hbm, q_ref),
            (k_hbm, k_ref),
            (wq_hbm, wq_ref),
            (wk_hbm, wk_ref),
            (wv_hbm, wv_ref),
            (normed_hbm, normed_ref),
            (wq_grad_ref, wq_grad_hbm),
            (wk_grad_ref, wk_grad_hbm),
            (wv_grad_ref, wv_grad_hbm),
        ],
        move_sems,
    )
    moves.start(*range(11))
    p.greet(partners)

    def meanwhile(count):
        for _ in range(count):
            for step in turns.pop(0) if turns else []:
                step()

    def wait(ref, sem, device):
        arrived(ref, sem, send_sems.at[0], device)

    def mean_start(n, total):
        means[n, p.t] = jnp.broadcast_to(total, (tok, 128)).T[0:8, :]
        for device in (p.x, p.c, opposite):
            sends.start(means.at[n, p.t], means.at[n, p.t], mean_sems.at[n, p.t], device)

    def mean_end(n):
        for device in (p.x, p.c, opposite):
            wait(means.at[n, device[1]], mean_sems.at[n, device[1]], device)
        whole = means[n, 0]
        for t in range(1, parts):
            whole += means[n, t]
        return as_column(whole[0:1, :]) / full

    scale_one, scale_two = scales_ref[:, 0:1], scales_ref[:, 1:2]
    grad, residual = grad_ref[...], res_ref[...]
    mine = pl.ds(pl.multiple_of(p.t * width, width), width)
    h2 = grad * gain2_ref[:, mine]
    mean_start(0, jnp.sum(h2 * residual, axis=-1, keepdims=True))
    norm2_ref[...] = jnp.sum(grad * residual * scale_two, axis=0, keepdims=True)
    upstream = cot_ref[...].astype(F32)
    res_grad[...] = upstream + scale_two * (
        h2 - residual * scale_two * scale_two * mean_end(0)
    )
    low[p.t] = res_grad[...].astype(BF)
    sends.start(low.at[p.t], low.at[p.t], low_sems.at[p.t], p.x)
    sends.start(low.at[p.t], low.at[p.t], low_sems.at[p.t], p.c)
    moves.wait(0, 1)
    attended = att_ref[...]

    def through_out(t, first=False):
        blocks = wo_part.shape[0] // parts
        product = rows_product(attended, low[t]).astype(BF)
        wo_part[pl.ds(t * blocks, blocks)] = product.reshape(blocks, 16, width)
        cols = pl.ds(pl.multiple_of(t * width, width), width)
        product = cols_product(low[t], wo_ref[:, cols])
        att_grad[...] = product if first else att_grad[...] + product

    through_out(p.t, True)
    tx, tc, to = p.x[1], p.c[1], opposite[1]
    wait(low.at[tc], low_sems.at[tc], p.c)
    through_out(tc)
    meanwhile(1)
    wait(low.at[tx], low_sems.at[tx], p.x)
    sends.start(low.at[tx], low.at[tx], low_sems.at[tx], p.c)
    through_out(tx)
    wait(low.at[to], low_sems.at[to], p.c)
    through_out(to)
    meanwhile(1)

    same = as_column(seg_row_ref[...]) == seg_row_ref[...].astype(F32)
    cosine, sine = cos_ref[...], sin_ref[...]
    factor = HEAD_DIM ** (-0.5)
    moves.wait(2, 3, 4, 5, 6)

    def to_pre(rot_grad, pre, gain):
        normed_grad = rot_grad * cosine - pltpu.roll(rot_grad, HEAD_DIM // 2, 1) * sine
        scale = lax.rsqrt(jnp.mean(pre * pre, axis=-1, keepdims=True) + EPSILON)
        gain_grad = jnp.sum(normed_grad * pre * scale, axis=0, keepdims=True)
        return rms_backward(pre, scale, normed_grad * gain).astype(BF), gain_grad

    query_gain, key_gain = jnp.zeros((1, HEAD_DIM), F32), jnp.zeros((1, HEAD_DIM), F32)
    for head in range(q_ref.shape[1] // HEAD_DIM):
        cols = slice(head * HEAD_DIM, (head + 1) * HEAD_DIM)
        q_rot, k_rot, value = q_rot_ref[:, cols], k_rot_ref[:, cols], v_ref[:, cols]
        scores = jnp.where(same, cols_product(q_rot, k_rot) * factor, -1e30)
        weights = jnp.exp(scores - jnp.max(scores, axis=-1, keepdims=True))
        probs = weights / jnp.sum(weights, axis=-1, keepdims=True)
        out_grad = att_grad[:, cols].astype(BF)
        dv[:, cols] = rows_product(probs.astype(BF), out_grad).astype(BF)
        prob_grad = cols_product(out_grad, value)
        score_grad = (
            probs * (prob_grad - jnp.sum(probs * prob_grad, axis=-1, keepdims=True))
        ).astype(BF)
        dq[:, cols], gain_grad = to_pre(dot(score_grad, k_rot) * factor, q_ref[:, cols], qg_ref[...])
        query_gain += gain_grad
        dk[:, cols], gain_grad = to_pre(
            rows_product(score_grad, q_rot) * factor, k_ref[:, cols], kg_ref[...]
        )
        key_gain += gain_grad
        meanwhile(1)
    gains_ref[:, :HEAD_DIM] = query_gain
    gains_ref[:, HEAD_DIM:] = key_gain
    moves.wait(7, 8, 9, 10)

    def normed_part(side, core):
        rows = pl.ds(pl.multiple_of((2 * side + core) * width, width), width)
        return (
            cols_product(dq[...], wq_ref[rows, :])
            + cols_product(dk[...], wk_ref[rows, :])
            + cols_product(dv[...], wv_ref[rows, :])
        )

    for i, side in enumerate((1 - p.side, p.side)):
        sent[i] = normed_part(side, 1 - p.core).astype(BF)
        sends.start(sent.at[i], from_c.at[side], c_sems.at[side], p.c)
    part = normed_part(1 - p.side, p.core)
    wait(from_c.at[1 - p.side], c_sems.at[1 - p.side], p.c)
    sent[2] = (part + from_c[1 - p.side].astype(F32)).astype(BF)
    sends.start(sent.at[2], from_x, x_sem, p.x)
    part = normed_part(p.side, p.core)
    meanwhile(1)
    for t in range(parts):
        rows = slice(t * width, (t + 1) * width)
        wq_grad_ref[rows, :] = rows_product(normed_ref[:, rows], dq[...]).astype(BF)
    moves.start(11)
    meanwhile(1)
    wait(from_c.at[p.side], c_sems.at[p.side], p.c)
    part += from_c[p.side].astype(F32)
    wait(from_x, x_sem, p.x)
    part += from_x[...].astype(F32)
    own = tokens_ref[...].astype(F32)
    h1 = part * gain1_ref[:, mine]
    mean_start(1, jnp.sum(h1 * own, axis=-1, keepdims=True))
    norm1_ref[...] = jnp.sum(part * own * scale_one, axis=0, keepdims=True)
    meanwhile(1)
    for t in range(parts):
        rows = slice(t * width, (t + 1) * width)
        wk_grad_ref[rows, :] = rows_product(normed_ref[:, rows], dk[...]).astype(BF)
    moves.start(12)
    meanwhile(1)
    for t in range(parts):
        rows = slice(t * width, (t + 1) * width)
        wv_grad_ref[rows, :] = rows_product(normed_ref[:, rows], dv[...]).astype(BF)
    moves.start(13)
    tokens_grad_ref[...] = res_grad[...] + scale_one * (
        h1 - own * scale_one * scale_one * mean_end(1)
    )
    meanwhile(len(turns))
    moves.wait(11, 12, 13)
    if reduce_refs:
        reduce.finish()
    sends.finish()


def backward(groups, direct, cid, *arrays):
    tok, width = arrays[3].shape
    full, here = arrays[19].shape
    parts = full // width
    dma = pltpu.SemaphoreType.DMA

    def shape(*dims, dtype=BF):
        return jax.ShapeDtypeStruct(dims, dtype)

    outs = [
        shape(tok, width, dtype=F32),
        shape(full, here),
        shape(full, here),
        shape(full, here),
        shape(full // 16, 16, here),
        shape(1, width, dtype=F32),
        shape(1, width, dtype=F32),
        shape(1, 2 * HEAD_DIM, dtype=F32),
    ]
    scratch = [
        pltpu.VMEM((tok, width), F32),
        pltpu.VMEM((parts, tok, width), BF),
        pltpu.VMEM((tok, here), F32),
        pltpu.VMEM((tok, here), BF),
        pltpu.VMEM((tok, here), BF),
        pltpu.VMEM((tok, here), BF),
        pltpu.VMEM((3, tok, width), BF),
        pltpu.VMEM((2, tok, width), BF),
        pltpu.VMEM((tok, width), BF),
        pltpu.VMEM((2, parts, 8, tok), F32),
        dma((12,)),
        dma((parts,)),
        dma((2,)),
        dma,
        dma((2, parts)),
    ]
    scratch += [pltpu.VMEM(a.shape, a.dtype) for a in arrays[12:]]
    scratch += [pltpu.VMEM((full, here), BF)] * 3 + [dma((14,))]
    out_specs = [VMEM] + [ANY] * 3 + [VMEM] * 4
    ua, ub = pieces(full // 32, groups)
    if direct:
        out_specs[4] = ANY
        bufs, sems = Reduce.scratch(2, groups // 2, ua, ub, width)
        scratch += [pltpu.VMEM(outs[4].shape, BF)] + bufs + sems
    return pl.pallas_call(
        functools.partial(backward_kernel, groups, ua, ub),
        name="backward",
        in_specs=[VMEM] * 12 + [ANY] * 11,
        out_specs=out_specs,
        out_shape=outs,
        scratch_shapes=scratch,
        compiler_params=pltpu.CompilerParams(
            collective_id=cid, has_side_effects=True, vmem_limit_bytes=62 * 2**20
        ),
        cost_estimate=pl.CostEstimate(
            flops=2 * tok * full * here * 8, bytes_accessed=36 * 2**20, transcendentals=0
        ),
    )(*arrays)


def chosen_here(chosen, rank, local, j):
    columns = lax.broadcasted_iota(jnp.int32, chosen.shape, 1)
    return jnp.where(columns == rank * local + j, chosen, 0.0)


def sigmoid(values):
    return 1.0 / (1.0 + jnp.exp(-values))


def softmax(values):
    weights = jnp.exp(values - jnp.max(values, axis=-1, keepdims=True))
    return weights / jnp.sum(weights, axis=-1, keepdims=True)


def expert_backward(gate, here, g, u, v):
    s = sigmoid(g)
    gs = g * s
    hidden = (gs * u).astype(BF).astype(F32)
    gate_grad = here * jnp.sum(hidden * v, axis=-1, keepdims=True)
    hidden_grad = gate * v
    uga = (hidden_grad * gs).astype(BF)
    gga = (hidden_grad * u * s * (1.0 + g * (1.0 - s))).astype(BF)
    return gga, uga, gate_grad


def router_backward(probs, prob_grad):
    logit_grad = probs * (prob_grad - jnp.sum(probs * prob_grad, axis=-1, keepdims=True))
    high = logit_grad.astype(BF)
    return high, (logit_grad - high.astype(F32)).astype(BF)


def plain_experts(rank, x_all, up_all, mask_all, router_t, w_gate, w_up, w_down):
    local = w_gate.shape[0]

    def joined(quarters):
        return quarters.transpose(1, 0, 2).reshape(quarters.shape[1], -1)

    def quarters(values, parts):
        return values.reshape(values.shape[0], parts, -1).transpose(1, 0, 2).astype(BF)

    def block(sums, pieces):
        x_parts, up_parts, mask = pieces
        x, up, chosen = joined(x_parts), joined(up_parts), mask.astype(F32).T
        probs = softmax(cols_product(x, router_t))
        out = grad = 0.0
        prob_grad = jnp.zeros_like(probs)
        grads = [[], [], []]
        for j in range(local):
            here = chosen_here(chosen, rank, local, j)
            gate = jnp.sum(here * probs, axis=-1, keepdims=True)
            g, u, v = dot(x, w_gate[j]), dot(x, w_up[j]), cols_product(up, w_down[j])
            hidden = (gate * (g * sigmoid(g) * u).astype(BF).astype(F32)).astype(BF)
            gga, uga, gate_grad = expert_backward(gate, here, g, u, v)
            prob_grad += gate_grad
            out += dot(hidden, w_down[j])
            grad += cols_product(gga, w_gate[j]) + cols_product(uga, w_up[j])
            for n, (left, right) in enumerate(((x, gga), (x, uga), (hidden, up))):
                grads[n].append(rows_product(left, right))
        high, low = router_backward(probs, prob_grad)
        grad += dot(high, router_t) + dot(low, router_t)
        grads = [jnp.stack(g) for g in grads] + [rows_product(high, x) + rows_product(low, x)]
        parts = x_parts.shape[0]
        sums = [total + more for total, more in zip(sums, grads)]
        return sums, (quarters(out, parts), quarters(grad, parts))

    zeros = [jnp.zeros(w.shape, F32) for w in (w_gate, w_up, w_down, router_t)]
    sums, (out_part, grad_part) = lax.scan(block, zeros, (x_all, up_all, mask_all))
    return out_part, grad_part, sums[:3], sums[3]


def expert_scatter_kernel(
    x_ref,
    up_ref,
    mask_ref,
    router_ref,
    wg_ref,
    wu_ref,
    wd_ref,
    grad_ref,
    out_ref,
    hid_ref,
    gga_ref,
    uga_ref,
    lg_ref,
    *refs,
):
    bufs, sems = refs[:6], refs[6:13]
    x_buf, up_buf, out_buf, out_other, from_c, other, mine, hid, acts = refs[13:22]
    joined, products, probs_ref, load_sems, store_sems, weight_sems = refs[22:28]
    out_send_sems, out_sems = refs[28:]
    groups, parts, tok, width = x_ref.shape
    experts = mask_ref.shape[1]
    local, full, ffe = wg_ref.shape
    hidden_units = local * ffe
    last = 2 * hidden_units
    p = Place(groups)
    rounds = p.rounds
    scatter = Scatter(p, bufs, sems)

    def round_of(k):
        return lax.rem(k + 1, rounds)

    def loads(k, i):
        e = scatter.block(round_of(k), i)
        return [
            pltpu.make_async_copy(
                ref.at[e, t], buf.at[i, :, pl.ds(t * width, width)], load_sems.at[n, i, t]
            )
            for t in range(parts)
            for n, (ref, buf) in enumerate(((x_ref, x_buf), (up_ref, up_buf)))
        ]

    def columns(n, j):
        return pl.ds(n * hidden_units + j * ffe, ffe)

    def weight_loads():
        return [
            pltpu.make_async_copy(ref.at[j], joined.at[:, columns(n, j)], weight_sems.at[n, j])
            for j in range(local)
            for n, ref in enumerate((wg_ref, wu_ref))
        ] + [
            pltpu.make_async_copy(router_ref, joined.at[:, pl.ds(last, 128)], weight_sems.at[2, 0])
        ]

    def stores(k, i):
        e = scatter.block(round_of(k), i)
        copies = []
        for j in range(local):
            pairs = (
                (hid.at[i, :, columns(0, j)], hid_ref.at[e, j]),
                (acts.at[i, :, columns(0, j)], gga_ref.at[e, j]),
                (acts.at[i, :, columns(1, j)], uga_ref.at[e, j]),
            )
            for n, (src, dst) in enumerate(pairs):
                copies.append(pltpu.make_async_copy(src, dst, store_sems.at[n, j, i]))
        for j, side in enumerate(scatter.sides):
            src, dst = out_buf.at[i, j], out_ref.at[e, side]
            copies.append(pltpu.make_async_copy(src, dst, store_sems.at[3, j, i]))
        return copies

    def out_send(i, j):
        return remote(
            out_other.at[i, j], from_c.at[i, j], out_send_sems.at[i, j], out_sems.at[i, j], p.c
        )

    def ended(k, i):
        for copy in stores(k, i):
            copy.wait()
        for j in range(2):
            scatter.core_sent(round_of(k), i, j, other.at[i, j])
            out_send(i, j).wait_send()

    def exchanged(k, i):
        for j in range(2):
            scatter.core_add(round_of(k), i, j, mine[i, j])
            scatter.first(round_of(k), i, j)

    def compute(k, i):
        r = round_of(k)
        e = scatter.block(r, i)
        for copy in loads(k, i):
            copy.wait()

        @pl.when(k > 0)
        def _():
            ended(k - 1, i)

        chosen = mask_ref[e].astype(F32).T
        products[...] = dot(x_buf[i], joined[...])
        probs_ref[...] = softmax(products[:, last : last + experts])
        for j in range(local):
            gate = jnp.sum(
                chosen_here(chosen, p.e, local, j) * probs_ref[...], axis=-1, keepdims=True
            )
            g, u = products[:, columns(0, j)], products[:, columns(1, j)]
            hidden = (g * sigmoid(g) * u).astype(BF).astype(F32)
            hid[i, :, columns(0, j)] = (gate * hidden).astype(BF)
        if i == 0:
            pl.when(k > 0)(lambda: exchanged(k - 1, 1))
        else:
            exchanged(k, 0)

        def outputs(t):
            return dot(hid[i], wd_ref[:, pl.ds(pl.multiple_of(t * width, width), width)])

        for j, side in enumerate(scatter.sides):
            out_other[i, j] = outputs(2 * side + 1 - p.core).astype(BF)
            out_send(i, j).start()
        probs = probs_ref[...]
        prob_grad = jnp.zeros_like(probs)
        for j in range(local):
            here = chosen_here(chosen, p.e, local, j)
            gate = jnp.sum(here * probs, axis=-1, keepdims=True)
            v = cols_product(up_buf[i], wd_ref[pl.ds(j * ffe, ffe), :])
            g, u = products[:, columns(0, j)], products[:, columns(1, j)]
            gga, uga, gate_grad = expert_backward(gate, here, g, u, v)
            acts[i, :, columns(0, j)] = gga
            acts[i, :, columns(1, j)] = uga
            prob_grad += gate_grad
        high, low = router_backward(probs, prob_grad)
        both = jnp.concatenate([high, low], axis=-1)
        lg_ref[e] = both
        acts[i, :, last : last + 2 * experts] = both

        def gradients(t):
            rows = pl.ds(pl.multiple_of(t * width, width), width)
            return cols_product(acts[i], joined[rows, :]).astype(BF)

        for j, side in enumerate(scatter.sides):
            other[i, j] = gradients(2 * side + 1 - p.core)
            scatter.core(r, i, j, other.at[i, j])
        for j, side in enumerate(scatter.sides):
            total = outputs(2 * side + p.core)
            out_send(i, j).wait_recv()
            out_buf[i, j] = (total + from_c[i, j].astype(F32)).astype(BF)
        for j, side in enumerate(scatter.sides):
            mine[i, j] = gradients(2 * side + p.core)
        for copy in stores(k, i):
            copy.start()

        @pl.when(k + 1 < rounds)
        def _():
            for copy in loads(k + 1, i):
                copy.start()

    for copy in weight_loads():
        copy.start()
    for i in range(2):
        for copy in loads(0, i):
            copy.start()
        acts[i, :, last:] = jnp.zeros((tok, acts.shape[2] - last), BF)
    p.greet([p.y, p.x, p.c] + [p.z(r) for r in range(1, rounds)])
    for copy in weight_loads():
        copy.wait()

    def body(k, carry):
        r1, r2 = round_of(k + rounds - 1), round_of(k + rounds - 2)

        @pl.when(k < rounds)
        def _():
            compute(k, 0)

        pl.when(k == rounds)(lambda: exchanged(rounds - 1, 1))

        @pl.when(k >= 2)
        def _():
            for h in range(2):
                scatter.third(r2, h)

        @pl.when(k < rounds)
        def _():
            compute(k, 1)

        @pl.when(jnp.logical_and(k >= 1, k <= rounds))
        def _():
            for i in range(2):
                scatter.second0(r1, i)
                scatter.second1(r1, i)

        return carry

    lax.fori_loop(0, rounds + 2, body, 0)
    scatter.finish(grad_ref)
    for i in range(2):
        ended(rounds - 1, i)


def expert_scatter(x_all, up_all, mask_all, router_wide, w_gate, w_up, w_down, cid):
    groups, parts, tok, width = x_all.shape
    local, full, ffe = w_gate.shape
    experts = mask_all.shape[1]
    dma = pltpu.SemaphoreType.DMA
    bufs, sems = Scatter.scratch(groups, tok, width, tok // 2)
    act = jax.ShapeDtypeStruct((groups, local, tok, ffe), BF)
    block = pltpu.VMEM((2, tok, full), BF)
    shards = pltpu.VMEM((2, 2, tok, width), BF)
    wide = 2 * local * ffe + 128
    return pl.pallas_call(
        expert_scatter_kernel,
        name="experts_scatter",
        in_specs=[ANY, ANY, VMEM, ANY, ANY, ANY, VMEM],
        out_specs=[VMEM] + [ANY] * 4 + [VMEM],
        out_shape=[
            jax.ShapeDtypeStruct((tok, width), F32),
            jax.ShapeDtypeStruct((groups, 2, tok, width), BF),
            act,
            act,
            act,
            jax.ShapeDtypeStruct((groups, tok, 2 * experts), BF),
        ],
        scratch_shapes=bufs
        + sems
        + [block, block, shards, shards, shards, shards, shards]
        + [
            pltpu.VMEM((2, tok, local * ffe), BF),
            pltpu.VMEM((2, tok, wide), BF),
            pltpu.VMEM((full, wide), BF),
            pltpu.VMEM((tok, wide), F32),
            pltpu.VMEM((tok, experts), F32),
        ]
        + [dma((2, 2, parts)), dma((4, 2, 2)), dma((3, local)), dma((2, 2)), dma((2, 2))],
        compiler_params=pltpu.CompilerParams(
            collective_id=cid, has_side_effects=True, vmem_limit_bytes=62 * 2**20
        ),
        cost_estimate=pl.CostEstimate(
            flops=12 * groups * tok * full * ffe * local,
            bytes_accessed=groups * tok * full * 8,
            transcendentals=0,
        ),
    )(x_all, up_all, mask_all, router_wide, w_gate, w_up, w_down.reshape(local * ffe, full))


def per_device(
    tokens,
    segments,
    routes,
    norm1_gain,
    w_query,
    w_key,
    w_value,
    w_out,
    query_gain,
    key_gain,
    norm2_gain,
    router,
    w_gate,
    w_up,
    w_down,
    cotangent,
):
    tok, quarter = tokens.shape
    experts = router.shape[1]
    tensors = lax.axis_size("tensor")
    groups = lax.axis_size("expert")
    tensor_rank = lax.axis_index("tensor")
    full = quarter * tensors
    direct = tensors == 4 and groups == 8 and 16 <= experts <= 32

    up_all = lax.all_gather(cotangent, BOTH, axis=0).reshape(groups, tensors, tok, quarter)
    expert_ids = jnp.arange(experts, dtype=jnp.int32)
    chosen = jnp.any(routes.T[None, :, :] == expert_ids[:, None, None], axis=1).astype(BF)

    cosine_row, sine_row = rope_tables(tok, HEAD_DIM)
    tables = (
        jnp.concatenate([cosine_row, cosine_row], axis=-1),
        jnp.concatenate([-sine_row, sine_row], axis=-1),
    )
    (
        normed,
        query_pre,
        key_pre,
        query_rot,
        key_rot,
        value_low,
        attended,
        residual,
        normed_two,
        scales,
    ) = attention(
        tokens,
        segments,
        norm1_gain,
        w_query,
        w_key,
        w_value,
        w_out,
        query_gain,
        key_gain,
        norm2_gain,
        tables,
        4,
    )
    if direct:
        x_all, mask_all, router_wide = gather_all(
            normed_two, chosen, router.T, groups, tensors, 1
        )
    else:
        mask_all = lax.all_gather(chosen, "expert", axis=0)
        x_all = lax.all_gather(normed_two, BOTH, axis=0).reshape(groups, tensors, tok, quarter)

    def to_home(values):
        return lax.psum_scatter(
            values.reshape(groups * tensors, tok, quarter), BOTH, scatter_dimension=0
        ).astype(F32)

    if direct:
        normed_two_grad, out_part, hid, gga, uga, lg = expert_scatter(
            x_all, up_all, mask_all, router_wide, w_gate, w_up, w_down, 2
        )
    else:
        out_part, grad_part, expert_grads, router_part = plain_experts(
            lax.axis_index("expert"), x_all, up_all, mask_all, router.T, w_gate, w_up, w_down
        )
        normed_two_grad = to_home(grad_part)

    (
        tokens_grad,
        query_w_grad,
        key_w_grad,
        value_w_grad,
        out_w_grad,
        norm1_grad,
        norm2_grad,
        gains,
    ) = backward(
        groups,
        direct,
        5,
        normed_two_grad,
        residual,
        cotangent,
        tokens,
        scales,
        norm1_gain[None, :],
        norm2_gain[None, :],
        segments[None, :],
        query_gain[None, :],
        key_gain[None, :],
        *tables,
        normed,
        query_pre,
        key_pre,
        query_rot,
        key_rot,
        value_low,
        attended,
        w_query,
        w_key,
        w_value,
        w_out,
    )

    def spread(part):
        mine = jnp.arange(tensors)[:, None] == tensor_rank
        return jnp.where(mine, part, 0.0)

    rest = jnp.concatenate(
        [
            spread(norm1_grad),
            spread(norm2_grad),
            jnp.pad(gains, ((0, 0), (0, quarter - gains.shape[1]))),
        ]
    )
    rest = jnp.pad(rest, ((0, -rest.shape[0] % 8), (0, 0)))
    weight_grads = [query_w_grad, key_w_grad, value_w_grad]
    out_w_grad = out_w_grad.reshape(full, quarter)
    if direct:
        rest = jnp.pad(rest, ((0, experts - rest.shape[0]), (0, 0)))
        weight_grads, small, moe_out, expert_grads = reduce_shared(
            weight_grads, rest, lg, out_part, (x_all, up_all, hid, gga, uga), 3
        )
        router_sum, rest = small[:tensors], small[tensors]
    else:
        moe_out = to_home(out_part)
        *weight_grads, out_w_grad = [
            lax.psum(part, "expert") for part in weight_grads + [out_w_grad]
        ]
        router_sum, rest = lax.psum(
            (router_part.reshape(experts, tensors, quarter).transpose(1, 0, 2), rest), BOTH
        )
    mixed = (residual + moe_out).astype(BF)
    weight_grads = [part.astype(F32) for part in weight_grads]
    router_sum = router_sum.transpose(0, 2, 1).reshape(full, experts)
    norm1_sum = rest[:tensors].reshape(full)
    norm2_sum = rest[tensors : 2 * tensors].reshape(full)
    query_gain_sum = rest[2 * tensors, :HEAD_DIM]
    key_gain_sum = rest[2 * tensors, HEAD_DIM : 2 * HEAD_DIM]
    out_w_sum = out_w_grad.astype(F32).reshape(tensors, quarter, quarter).transpose(1, 0, 2)
    return (
        mixed,
        tokens_grad,
        norm1_sum,
        weight_grads[0],
        weight_grads[1],
        weight_grads[2],
        out_w_sum.reshape(quarter, full),
        query_gain_sum,
        key_gain_sum,
        norm2_sum,
        router_sum,
        *expert_grads,
    )


def solution(mesh):
    return jax.shard_map(
        per_device,
        mesh=mesh,
        in_specs=(
            P("expert", "tensor"),
            P("expert"),
            P("expert", None),
            P(),
            P(None, "tensor"),
            P(None, "tensor"),
            P(None, "tensor"),
            P("tensor", None),
            P(),
            P(),
            P(),
            P(),
            P("expert", None, "tensor"),
            P("expert", None, "tensor"),
            P("expert", "tensor", None),
            P("expert", "tensor"),
        ),
        out_specs=(
            P("expert", "tensor"),
            P("expert", "tensor"),
            P(),
            P(None, "tensor"),
            P(None, "tensor"),
            P(None, "tensor"),
            P("tensor", None),
            P(),
            P(),
            P(),
            P(),
            P("expert", None, "tensor"),
            P("expert", None, "tensor"),
            P("expert", "tensor", None),
        ),
        check_vma=False,
    )
```
